32 devices in a mesh: pipe: 4 (over y, x), rows: 8 (over z, core).
Axes of the slice: x: 2, y: 2, z: 4, core: 2. Of those that a mesh axis runs over, the one named last changes fastest.
Arguments:
- features: bfloat16 [2, 64, 32, 384], P(None, 'rows'), may hold values from -6 to 6
- section_layers: int32 [4], P('pipe'), may hold values from 1 to 2, as said below
- kernels: float32 [8, 49, 384], P('pipe'), may hold values from -0.875 to 0.875
- gains: float32 [8, 384], P('pipe'), may hold values from 0.5 to 1.5
- w_in: bfloat16 [8, 384, 1536], P('pipe'), may hold values from -0.3125 to 0.3125
- w_out: bfloat16 [8, 1536, 384], P('pipe'), may hold values from -0.15625 to 0.15625
- scales: float32 [8, 384], P('pipe'), may hold values from 0.2 to 1
- head_weight: bfloat16 [384, 8], replicated, may hold values from -0.3125 to 0.3125
- labels: int32 [2, 64, 32], P(None, 'rows'), may hold values from 0 to 7
Outputs:
- boundary_grad: bfloat16 [4, 2, 64, 32, 384], P('pipe', None, 'rows')
- kernel_grad: float32 [8, 49, 384], P('pipe')
- w_in_grad: bfloat16 [8, 384, 1536], P('pipe')
- w_out_grad: bfloat16 [8, 1536, 384], P('pipe')
The draws below stay inside these ranges and needn't reach their ends.
Inputs may be any that keep to these rules, and one draw needn't show every extreme that they name: section p applies the first section_layers[p] of its 2 slots; in every draw some section applies all 2 and some applies one.
All inputs are finite; a program needn't handle non-finite values.
Results may differ from the reference program's by a relative error of at most 0.03.
Values may be sent and summed in bfloat16 or wider, within the bound.
No kernel may reach another device: no remote copies, remote signals or barrier semaphores. Data moves between devices by JAX's collectives and lax.ppermute only.
A program may use at most 128 MiB of HBM per device.

```python
import math
import jax
import jax.numpy as jnp
from jax import lax

C = 384
FF = 1536
K = 8
W = 32
M = 2
LSLOT = 2
H = 64
LAYERS = 8
N_PIPE = 4


def draw_section_layers(key, part):
    key = jax.random.fold_in(key, 5)
    first_key, second_key = jax.random.split(key)
    counts = jax.random.randint(first_key, (N_PIPE,), 1, LSLOT + 1)
    order = jax.random.permutation(second_key, N_PIPE)
    counts = jnp.where(order == 0, LSLOT, counts)
    counts = jnp.where(order == 1, 1, counts)
    return counts.astype(jnp.int32)


def plant(entries, own_key, smallest, top_value):
    spot = [jax.random.randint(jax.random.fold_in(own_key, axis), (), 0, length) for axis, length in enumerate(entries.shape)]
    main_axis = entries.shape.index(max(entries.shape))
    neighbour = spot[:main_axis] + [(spot[main_axis] + 1) % entries.shape[main_axis]] + spot[main_axis + 1:]
    return entries.at[tuple(spot)].set(smallest).at[tuple(neighbour)].set(top_value)


def steps_of(rng, dims, shards, smallest, high):
    def one(axis_at, parts):
        heights = jax.random.uniform(jax.random.fold_in(jax.random.fold_in(rng, 6), axis_at), (parts,), jnp.float32, smallest / len(shards), high / len(shards))
        return jnp.repeat(jnp.exp(heights), dims[axis_at] // parts).reshape((-1,) + (1,) * (len(dims) - axis_at - 1))

    level = one(*shards[0])
    for cut in shards[1:]:
        level = level * one(*cut)
    return level


def scatter_about(own_key, extent, scale, limit, cuts=(), held_as=jnp.bfloat16):
    result = scale * jax.random.normal(own_key, extent, jnp.float32)
    if cuts:
        result = result * steps_of(own_key, extent, cuts, -0.22, 0.18)
    return jnp.clip(result, -limit, limit).astype(held_as)


def setup_inputs(seed: int = 0) -> dict:
    arg_keys = jax.random.split(jax.random.key(seed), 10)
    return {
        "features": scatter_about(arg_keys[0], (M, H, W, C), 1.0, 6.0, ((1, 8),)),
        "section_layers": draw_section_layers(jax.random.fold_in(arg_keys[9], 71), 0),
        "kernels": scatter_about(arg_keys[2], (LAYERS, 49, C), 49 ** -0.5, 0.875, ((0, 4),), jnp.float32),
        "gains": jnp.clip(1.0 + 0.1 * jax.random.normal(arg_keys[3], (LAYERS, C), jnp.float32), 0.5, 1.5),
        "w_in": scatter_about(arg_keys[4], (LAYERS, C, FF), C ** -0.5, 0.3125, ((0, 4),)),
        "w_out": scatter_about(arg_keys[5], (LAYERS, FF, C), FF ** -0.5, 0.15625, ((0, 4),)),
        "scales": jnp.clip(jnp.exp(math.log(1.0) - 1.609438 * jax.random.uniform(arg_keys[6], (LAYERS, C), jnp.float32) ** steps_of(arg_keys[6], (LAYERS, C), ((0, 4),), -0.2, 0.2)), 0.2, 1.0),
        "head_weight": scatter_about(arg_keys[7], (C, K), C ** -0.5, 0.3125),
        "labels": plant(jax.random.randint(arg_keys[8], (M, H, W), 0, K), jax.random.fold_in(arg_keys[8], 1), 0, K - 1).astype(jnp.int32),
    }


root_half = 1.0 / math.sqrt(2.0)
root_tau = 1.0 / math.sqrt(2.0 * math.pi)
norm_eps = 1e-06
loss_scale = 1024.0

def gelu_value(hidden):
    return 0.5 * hidden * (1.0 + lax.erf(hidden * root_half))

def gelu_slope(hidden):
    return 0.5 * (1.0 + lax.erf(hidden * root_half)) + hidden * jnp.exp(-0.5 * hidden * hidden) * root_tau

def normalize(conv_out, norm_gain):
    centred = conv_out - lax.optimization_barrier(jnp.mean(conv_out, axis=-1, keepdims=True))
    spread_sq = lax.optimization_barrier(jnp.mean(centred * centred, axis=-1, keepdims=True))
    return centred * lax.rsqrt(spread_sq + norm_eps) * norm_gain

def depthwise(padded, kernel, band_rows, band_cols):
    start = jnp.zeros((band_rows, band_cols, padded.shape[2]), jnp.float32)

    def row_step(row_off, summed):
        row_at = jnp.asarray(row_off).astype(jnp.int32)
        strip = lax.dynamic_slice_in_dim(padded, row_at, band_rows, 0)
        taps = lax.dynamic_slice_in_dim(kernel, row_at * 7, 7, 0)
        for col_off in range(7):
            summed = summed + strip[:, col_off:col_off + band_cols] * taps[col_off]
        return summed
    return lax.fori_loop(0, 7, row_step, start)

def kernel_terms(padded, grad_conv, band_rows, band_cols):
    start = jnp.zeros((49, grad_conv.shape[2]), jnp.float32)

    def row_step(row_off, rows_done):
        row_at = jnp.asarray(row_off).astype(jnp.int32)
        strip = lax.dynamic_slice_in_dim(padded, row_at, band_rows, 0)
        found = jnp.stack([lax.optimization_barrier(jnp.sum(grad_conv * strip[:, col_off:col_off + band_cols], axis=(0, 1))) for col_off in range(7)])
        return lax.dynamic_update_slice_in_dim(rows_done, found, row_at * 7, 0)
    return lax.fori_loop(0, 7, row_step, start)

def layer_front(current, padded, kernel, norm_gain, w_first, w_second, layer_scale):
    band_rows, band_cols, feat_width = current.shape
    conv_out = depthwise(padded, kernel, band_rows, band_cols)
    normed = normalize(conv_out, norm_gain).reshape(band_rows * band_cols, feat_width).astype(jnp.bfloat16)
    hidden = jnp.dot(normed, w_first, preferred_element_type=jnp.float32)
    active = gelu_value(hidden).astype(jnp.bfloat16)
    output = jnp.dot(active, w_second, preferred_element_type=jnp.float32).reshape(band_rows, band_cols, feat_width)
    return (current + layer_scale * output, (padded, conv_out, normed, hidden, active))

def layer_back(cotangent, saved, kernel, norm_gain, w_first, w_second, layer_scale):
    padded, conv_out, normed, hidden, active = saved
    band_rows, band_cols, feat_width = cotangent.shape
    grad_scaled = (layer_scale * cotangent).reshape(band_rows * band_cols, feat_width).astype(jnp.bfloat16)
    grad_second = jnp.dot(active.T, grad_scaled, preferred_element_type=jnp.float32)
    grad_hidden = (jnp.dot(grad_scaled, w_second.T, preferred_element_type=jnp.float32) * gelu_slope(hidden)).astype(jnp.bfloat16)
    grad_first = jnp.dot(normed.T, grad_hidden, preferred_element_type=jnp.float32)
    grad_normed = jnp.dot(grad_hidden, w_first.T, preferred_element_type=jnp.float32).reshape(band_rows, band_cols, feat_width)
    _, pullback = jax.vjp(lambda field: normalize(field, norm_gain), conv_out)
    grad_conv = pullback(grad_normed)[0]
    grad_kernel = kernel_terms(padded, grad_conv, band_rows, band_cols)
    grad_wide = jnp.pad(grad_conv, ((6, 6), (6, 6), (0, 0)))
    spread = depthwise(grad_wide, kernel[::-1], band_rows + 6, band_cols + 6)
    return (spread, grad_kernel, grad_first, grad_second)

def blank_saves(band_rows, band_cols, feat_width, hidden_width):
    return (jnp.zeros((band_rows + 6, band_cols + 6, feat_width), jnp.float32), jnp.zeros((band_rows, band_cols, feat_width), jnp.float32), jnp.zeros((band_rows * band_cols, feat_width), jnp.bfloat16), jnp.zeros((band_rows * band_cols, hidden_width), jnp.float32), jnp.zeros((band_rows * band_cols, hidden_width), jnp.bfloat16))

def section_run(section_in, layer_count, params):
    kernels, gains, w_in, w_out, scales = params
    current = section_in.astype(jnp.float32)
    band_rows, band_cols, feat_width = current.shape
    stored = []
    for slot_no in range(kernels.shape[0]):
        layer_params = (kernels[slot_no], gains[slot_no], w_in[slot_no], w_out[slot_no], scales[slot_no])

        def run_slot(field, layer_params=layer_params):
            padded = jnp.pad(field, ((3, 3), (3, 3), (0, 0)))
            return layer_front(field, padded, *layer_params)

        def pass_slot(field):
            return (field, blank_saves(band_rows, band_cols, feat_width, w_in.shape[2]))
        current, saved = lax.cond(slot_no < layer_count, run_slot, pass_slot, current)
        stored.append(saved)
    return (current.astype(jnp.bfloat16), stored)

def section_back(cotangent_in, layer_count, params, stored):
    kernels, gains, w_in, w_out, scales = params
    cotangent = cotangent_in.astype(jnp.float32)
    pieces = []
    for slot_no in reversed(range(kernels.shape[0])):
        layer_params = (kernels[slot_no], gains[slot_no], w_in[slot_no], w_out[slot_no], scales[slot_no])

        def run_slot(field, layer_params=layer_params, saved=stored[slot_no]):
            spread, grad_kernel, grad_first, grad_second = layer_back(field, saved, *layer_params)
            return (field + spread[3:-3, 3:-3], grad_kernel, grad_first, grad_second)

        def pass_slot(field):
            return (field, jnp.zeros(kernels.shape[1:], jnp.float32), jnp.zeros(w_in.shape[1:], jnp.float32), jnp.zeros(w_out.shape[1:], jnp.float32))
        cotangent, grad_kernel, grad_first, grad_second = lax.cond(slot_no < layer_count, run_slot, pass_slot, cotangent)
        pieces.insert(0, (grad_kernel, grad_first, grad_second))
    stacked = tuple((jnp.stack([piece[which] for piece in pieces]) for which in range(3)))
    return (cotangent.astype(jnp.bfloat16), stacked)

def reference(features, section_layers, kernels, gains, w_in, w_out, scales, head_weight, labels):
    params = tuple((item.reshape((N_PIPE, LSLOT) + item.shape[1:]) for item in (kernels, gains, w_in, w_out, scales)))
    kernel_sum = jnp.zeros((N_PIPE, LSLOT) + kernels.shape[1:], jnp.float32)
    first_sum = jnp.zeros((N_PIPE, LSLOT) + w_in.shape[1:], jnp.float32)
    second_sum = jnp.zeros((N_PIPE, LSLOT) + w_out.shape[1:], jnp.float32)
    boundary = []
    for micro_no in range(M):

        def forward(carried, item):
            section_out, _ = section_run(carried, item[0], item[1])
            return (section_out, carried)
        final, inputs = lax.scan(forward, features[micro_no], (section_layers, params))
        logits = jnp.dot(final.reshape(H * W, C), head_weight, preferred_element_type=jnp.float32)
        target = (labels[micro_no].reshape(H * W)[:, None] == jnp.arange(K)[None, :]).astype(jnp.float32)
        grad_logits = (loss_scale * 2.0 * (logits - target) / (M * H * W)).astype(jnp.bfloat16)
        grad_final = jnp.dot(grad_logits, head_weight.T, preferred_element_type=jnp.float32).reshape(H, W, C).astype(jnp.bfloat16)

        def backward(carried, item):
            layer_count, section_params, section_in = item
            _, stored = section_run(section_in, layer_count, section_params)
            cotangent, stacked = section_back(carried, layer_count, section_params, stored)
            return (cotangent, (cotangent, stacked))
        _, (cotangents, stacked) = lax.scan(backward, grad_final, (section_layers, params, inputs), reverse=True)
        boundary.append(cotangents)
        kernel_sum = kernel_sum + stacked[0]
        first_sum = first_sum + stacked[1]
        second_sum = second_sum + stacked[2]
    boundary_grad = jnp.stack(boundary, axis=1)
    kernel_grad = kernel_sum.reshape(kernels.shape)
    w_in_grad = first_sum.reshape(w_in.shape).astype(jnp.bfloat16)
    w_out_grad = second_sum.reshape(w_out.shape).astype(jnp.bfloat16)
    return (boundary_grad, kernel_grad, w_in_grad, w_out_grad)
```

```python
import functools
import math

import jax
import jax.numpy as jnp
from jax import lax
from jax.experimental import pallas as pl
from jax.experimental.pallas import tpu as pltpu
from jax.sharding import PartitionSpec as P

root_tau = 1.0 / math.sqrt(2.0 * math.pi)
norm_eps = 1e-06
loss_scale = 1024.0
erf_p = 0.3275911
erf_poly = (1.061405429, -1.453152027, 1.421413741, -0.284496736, 0.254829592)
LANES = 128
SUB = 8
NT = (((1,), (1,)), ((), ()))
TN = (((0,), (0,)), ((), ()))
VMEM_LIMIT = 48 * 1024 * 1024


def full_spec(shape):
    return pl.BlockSpec(shape, lambda *_: (0,) * len(shape))


def slot_spec(shape, slot):
    return pl.BlockSpec((None,) + tuple(shape[1:]), lambda *_: (slot,) + (0,) * (len(shape) - 1))


def call(body, operands, outs, scratch, flops):
    arrays, specs = [], []
    for item in operands:
        if isinstance(item, tuple):
            arrays.append(item[0])
            specs.append(slot_spec(item[0].shape, item[1]))
        else:
            arrays.append(item)
            specs.append(full_spec(item.shape))
    size = sum(math.prod(o[0]) * jnp.dtype(o[1]).itemsize for o in outs)
    size += sum(a.size * a.dtype.itemsize for a in arrays)
    return pl.pallas_call(
        body,
        grid=(1,),
        in_specs=specs,
        out_specs=[full_spec(o[0]) for o in outs],
        out_shape=[jax.ShapeDtypeStruct(*o) for o in outs],
        scratch_shapes=scratch,
        compiler_params=pltpu.CompilerParams(vmem_limit_bytes=VMEM_LIMIT),
        cost_estimate=pl.CostEstimate(flops=flops, bytes_accessed=size, transcendentals=0),
    )(*arrays)


def gelu_pair(h):
    e = jnp.exp(-0.5 * h * h)
    t = 1.0 / (1.0 + (erf_p * math.sqrt(0.5)) * jnp.abs(h))
    q = 0.5 * erf_poly[0]
    for coef in erf_poly[1:]:
        q = q * t + 0.5 * coef
    q = q * t * e
    phi = jnp.where(h >= 0.0, 1.0 - q, q)
    return h * phi, phi + h * (e * root_tau)


def build_shifts(own_rows, top_ref, bot_ref, m, cols, halo, shifts):
    planes = halo.shape[0]
    width = planes * LANES
    for q in range(3):
        at = pl.ds((m * 3 + q) * cols, cols)
        for lane in range(planes):
            lanes = slice(lane * LANES, (lane + 1) * LANES)
            plane = halo.at[lane]
            plane[pl.ds(5 + q, cols, stride=SUB), :] = top_ref[at, lanes].astype(jnp.float32)
            plane[pl.ds(q, cols, stride=SUB), :] = bot_ref[at, lanes].astype(jnp.float32)
    blank = jnp.zeros((3, SUB, width), jnp.float32)
    for a in range(7):
        shifts[a, 0:3] = blank
        shifts[a, cols + 3 : cols + 6] = blank
    sub = lax.broadcasted_iota(jnp.int32, (SUB, LANES), 0)

    def column(j, carry):
        for lane in range(planes):
            lanes = slice(lane * LANES, (lane + 1) * LANES)
            own = own_rows(j, lanes)
            edge = halo[lane, pl.ds(pl.multiple_of(j * SUB, SUB), SUB), :]
            for a in range(7):
                if a == 3:
                    shifts[a, j + 3, :, lanes] = own
                else:
                    mask = sub >= 5 + a if a < 3 else sub < a - 3
                    shifts[a, j + 3, :, lanes] = pltpu.roll(
                        jnp.where(mask, edge, own), (3 - a) % SUB, 0
                    )
        return carry

    lax.fori_loop(0, cols, column, 0, unroll=4)


def convolve(shifts, taps_ref, flip, cols, width, store):
    for lane in range(width // LANES):
        lanes = slice(lane * LANES, (lane + 1) * LANES)

        def block(cb, carry, lanes=lanes):
            acc = jnp.zeros((8, SUB, LANES), jnp.float32)
            for a in range(7):
                strip = shifts[a, pl.ds(cb * 8, 14), :, lanes]
                for b in range(7):
                    tap = 48 - (a * 7 + b) if flip else a * 7 + b
                    acc = acc + strip[b : b + 8] * taps_ref[tap, :, lanes][None]
            store(cb, lanes, acc.reshape(8 * SUB, LANES))
            return carry

        lax.fori_loop(0, cols // 8, block, 0)


def write_edges(source_ref, etop_ref, ebot_ref, halo, micros, cols):
    for m in range(micros):
        for lane in range(halo.shape[0]):
            lanes = slice(lane * LANES, (lane + 1) * LANES)
            plane = halo.at[lane]
            plane[...] = source_ref[m * cols * SUB : (m + 1) * cols * SUB, lanes]
            for q in range(3):
                to = pl.ds((m * 3 + q) * cols, cols)
                etop_ref[to, lanes] = plane[pl.ds(q, cols, stride=SUB), :].astype(jnp.bfloat16)
                ebot_ref[to, lanes] = plane[pl.ds(q + 5, cols, stride=SUB), :].astype(jnp.bfloat16)


def row_loop(rows, step, fn):
    def body(i, carry):
        fn(pl.ds(pl.multiple_of(i * step, step), step))
        return carry

    lax.fori_loop(0, rows // step, body, 0)


def load_rows(ref, cols, m):
    def own_rows(j, lanes):
        return ref[pl.ds(pl.multiple_of((m * cols + j) * SUB, SUB), SUB), lanes]

    return own_rows


def front_body(
    micros, cols,
    x_ref, top_ref, bot_ref, taps_ref, gain_ref, w_in_ref, w_out_ref, scale_ref,
    y_ref, out_ref, etop_ref, ebot_ref, conv_ref, normed_ref, active_ref, slope_ref,
    field, halo, shifts, hidden,
):
    rows, width = x_ref.shape
    hidden_width = w_in_ref.shape[1]
    field[...] = x_ref[...].astype(jnp.float32)
    for m in range(micros):
        build_shifts(load_rows(field, cols, m), top_ref, bot_ref, m, cols, halo, shifts)

        def store(cb, lanes, value, m=m):
            at = pl.ds(pl.multiple_of(m * cols * SUB + cb * 64, 64), 64)
            conv_ref[at, lanes] = value

        convolve(shifts, taps_ref, False, cols, width, store)

    def norm(at):
        conv = conv_ref[at, :]
        centred = conv - jnp.mean(conv, axis=-1, keepdims=True)
        spread = jnp.mean(centred * centred, axis=-1, keepdims=True)
        normed_ref[at, :] = (centred * lax.rsqrt(spread + norm_eps) * gain_ref[...]).astype(
            jnp.bfloat16
        )

    row_loop(rows, 32, norm)
    hidden[...] = jnp.dot(normed_ref[...], w_in_ref[...], preferred_element_type=jnp.float32)

    def gelu(at):
        for part in range(hidden_width // 512):
            lanes = slice(part * 512, (part + 1) * 512)
            value, slope = gelu_pair(hidden[at, lanes])
            active_ref[at, lanes] = value.astype(jnp.bfloat16)
            slope_ref[at, lanes] = slope.astype(jnp.bfloat16)

    row_loop(rows, 16, gelu)
    y_ref[...] = field[...] + scale_ref[...] * jnp.dot(
        active_ref[...], w_out_ref[...], preferred_element_type=jnp.float32
    )
    out_ref[...] = y_ref[...].astype(jnp.bfloat16)
    write_edges(y_ref, etop_ref, ebot_ref, halo, micros, cols)


def layer_front(x, top, bot, params, slot, micros, cols):
    taps, gains, w_in, w_out, scales = params
    rows, width = x.shape
    hidden_width = w_in.shape[2]
    f32, b16 = jnp.float32, jnp.bfloat16
    return call(
        functools.partial(front_body, micros, cols),
        (x, top, bot, (taps, slot), (gains, slot), (w_in, slot), (w_out, slot), (scales, slot)),
        [
            ((rows, width), f32), ((rows, width), b16), (top.shape, b16), (bot.shape, b16),
            ((rows, width), f32), ((rows, width), b16),
            ((rows, hidden_width), b16), ((rows, hidden_width), b16),
        ],
        [
            pltpu.VMEM((rows, width), f32),
            pltpu.VMEM((width // LANES, cols * SUB, LANES), f32),
            pltpu.VMEM((7, cols + 6, SUB, width), f32),
            pltpu.VMEM((rows, hidden_width), f32),
        ],
        4 * rows * width * hidden_width,
    )


def point_body(
    micros, cols,
    g_ref, conv_ref, slope_ref, gain_ref, w_in_ref, w_out_ref, scale_ref,
    gs_ref, gh_ref, gc_ref, etop_ref, ebot_ref, wide, halo,
):
    rows, width = g_ref.shape
    hidden_width = w_in_ref.shape[1]
    gs_ref[...] = (scale_ref[...] * g_ref[...].astype(jnp.float32)).astype(jnp.bfloat16)
    wide[...] = lax.dot_general(gs_ref[...], w_out_ref[...], NT, preferred_element_type=jnp.float32)

    def slope(at):
        for part in range(hidden_width // 512):
            lanes = slice(part * 512, (part + 1) * 512)
            gh_ref[at, lanes] = (wide[at, lanes] * slope_ref[at, lanes].astype(jnp.float32)).astype(
                jnp.bfloat16
            )

    row_loop(rows, 32, slope)
    gc_ref[...] = lax.dot_general(gh_ref[...], w_in_ref[...], NT, preferred_element_type=jnp.float32)

    def norm_back(at):
        conv = conv_ref[at, :]
        centred = conv - jnp.mean(conv, axis=-1, keepdims=True)
        spread = jnp.mean(centred * centred, axis=-1, keepdims=True)
        scale = lax.rsqrt(spread + norm_eps)
        unit = centred * scale
        grad = gc_ref[at, :] * gain_ref[...]
        first = jnp.mean(grad, axis=-1, keepdims=True)
        second = jnp.mean(grad * unit, axis=-1, keepdims=True)
        gc_ref[at, :] = scale * (grad - first - unit * second)

    row_loop(rows, 32, norm_back)
    write_edges(gc_ref, etop_ref, ebot_ref, halo, micros, cols)


def layer_point(g, conv, slope, params, slot, micros, cols):
    taps, gains, w_in, w_out, scales = params
    rows, width = g.shape
    hidden_width = w_in.shape[2]
    f32, b16 = jnp.float32, jnp.bfloat16
    edge = (micros * 3 * cols, width)
    return call(
        functools.partial(point_body, micros, cols),
        (g, conv, slope, (gains, slot), (w_in, slot), (w_out, slot), (scales, slot)),
        [((rows, width), b16), ((rows, hidden_width), b16), ((rows, width), f32), (edge, b16), (edge, b16)],
        [
            pltpu.VMEM((rows, hidden_width), f32),
            pltpu.VMEM((width // LANES, cols * SUB, LANES), f32),
        ],
        4 * rows * width * hidden_width,
    )


def spread_body(micros, cols, g_ref, gc_ref, top_ref, bot_ref, taps_ref, out_ref, halo, shifts):
    width = g_ref.shape[1]
    for m in range(micros):
        build_shifts(load_rows(gc_ref, cols, m), top_ref, bot_ref, m, cols, halo, shifts)

        def store(cb, lanes, value, m=m):
            at = pl.ds(pl.multiple_of(m * cols * SUB + cb * 64, 64), 64)
            out_ref[at, lanes] = (g_ref[at, lanes].astype(jnp.float32) + value).astype(out_ref.dtype)

        convolve(shifts, taps_ref, True, cols, width, store)


def layer_spread(g, gc, top, bot, params, slot, micros, cols, dtype):
    taps = params[0]
    rows, width = g.shape
    return call(
        functools.partial(spread_body, micros, cols),
        (g, gc, top, bot, (taps, slot)),
        [((rows, width), dtype)],
        [
            pltpu.VMEM((width // LANES, cols * SUB, LANES), jnp.float32),
            pltpu.VMEM((7, cols + 6, SUB, width), jnp.float32),
        ],
        98 * rows * width,
    )[0]


def weight_body(
    micros, cols,
    x_ref, top_ref, bot_ref, gc_ref, normed_ref, gh_ref, active_ref, gs_ref,
    first_ref, second_ref, kernel_ref, field, halo, shifts,
):
    width = x_ref.shape[1]
    first_ref[...] = lax.dot_general(
        normed_ref[...], gh_ref[...], TN, preferred_element_type=jnp.float32
    ).astype(jnp.bfloat16)
    second_ref[...] = lax.dot_general(
        active_ref[...], gs_ref[...], TN, preferred_element_type=jnp.float32
    ).astype(jnp.bfloat16)
    field[...] = x_ref[...].astype(jnp.float32)
    for m in range(micros):
        build_shifts(load_rows(field, cols, m), top_ref, bot_ref, m, cols, halo, shifts)
        for lane in range(width // LANES):
            lanes = slice(lane * LANES, (lane + 1) * LANES)

            def tap_row(a, carry, lanes=lanes, m=m):
                sums = [jnp.zeros((SUB, LANES), jnp.float32) for _ in range(7)]
                for cb in range(cols // 8):
                    strip = shifts[a, cb * 8 : cb * 8 + 14, :, lanes]
                    at = pl.ds((m * cols + cb * 8) * SUB, 64)
                    grad = gc_ref[at, lanes].reshape(8, SUB, LANES)
                    for b in range(7):
                        sums[b] = sums[b] + jnp.sum(strip[b : b + 8] * grad, axis=0)
                for b in range(7):
                    if m == 0:
                        kernel_ref[a * 7 + b, :, lanes] = sums[b]
                    else:
                        kernel_ref[a * 7 + b, :, lanes] += sums[b]
                return carry

            lax.fori_loop(0, 7, tap_row, 0)


def layer_weights(x, top, bot, gc, normed, gh, active, gs, micros, cols):
    rows, width = x.shape
    hidden_width = gh.shape[1]
    f32, b16 = jnp.float32, jnp.bfloat16
    return call(
        functools.partial(weight_body, micros, cols),
        (x, top, bot, gc, normed, gh, active, gs),
        [((width, hidden_width), b16), ((hidden_width, width), b16), ((49, SUB, width), f32)],
        [
            pltpu.VMEM((rows, width), f32),
            pltpu.VMEM((width // LANES, cols * SUB, LANES), f32),
            pltpu.VMEM((7, cols + 6, SUB, width), f32),
        ],
        4 * rows * width * hidden_width,
    )


def loss_body(factor, y_ref, head_ref, labels_ref, g_ref):
    logits = jnp.dot(y_ref[...], head_ref[...], preferred_element_type=jnp.float32)
    spots = lax.broadcasted_iota(jnp.int32, logits.shape, 1)
    target = (labels_ref[...] == spots).astype(jnp.float32)
    grad = (factor * (logits - target)).astype(jnp.bfloat16)
    g_ref[...] = lax.dot_general(
        grad, head_ref[...], NT, preferred_element_type=jnp.float32
    ).astype(jnp.bfloat16)


def on_device(features, section_layers, kernels, gains, w_in, w_out, scales, head_weight, labels):
    sections = lax.axis_size("pipe")
    section_index = lax.axis_index("pipe")
    bands = lax.axis_size("rows")
    micros, band_rows, cols, width = features.shape
    hidden_width = w_in.shape[2]
    layer_count = section_layers[0]
    rows = micros * band_rows * cols
    f32, b16 = jnp.float32, jnp.bfloat16
    two = layer_count > 1

    taps = jnp.broadcast_to(kernels[:, :, None, :], kernels.shape[:2] + (SUB, width))
    params = (taps, gains[:, None, :], w_in, w_out, scales[:, None, :])
    dims = (micros, cols)

    def to_rows(x):
        return x.transpose(0, 2, 1, 3).reshape(rows, width)

    up = [(i, i + 1) for i in range(bands - 1)]
    down = [(i + 1, i) for i in range(bands - 1)]

    def halo(etop, ebot):
        return lax.ppermute(ebot, "rows", up), lax.ppermute(etop, "rows", down)

    def hop(x, etop, ebot):
        def pairs(by):
            return [
                (p * bands + r, (p + 1) * bands + r + by)
                for p in range(sections - 1)
                for r in range(bands)
                if 0 <= r + by < bands
            ]

        axes = ("pipe", "rows")
        return (
            lax.ppermute(x, axes, pairs(0)),
            lax.ppermute(ebot, axes, pairs(1)),
            lax.ppermute(etop, axes, pairs(-1)),
        )

    edge_shape = (micros * 3 * cols, width)

    def blank(dtype_x):
        return (
            jnp.zeros((rows, width), dtype_x), jnp.zeros(edge_shape, b16), jnp.zeros(edge_shape, b16),
            jnp.zeros((rows, width), f32), jnp.zeros((rows, width), b16),
            jnp.zeros((rows, hidden_width), b16), jnp.zeros((rows, hidden_width), b16),
        )

    first_in = (
        to_rows(features),
        *halo(features[:, :3].reshape(edge_shape), features[:, band_rows - 3 :].reshape(edge_shape)),
    )

    def forward_tick(tick, state):
        received, kept0, kept1, sent = state

        def run(operand):
            x, top, bot = operand[0]
            y, out, etop, ebot, conv, normed, active, slope = layer_front(
                x, top, bot, params, 0, *dims
            )
            kept0 = (x, top, bot, conv, normed, active, slope)

            def second(inner):
                y, _, etop, ebot, _ = inner
                top, bot = halo(etop, ebot)
                _, out, etop, ebot, conv, normed, active, slope = layer_front(
                    y, top, bot, params, 1, *dims
                )
                return (out, etop, ebot), (y, top, bot, conv, normed, active, slope)

            def only(inner):
                return inner[1:4], inner[4]

            sent, kept1 = lax.cond(two, second, only, (y, out, etop, ebot, operand[2]))
            return kept0, kept1, sent

        def leave(operand):
            return operand[1:]

        kept0, kept1, sent = lax.cond(
            tick == section_index, run, leave, (received, kept0, kept1, sent)
        )
        received = lax.cond(tick < sections - 1, lambda s: hop(*s), lambda s: tuple(s), sent)
        return received, kept0, kept1, sent

    state = (
        first_in, blank(b16), blank(f32),
        (jnp.zeros((rows, width), b16), jnp.zeros(edge_shape, b16), jnp.zeros(edge_shape, b16)),
    )
    _, kept0, kept1, sent = lax.fori_loop(0, sections, forward_tick, state)

    total = micros * band_rows * bands * cols
    (from_loss,) = call(
        functools.partial(loss_body, loss_scale * 2.0 / total),
        (sent[0], head_weight, labels.transpose(0, 2, 1).reshape(rows, 1)),
        [((rows, width), b16)],
        [],
        4 * rows * width * head_weight.shape[1],
    )

    def blank_back():
        return (
            jnp.zeros((rows, width), b16), jnp.zeros((rows, hidden_width), b16),
            jnp.zeros((rows, width), f32),
        )

    back_pairs = [(p + 1, p) for p in range(sections - 1)]

    def backward_tick(tick, state):
        incoming, back0, back1, cotangent = state

        def run(operand):
            g = operand[0]

            def second(inner):
                g, _ = inner
                gs, gh, gc, etop, ebot = layer_point(
                    g, kept1[3], kept1[6], params, 1, *dims
                )
                top, bot = halo(etop, ebot)
                g = layer_spread(g, gc, top, bot, params, 1, *dims, f32)
                return g, (gs, gh, gc)

            def only(inner):
                return inner[0].astype(f32), inner[1]

            g, back1 = lax.cond(two, second, only, (g, operand[2]))
            gs, gh, gc, etop, ebot = layer_point(g, kept0[3], kept0[6], params, 0, *dims)
            top, bot = halo(etop, ebot)
            g = layer_spread(g, gc, top, bot, params, 0, *dims, b16)
            return (gs, gh, gc), back1, g

        def leave(operand):
            return operand[1:]

        back0, back1, cotangent = lax.cond(
            tick == sections - 1 - section_index, run, leave, (incoming, back0, back1, cotangent)
        )
        incoming = lax.cond(
            tick < sections - 1,
            lambda g: lax.ppermute(g, "pipe", back_pairs),
            lambda g: g,
            cotangent,
        )
        return incoming, back0, back1, cotangent

    state = (from_loss, blank_back(), blank_back(), jnp.zeros((rows, width), b16))
    _, back0, back1, cotangent = lax.fori_loop(0, sections, backward_tick, state)

    found = []
    for kept, back in ((kept0, back0), (kept1, back1)):
        x, top, bot, _, normed, active, _ = kept
        gs, gh, gc = back
        found.append(layer_weights(x, top, bot, gc, normed, gh, active, gs, *dims))
    firsts, seconds, taps_found = zip(*found)
    w_in_grad = lax.psum(jnp.stack(firsts), "rows")
    w_out_grad = lax.psum(jnp.stack(seconds), "rows")
    kernel_part = jnp.sum(jnp.stack(taps_found), axis=2).astype(b16)
    kernel_grad = lax.psum(kernel_part, "rows").astype(f32)
    boundary = cotangent.reshape(micros, cols, band_rows, width).transpose(0, 2, 1, 3)
    return (boundary[None], kernel_grad, w_in_grad, w_out_grad)


def solution(mesh):
    return jax.shard_map(
        on_device,
        mesh=mesh,
        in_specs=(
            P(None, "rows", None, None),
            P("pipe"),
            P("pipe", None, None),
            P("pipe", None),
            P("pipe", None, None),
            P("pipe", None, None),
            P("pipe", None),
            P(),
            P(None, "rows", None),
        ),
        out_specs=(
            P("pipe", None, "rows", None, None),
            P("pipe", None, None),
            P("pipe", None, None),
            P("pipe", None, None),
        ),
        check_vma=False,
    )
```

```python
import functools
import math

import jax
import jax.numpy as jnp
from jax import lax
from jax.experimental import pallas as pl
from jax.experimental.pallas import tpu as pltpu
from jax.sharding import PartitionSpec as P

root_tau = 1.0 / math.sqrt(2.0 * math.pi)
norm_eps = 1e-06
loss_scale = 1024.0
erf_p = 0.3275911
erf_poly = (1.061405429, -1.453152027, 1.421413741, -0.284496736, 0.254829592)
LANES = 128
SUB = 8
NT = (((1,), (1,)), ((), ()))
TN = (((0,), (0,)), ((), ()))
VMEM_LIMIT = 48 * 1024 * 1024
CHUNK = 256
GELU = jnp.bfloat16


def block_spec(array_rows, shape, micros):
    if array_rows:
        return pl.BlockSpec((shape[0] // micros,) + tuple(shape[1:]), lambda m: (m,) + (0,) * (len(shape) - 1))
    return pl.BlockSpec(shape, lambda m: (0,) * len(shape))


def slot_spec(shape, slot):
    return pl.BlockSpec((None,) + tuple(shape[1:]), lambda m: (slot,) + (0,) * (len(shape) - 1))


def per_micro(body, micros, operands, outs, scratch, flops):
    arrays, specs = [], []
    for item in operands:
        if isinstance(item, tuple):
            arrays.append(item[0])
            specs.append(slot_spec(item[0].shape, item[1]))
        else:
            arrays.append(item)
            specs.append(block_spec(True, item.shape, micros))
    size = sum(math.prod(o[0]) * jnp.dtype(o[1]).itemsize for o in outs)
    size += sum(a.size * a.dtype.itemsize for a in arrays)
    return pl.pallas_call(
        body,
        grid=(micros,),
        in_specs=specs,
        out_specs=[block_spec(True, o[0], micros) for o in outs],
        out_shape=[jax.ShapeDtypeStruct(*o) for o in outs],
        scratch_shapes=scratch,
        compiler_params=pltpu.CompilerParams(vmem_limit_bytes=VMEM_LIMIT),
        cost_estimate=pl.CostEstimate(flops=flops, bytes_accessed=size, transcendentals=0),
    )(*arrays)


def unwritten(shapes):
    return pl.pallas_call(
        lambda *refs: None,
        out_specs=[pl.BlockSpec(memory_space=pl.ANY) for _ in shapes],
        out_shape=[jax.ShapeDtypeStruct(*s) for s in shapes],
    )()


def gelu_pair(h):
    e = jnp.exp(h * h * -0.5)
    t = 1.0 / (1.0 + (erf_p * math.sqrt(0.5)) * jnp.abs(h))
    q = t * (0.5 * erf_poly[0]) + 0.5 * erf_poly[1]
    for coef in erf_poly[2:]:
        q = q * t + 0.5 * coef
    q = q * t * e
    phi = jnp.where(h >= 0.0, 1.0 - q, q)
    return h * phi, phi + h * (e * root_tau)


def spread_taps(taps_ref, wide_taps):
    count, width = taps_ref.shape
    for tap in range(count):
        row = jnp.broadcast_to(taps_ref[tap : tap + 1, :], (2 * SUB, width))
        wide_taps[tap] = row.astype(jnp.bfloat16)


def build_shifts(own_ref, top_ref, bot_ref, cols, halo, shifts):
    planes = halo.shape[0]
    half = cols // 2
    for q in range(3):
        at = pl.ds(q * cols, cols)
        for lane in range(planes):
            lanes = slice(lane * LANES, (lane + 1) * LANES)
            plane = halo.at[lane]
            plane[pl.ds(5 + q, cols, stride=SUB), :] = top_ref[at, lanes].astype(jnp.float32)
            plane[pl.ds(q, cols, stride=SUB), :] = bot_ref[at, lanes].astype(jnp.float32)
    sub = lax.broadcasted_iota(jnp.int32, (SUB, LANES), 0)

    def pair(k, carry):
        for lane in range(planes):
            lanes = slice(lane * LANES, (lane + 1) * LANES)
            at = pl.ds(pl.multiple_of(k * 2 * SUB, 2 * SUB), 2 * SUB)
            own = own_ref[at, lanes].astype(jnp.float32)
            edge = halo[lane, at, :]
            for a in range(7):
                if a == 3:
                    both = own
                else:
                    mask = sub >= 5 + a if a < 3 else sub < a - 3
                    both = jnp.concatenate(
                        [
                            pltpu.roll(
                                jnp.where(mask, edge[h * SUB : (h + 1) * SUB], own[h * SUB : (h + 1) * SUB]),
                                (3 - a) % SUB,
                                0,
                            )
                            for h in range(2)
                        ],
                        axis=0,
                    )
                shifts[a, k + 3, :, lanes] = both.astype(jnp.bfloat16)
        return carry

    lax.fori_loop(0, half, pair, 0, unroll=2)
    blank = jnp.zeros((SUB, planes * LANES), jnp.float32)
    for a in range(7):
        for k in range(3):
            right = shifts[a, k + 3].astype(jnp.float32)[SUB:]
            shifts[a, half + 3 + k] = jnp.concatenate([right, blank], axis=0).astype(jnp.bfloat16)
            left = shifts[a, half + k].astype(jnp.float32)[:SUB]
            shifts[a, k] = jnp.concatenate([blank, left], axis=0).astype(jnp.bfloat16)


def convolve(shifts, wide_taps, flip, cols, width, store):
    for lane in range(width // LANES):
        lanes = slice(lane * LANES, (lane + 1) * LANES)

        def block(kb, carry, lanes=lanes):
            acc = jnp.zeros((8, 2 * SUB, LANES), jnp.float32)
            for a in range(7):
                strip = shifts[a, pl.ds(kb * 8, 14), :, lanes]
                line = None
                for b in range(7):
                    tap = 48 - (a * 7 + b) if flip else a * 7 + b
                    term = strip[b : b + 8] * wide_taps[tap, :, lanes][None]
                    line = term if line is None else line + term
                acc = acc + line.astype(jnp.float32)
            store(pl.ds(pl.multiple_of(kb * 128, 128), 128), lanes, acc.reshape(16 * SUB, LANES))
            return carry

        lax.fori_loop(0, cols // 16, block, 0)


def write_edges(source_ref, etop_ref, ebot_ref, halo, cols):
    for lane in range(halo.shape[0]):
        lanes = slice(lane * LANES, (lane + 1) * LANES)
        plane = halo.at[lane]
        plane[...] = source_ref[:, lanes]
        for q in range(3):
            to = pl.ds(q * cols, cols)
            etop_ref[to, lanes] = plane[pl.ds(q, cols, stride=SUB), :].astype(jnp.bfloat16)
            ebot_ref[to, lanes] = plane[pl.ds(q + 5, cols, stride=SUB), :].astype(jnp.bfloat16)


def row_loop(rows, step, fn):
    def body(i, carry):
        fn(pl.ds(pl.multiple_of(i * step, step), step))
        return carry

    lax.fori_loop(0, rows // step, body, 0)


def conv_scratch(cols, width):
    return [
        pltpu.VMEM((width // LANES, cols * SUB, LANES), jnp.float32),
        pltpu.VMEM((7, cols // 2 + 6, 2 * SUB, width), jnp.bfloat16),
        pltpu.VMEM((49, 2 * SUB, width), jnp.bfloat16),
    ]


def front_body(
    cols,
    x_ref, top_ref, bot_ref, taps_ref, gain_ref, w_in_ref, w_out_ref, scale_ref,
    y_ref, out_ref, etop_ref, ebot_ref, conv_ref, normed_ref, active_ref, slope_ref,
    halo, shifts, wide_taps, hidden,
):
    rows, width = x_ref.shape
    hidden_width = w_in_ref.shape[1]

    @pl.when(pl.program_id(0) == 0)
    def first_step():
        spread_taps(taps_ref, wide_taps)

    build_shifts(x_ref, top_ref, bot_ref, cols, halo, shifts)

    def store(at, lanes, value):
        conv_ref[at, lanes] = value

    convolve(shifts, wide_taps, False, cols, width, store)

    def norm(at):
        conv = conv_ref[at, :]
        centred = conv - jnp.mean(conv, axis=-1, keepdims=True)
        spread = jnp.mean(centred * centred, axis=-1, keepdims=True)
        normed_ref[at, :] = (centred * lax.rsqrt(spread + norm_eps) * gain_ref[...]).astype(
            jnp.bfloat16
        )

    row_loop(rows, 64, norm)
    normed = normed_ref[...]
    chunks = hidden_width // CHUNK

    def expand(n):
        hidden[n % 2] = jnp.dot(
            normed, w_in_ref[:, n * CHUNK : (n + 1) * CHUNK], preferred_element_type=jnp.float32
        )

    expand(0)
    for n in range(chunks):
        if n + 1 < chunks:
            expand(n + 1)
        lanes = slice(n * CHUNK, (n + 1) * CHUNK)
        for i in range(rows // 32):
            at = slice(i * 32, (i + 1) * 32)
            value, slope = gelu_pair(hidden[n % 2, at, :].astype(GELU))
            active_ref[at, lanes] = value.astype(jnp.bfloat16)
            slope_ref[at, lanes] = slope.astype(jnp.bfloat16)
    y_ref[...] = x_ref[...].astype(jnp.float32) + scale_ref[...] * jnp.dot(
        active_ref[...], w_out_ref[...], preferred_element_type=jnp.float32
    )
    out_ref[...] = y_ref[...].astype(jnp.bfloat16)
    write_edges(y_ref, etop_ref, ebot_ref, halo, cols)


def layer_front(x, top, bot, params, slot, micros, cols):
    taps, gains, w_in, w_out, scales = params
    rows, width = x.shape
    hidden_width = w_in.shape[2]
    f32, b16 = jnp.float32, jnp.bfloat16
    return per_micro(
        functools.partial(front_body, cols),
        micros,
        (x, top, bot, (taps, slot), (gains, slot), (w_in, slot), (w_out, slot), (scales, slot)),
        [
            ((rows, width), f32), ((rows, width), b16), (top.shape, b16), (bot.shape, b16),
            ((rows, width), f32), ((rows, width), b16),
            ((rows, hidden_width), b16), ((rows, hidden_width), b16),
        ],
        conv_scratch(cols, width) + [pltpu.VMEM((2, rows // micros, CHUNK), f32)],
        4 * rows * width * hidden_width,
    )


def point_body(
    cols,
    g_ref, conv_ref, slope_ref, gain_ref, w_in_ref, w_out_ref, scale_ref,
    gs_ref, gh_ref, gc_ref, etop_ref, ebot_ref, wide, halo,
):
    rows, width = g_ref.shape
    hidden_width = w_in_ref.shape[1]
    gs_ref[...] = (scale_ref[...] * g_ref[...].astype(jnp.float32)).astype(jnp.bfloat16)
    grad = gs_ref[...]
    chunks = hidden_width // CHUNK

    def expand(n):
        wide[n % 2] = lax.dot_general(
            grad, w_out_ref[n * CHUNK : (n + 1) * CHUNK, :], NT, preferred_element_type=jnp.float32
        )

    expand(0)
    for n in range(chunks):
        if n + 1 < chunks:
            expand(n + 1)
        lanes = slice(n * CHUNK, (n + 1) * CHUNK)
        for i in range(rows // 32):
            at = slice(i * 32, (i + 1) * 32)
            gh_ref[at, lanes] = (wide[n % 2, at, :] * slope_ref[at, lanes].astype(jnp.float32)).astype(
                jnp.bfloat16
            )
    gc_ref[...] = lax.dot_general(gh_ref[...], w_in_ref[...], NT, preferred_element_type=jnp.float32)

    def norm_back(at):
        conv = conv_ref[at, :]
        centred = conv - jnp.mean(conv, axis=-1, keepdims=True)
        spread = jnp.mean(centred * centred, axis=-1, keepdims=True)
        scale = lax.rsqrt(spread + norm_eps)
        unit = centred * scale
        grad = gc_ref[at, :] * gain_ref[...]
        first = jnp.mean(grad, axis=-1, keepdims=True)
        second = jnp.mean(grad * unit, axis=-1, keepdims=True)
        gc_ref[at, :] = scale * (grad - first - unit * second)

    row_loop(rows, 64, norm_back)
    write_edges(gc_ref, etop_ref, ebot_ref, halo, cols)


def layer_point(g, conv, slope, params, slot, micros, cols):
    taps, gains, w_in, w_out, scales = params
    rows, width = g.shape
    hidden_width = w_in.shape[2]
    f32, b16 = jnp.float32, jnp.bfloat16
    edge = (micros * 3 * cols, width)
    return per_micro(
        functools.partial(point_body, cols),
        micros,
        (g, conv, slope, (gains, slot), (w_in, slot), (w_out, slot), (scales, slot)),
        [((rows, width), b16), ((rows, hidden_width), b16), ((rows, width), f32), (edge, b16), (edge, b16)],
        [
            pltpu.VMEM((2, rows // micros, CHUNK), f32),
            pltpu.VMEM((width // LANES, cols * SUB, LANES), f32),
        ],
        4 * rows * width * hidden_width,
    )


def spread_body(
    cols, g_ref, gc_ref, top_ref, bot_ref, taps_ref, out_ref, halo, shifts, wide_taps
):
    @pl.when(pl.program_id(0) == 0)
    def first_step():
        spread_taps(taps_ref, wide_taps)

    build_shifts(gc_ref, top_ref, bot_ref, cols, halo, shifts)

    def store(at, lanes, value):
        out_ref[at, lanes] = (g_ref[at, lanes].astype(jnp.float32) + value).astype(out_ref.dtype)

    convolve(shifts, wide_taps, True, cols, g_ref.shape[1], store)


def layer_spread(g, gc, top, bot, params, slot, micros, cols, dtype):
    rows, width = g.shape
    return per_micro(
        functools.partial(spread_body, cols),
        micros,
        (g, gc, top, bot, (params[0], slot)),
        [((rows, width), dtype)],
        conv_scratch(cols, width),
        98 * rows * width,
    )[0]


def weight_body(
    micros, cols, slot,
    count_ref, x_ref, top_ref, bot_ref, gc_ref, normed_ref, gh_ref, active_ref, gs_ref,
    first_ref, second_ref, kernel_ref, halo, shifts, sums,
):
    width = x_ref.shape[1]
    applied = slot < count_ref[0]

    @pl.when(jnp.logical_not(applied))
    def passed():
        first_ref[...] = jnp.zeros_like(first_ref)
        second_ref[...] = jnp.zeros_like(second_ref)
        kernel_ref[...] = jnp.zeros_like(kernel_ref)

    @pl.when(applied)
    def run():
        first_ref[...] = lax.dot_general(
            normed_ref[...], gh_ref[...], TN, preferred_element_type=jnp.float32
        ).astype(jnp.bfloat16)
        second_ref[...] = lax.dot_general(
            active_ref[...], gs_ref[...], TN, preferred_element_type=jnp.float32
        ).astype(jnp.bfloat16)
        pixels = cols * SUB
        for m in range(micros):
            at_edge = pl.ds(m * 3 * cols, 3 * cols)
            build_shifts(
                x_ref.at[pl.ds(m * pixels, pixels)], top_ref.at[at_edge], bot_ref.at[at_edge],
                cols, halo, shifts,
            )
            for lane in range(width // LANES):
                lanes = slice(lane * LANES, (lane + 1) * LANES)

                def tap_row(a, carry, lanes=lanes, m=m):
                    found = [jnp.zeros((2 * SUB, LANES), jnp.float32) for _ in range(7)]
                    for kb in range(cols // 16):
                        strip = shifts[a, kb * 8 : kb * 8 + 14, :, lanes]
                        at = pl.ds(m * pixels + kb * 128, 128)
                        grad = gc_ref[at, lanes].astype(jnp.bfloat16).reshape(8, 2 * SUB, LANES)
                        for b in range(7):
                            term = strip[b : b + 8] * grad
                            term = (term[0] + term[1]) + (term[2] + term[3]), (term[4] + term[5]) + (term[6] + term[7])
                            found[b] = found[b] + (term[0].astype(jnp.float32) + term[1].astype(jnp.float32))
                    for b in range(7):
                        total = found[b][:SUB] + found[b][SUB:]
                        if m == 0:
                            sums[a * 7 + b, :, lanes] = total
                        else:
                            sums[a * 7 + b, :, lanes] += total
                    return carry

                lax.fori_loop(0, 7, tap_row, 0)
        kernel_ref[...] = jnp.sum(sums[...], axis=1).astype(jnp.bfloat16)


def layer_weights(count, kept, back, slot, micros, cols):
    x, top, bot, _, normed, active, _ = kept
    gs, gh, gc = back
    rows, width = x.shape
    hidden_width = gh.shape[1]
    f32, b16 = jnp.float32, jnp.bfloat16
    arrays = (x, top, bot, gc, normed, gh, active, gs)
    outs = [((width, hidden_width), b16), ((hidden_width, width), b16), ((49, width), b16)]
    size = sum(math.prod(o[0]) * jnp.dtype(o[1]).itemsize for o in outs)
    size += sum(a.size * a.dtype.itemsize for a in arrays)
    return pl.pallas_call(
        functools.partial(weight_body, micros, cols, slot),
        grid=(1,),
        in_specs=[pl.BlockSpec(memory_space=pltpu.SMEM)] + [block_spec(False, a.shape, 1) for a in arrays],
        out_specs=[block_spec(False, o[0], 1) for o in outs],
        out_shape=[jax.ShapeDtypeStruct(*o) for o in outs],
        scratch_shapes=conv_scratch(cols, width)[:2] + [pltpu.VMEM((49, SUB, width), f32)],
        compiler_params=pltpu.CompilerParams(vmem_limit_bytes=VMEM_LIMIT),
        cost_estimate=pl.CostEstimate(
            flops=4 * rows * width * hidden_width, bytes_accessed=size, transcendentals=0
        ),
    )(count, *arrays)


def loss_body(factor, y_ref, head_ref, labels_ref, g_ref):
    logits = jnp.dot(y_ref[...], head_ref[...], preferred_element_type=jnp.float32)
    spots = lax.broadcasted_iota(jnp.int32, logits.shape, 1)
    target = (labels_ref[...] == spots).astype(jnp.float32)
    grad = (factor * (logits - target)).astype(jnp.bfloat16)
    g_ref[...] = lax.dot_general(
        grad, head_ref[...], NT, preferred_element_type=jnp.float32
    ).astype(jnp.bfloat16)


def on_device(features, section_layers, kernels, gains, w_in, w_out, scales, head_weight, labels):
    sections = lax.axis_size("pipe")
    section_index = lax.axis_index("pipe")
    bands = lax.axis_size("rows")
    micros, band_rows, cols, width = features.shape
    hidden_width = w_in.shape[2]
    classes = head_weight.shape[1]
    layer_count = section_layers[0]
    rows = micros * band_rows * cols
    half = cols // 2
    f32, b16 = jnp.float32, jnp.bfloat16
    params = (kernels, gains[:, None, :], w_in, w_out, scales[:, None, :])
    dims = (micros, cols)
    edge_shape = (micros * 3 * cols, width)

    up = [(i, i + 1) for i in range(bands - 1)]
    down = [(i + 1, i) for i in range(bands - 1)]

    def halo(etop, ebot):
        return lax.ppermute(ebot, "rows", up), lax.ppermute(etop, "rows", down)

    def hop(x, etop, ebot):
        def pairs(by):
            return [
                (p * bands + r, (p + 1) * bands + r + by)
                for p in range(sections - 1)
                for r in range(bands)
                if 0 <= r + by < bands
            ]

        axes = ("pipe", "rows")
        return (
            lax.ppermute(x, axes, pairs(0)),
            lax.ppermute(ebot, axes, pairs(1)),
            lax.ppermute(etop, axes, pairs(-1)),
        )

    def edge_rows(part):
        part = part.reshape(micros, 3, 2, half, width).transpose(0, 1, 3, 2, 4)
        return part.reshape(edge_shape)

    first_x = features.reshape(micros, band_rows, 2, half, width).transpose(0, 3, 2, 1, 4)
    first_in = (
        first_x.reshape(rows, width),
        *halo(edge_rows(features[:, :3]), edge_rows(features[:, band_rows - 3 :])),
    )

    def kept_shapes(dtype_x):
        return [
            ((rows, width), dtype_x), (edge_shape, b16), (edge_shape, b16), ((rows, width), f32),
            ((rows, width), b16), ((rows, hidden_width), b16), ((rows, hidden_width), b16),
        ]

    sent_shapes = [((rows, width), b16), (edge_shape, b16), (edge_shape, b16)]
    back_shapes = [((rows, width), b16), ((rows, hidden_width), b16), ((rows, width), f32)]

    def front(x, top, bot, slot):
        y, out, etop, ebot, conv, normed, active, slope = layer_front(x, top, bot, params, slot, *dims)
        return y, (out, etop, ebot), (x, top, bot, conv, normed, active, slope)

    def forward_section(tick, received, kept0, kept1, sent):
        def leave(received, kept0, kept1, sent):
            return kept0, kept1, sent

        def one(received, kept0, kept1, sent):
            _, sent, kept0 = front(*received, 0)
            return kept0, kept1, sent

        def both(received, kept0, kept1, sent):
            y, (_, etop, ebot), kept0 = front(*received, 0)
            _, sent, kept1 = front(y, *halo(etop, ebot), 1)
            return kept0, kept1, sent

        which = jnp.where(tick == section_index, layer_count, 0)
        return lax.switch(which, (leave, one, both), received, kept0, kept1, sent)

    def forward_tick(tick, state):
        received, kept0, kept1, sent = state
        kept0, kept1, sent = forward_section(tick, received, kept0, kept1, sent)
        return hop(*sent), kept0, kept1, sent

    buffers = unwritten(kept_shapes(b16) + kept_shapes(f32) + sent_shapes)
    state = (first_in, tuple(buffers[:7]), tuple(buffers[7:14]), tuple(buffers[14:]))
    state = lax.fori_loop(0, sections - 1, forward_tick, state)
    kept0, kept1, sent = forward_section(sections - 1, *state)

    total = micros * band_rows * bands * cols
    pixel_labels = labels.reshape(micros, band_rows, 2, half).transpose(0, 3, 2, 1).reshape(rows, 1)
    from_loss = pl.pallas_call(
        functools.partial(loss_body, loss_scale * 2.0 / total),
        out_shape=jax.ShapeDtypeStruct((rows, width), b16),
    )(sent[0], head_weight, pixel_labels)

    def back_layer(g, slot, kept, dtype):
        gs, gh, gc, etop, ebot = layer_point(g, kept[3], kept[6], params, slot, *dims)
        g = layer_spread(g, gc, *halo(etop, ebot), params, slot, *dims, dtype)
        return g, (gs, gh, gc)

    back_pairs = [(p + 1, p) for p in range(sections - 1)]

    def backward_section(tick, incoming, back0, back1, cotangent):
        def leave(incoming, back0, back1, cotangent):
            return back0, back1, cotangent

        def one(incoming, back0, back1, cotangent):
            cotangent, back0 = back_layer(incoming, 0, kept0, b16)
            return back0, back1, cotangent

        def both(incoming, back0, back1, cotangent):
            g, back1 = back_layer(incoming, 1, kept1, f32)
            cotangent, back0 = back_layer(g, 0, kept0, b16)
            return back0, back1, cotangent

        which = jnp.where(tick == sections - 1 - section_index, layer_count, 0)
        return lax.switch(which, (leave, one, both), incoming, back0, back1, cotangent)

    def backward_tick(tick, state):
        incoming, back0, back1, cotangent = state
        back0, back1, cotangent = backward_section(tick, incoming, back0, back1, cotangent)
        return lax.ppermute(cotangent, "pipe", back_pairs), back0, back1, cotangent

    buffers = unwritten(back_shapes + back_shapes + sent_shapes[:1])
    state = (from_loss, tuple(buffers[:3]), tuple(buffers[3:6]), buffers[6])
    state = lax.fori_loop(0, sections - 1, backward_tick, state)
    back0, back1, cotangent = backward_section(sections - 1, *state)

    found = [
        layer_weights(section_layers, kept, back, slot, *dims)
        for slot, kept, back in ((0, kept0, back0), (1, kept1, back1))
    ]
    firsts, seconds, taps_found = zip(*found)
    w_in_grad = lax.psum(jnp.stack(firsts), "rows")
    w_out_grad = lax.psum(jnp.stack(seconds), "rows")
    kernel_grad = lax.psum(jnp.stack(taps_found), "rows").astype(f32)
    boundary = cotangent.reshape(micros, half, 2, band_rows, width).transpose(0, 3, 2, 1, 4)
    boundary = boundary.reshape(micros, band_rows, cols, width)
    return (boundary[None], kernel_grad, w_in_grad, w_out_grad)


def solution(mesh):
    return jax.shard_map(
        on_device,
        mesh=mesh,
        in_specs=(
            P(None, "rows", None, None),
            P("pipe"),
            P("pipe", None, None),
            P("pipe", None),
            P("pipe", None, None),
            P("pipe", None, None),
            P("pipe", None),
            P(),
            P(None, "rows", None),
        ),
        out_specs=(
            P("pipe", None, "rows", None, None),
            P("pipe", None, None),
            P("pipe", None, None),
            P("pipe", None, None),
        ),
        check_vma=False,
    )
```

```python
import functools
import math

import jax
import jax.numpy as jnp
from jax import lax
from jax.experimental import pallas as pl
from jax.experimental.pallas import tpu as pltpu
from jax.sharding import PartitionSpec as P

root_tau = 1.0 / math.sqrt(2.0 * math.pi)
norm_eps = 1e-06
loss_scale = 1024.0
erf_p = 0.3275911
erf_poly = (1.061405429, -1.453152027, 1.421413741, -0.284496736, 0.254829592)
LANES = 128
SUB = 8
NT = (((1,), (1,)), ((), ()))
TN = (((0,), (0,)), ((), ()))
VMEM_LIMIT = 48 * 1024 * 1024
CHUNK = 256
GELU = jnp.bfloat16
TAP_ROWS = 64


def block_spec(array_rows, shape, micros):
    if array_rows:
        return pl.BlockSpec((shape[0] // micros,) + tuple(shape[1:]), lambda m: (m,) + (0,) * (len(shape) - 1))
    return pl.BlockSpec(shape, lambda m: (0,) * len(shape))


def slot_spec(shape, slot):
    return pl.BlockSpec((None,) + tuple(shape[1:]), lambda m: (slot,) + (0,) * (len(shape) - 1))


def per_micro(body, micros, operands, outs, scratch, flops):
    arrays, specs = [], []
    for item in operands:
        if isinstance(item, tuple):
            arrays.append(item[0])
            specs.append(slot_spec(item[0].shape, item[1]))
        else:
            arrays.append(item)
            specs.append(block_spec(True, item.shape, micros))
    size = sum(math.prod(o[0]) * jnp.dtype(o[1]).itemsize for o in outs)
    size += sum(a.size * a.dtype.itemsize for a in arrays)
    return pl.pallas_call(
        body,
        grid=(micros,),
        in_specs=specs,
        out_specs=[block_spec(True, o[0], micros) for o in outs],
        out_shape=[jax.ShapeDtypeStruct(*o) for o in outs],
        scratch_shapes=scratch,
        compiler_params=pltpu.CompilerParams(vmem_limit_bytes=VMEM_LIMIT),
        cost_estimate=pl.CostEstimate(flops=flops, bytes_accessed=size, transcendentals=0),
    )(*arrays)


def unwritten(shapes):
    return pl.pallas_call(
        lambda *refs: None,
        out_specs=[pl.BlockSpec(memory_space=pl.ANY) for _ in shapes],
        out_shape=[jax.ShapeDtypeStruct(*s) for s in shapes],
    )()


def gelu_pair(h):
    e = jnp.exp(h * h * -0.5)
    t = 1.0 / (1.0 + (erf_p * math.sqrt(0.5)) * jnp.abs(h))
    q = t * (0.5 * erf_poly[0]) + 0.5 * erf_poly[1]
    for coef in erf_poly[2:]:
        q = q * t + 0.5 * coef
    q = q * t * e
    phi = jnp.where(h >= 0.0, 1.0 - q, q)
    return h * phi, phi + h * (e * root_tau)


def spread_taps(taps_ref, wide_taps):
    count, width = taps_ref.shape
    for tap in range(count):
        row = jnp.broadcast_to(taps_ref[tap : tap + 1, :], (2 * SUB, width))
        wide_taps[tap] = row.astype(jnp.bfloat16)


def build_shifts(own_ref, top_ref, bot_ref, cols, halo, shifts):
    planes = halo.shape[0]
    half = cols // 2
    for q in range(3):
        at = pl.ds(q * cols, cols)
        for lane in range(planes):
            lanes = slice(lane * LANES, (lane + 1) * LANES)
            plane = halo.at[lane]
            plane[pl.ds(5 + q, cols, stride=SUB), :] = top_ref[at, lanes].astype(jnp.float32)
            plane[pl.ds(q, cols, stride=SUB), :] = bot_ref[at, lanes].astype(jnp.float32)
    sub = lax.broadcasted_iota(jnp.int32, (SUB, LANES), 0)

    def pair(k, carry):
        for lane in range(planes):
            lanes = slice(lane * LANES, (lane + 1) * LANES)
            at = pl.ds(pl.multiple_of(k * 2 * SUB, 2 * SUB), 2 * SUB)
            own = own_ref[at, lanes].astype(jnp.float32)
            edge = halo[lane, at, :]
            for a in range(7):
                if a == 3:
                    both = own
                else:
                    mask = sub >= 5 + a if a < 3 else sub < a - 3
                    both = jnp.concatenate(
                        [
                            pltpu.roll(
                                jnp.where(mask, edge[h * SUB : (h + 1) * SUB], own[h * SUB : (h + 1) * SUB]),
                                (3 - a) % SUB,
                                0,
                            )
                            for h in range(2)
                        ],
                        axis=0,
                    )
                shifts[a, k + 3, :, lanes] = both.astype(jnp.bfloat16)
        return carry

    lax.fori_loop(0, half, pair, 0, unroll=2)
    blank = jnp.zeros((SUB, planes * LANES), jnp.float32)
    for a in range(7):
        for k in range(3):
            right = shifts[a, k + 3].astype(jnp.float32)[SUB:]
            shifts[a, half + 3 + k] = jnp.concatenate([right, blank], axis=0).astype(jnp.bfloat16)
            left = shifts[a, half + k].astype(jnp.float32)[:SUB]
            shifts[a, k] = jnp.concatenate([blank, left], axis=0).astype(jnp.bfloat16)


def convolve(shifts, wide_taps, flip, cols, width, store):
    for lane in range(width // LANES):
        lanes = slice(lane * LANES, (lane + 1) * LANES)

        def block(kb, carry, lanes=lanes):
            acc = jnp.zeros((8, 2 * SUB, LANES), jnp.float32)
            for a in range(7):
                strip = shifts[a, pl.ds(kb * 8, 14), :, lanes]
                line = None
                for b in range(7):
                    tap = 48 - (a * 7 + b) if flip else a * 7 + b
                    term = strip[b : b + 8] * wide_taps[tap, :, lanes][None]
                    line = term if line is None else line + term
                acc = acc + line.astype(jnp.float32)
            store(pl.ds(pl.multiple_of(kb * 128, 128), 128), lanes, acc.reshape(16 * SUB, LANES))
            return carry

        lax.fori_loop(0, cols // 16, block, 0)


def write_edges(source_ref, etop_ref, ebot_ref, halo, cols):
    for lane in range(halo.shape[0]):
        lanes = slice(lane * LANES, (lane + 1) * LANES)
        plane = halo.at[lane]
        plane[...] = source_ref[:, lanes]
        for q in range(3):
            to = pl.ds(q * cols, cols)
            etop_ref[to, lanes] = plane[pl.ds(q, cols, stride=SUB), :].astype(jnp.bfloat16)
            ebot_ref[to, lanes] = plane[pl.ds(q + 5, cols, stride=SUB), :].astype(jnp.bfloat16)


def row_loop(rows, step, fn):
    def body(i, carry):
        fn(pl.ds(pl.multiple_of(i * step, step), step))
        return carry

    lax.fori_loop(0, rows // step, body, 0)


def conv_scratch(cols, width):
    return [
        pltpu.VMEM((width // LANES, cols * SUB, LANES), jnp.float32),
        pltpu.VMEM((7, cols // 2 + 6, 2 * SUB, width), jnp.bfloat16),
        pltpu.VMEM((49, 2 * SUB, width), jnp.bfloat16),
    ]


def front_body(
    cols,
    x_ref, top_ref, bot_ref, taps_ref, gain_ref, w_in_ref, w_out_ref, scale_ref,
    y_ref, out_ref, etop_ref, ebot_ref, conv_ref, normed_ref, active_ref, slope_ref,
    halo, shifts, wide_taps, hidden,
):
    rows, width = x_ref.shape
    hidden_width = w_in_ref.shape[1]

    @pl.when(pl.program_id(0) == 0)
    def first_step():
        spread_taps(taps_ref, wide_taps)

    build_shifts(x_ref, top_ref, bot_ref, cols, halo, shifts)

    def store(at, lanes, value):
        conv_ref[at, lanes] = value

    convolve(shifts, wide_taps, False, cols, width, store)

    def norm(at):
        conv = conv_ref[at, :]
        centred = conv - jnp.mean(conv, axis=-1, keepdims=True)
        spread = jnp.mean(centred * centred, axis=-1, keepdims=True)
        normed_ref[at, :] = (centred * lax.rsqrt(spread + norm_eps) * gain_ref[...]).astype(
            jnp.bfloat16
        )

    row_loop(rows, 64, norm)
    normed = normed_ref[...]
    chunks = hidden_width // CHUNK

    def expand(n):
        hidden[n % 2] = jnp.dot(
            normed, w_in_ref[:, n * CHUNK : (n + 1) * CHUNK], preferred_element_type=jnp.float32
        )

    expand(0)
    for n in range(chunks):
        if n + 1 < chunks:
            expand(n + 1)
        lanes = slice(n * CHUNK, (n + 1) * CHUNK)
        for i in range(rows // 32):
            at = slice(i * 32, (i + 1) * 32)
            value, slope = gelu_pair(hidden[n % 2, at, :].astype(GELU))
            active_ref[at, lanes] = value.astype(jnp.bfloat16)
            slope_ref[at, lanes] = slope.astype(jnp.bfloat16)
    y_ref[...] = x_ref[...].astype(jnp.float32) + scale_ref[...] * jnp.dot(
        active_ref[...], w_out_ref[...], preferred_element_type=jnp.float32
    )
    out_ref[...] = y_ref[...].astype(jnp.bfloat16)
    write_edges(y_ref, etop_ref, ebot_ref, halo, cols)


def layer_front(x, top, bot, params, slot, micros, cols):
    taps, gains, w_in, w_out, scales = params
    rows, width = x.shape
    hidden_width = w_in.shape[2]
    f32, b16 = jnp.float32, jnp.bfloat16
    return per_micro(
        functools.partial(front_body, cols),
        micros,
        (x, top, bot, (taps, slot), (gains, slot), (w_in, slot), (w_out, slot), (scales, slot)),
        [
            ((rows, width), f32), ((rows, width), b16), (top.shape, b16), (bot.shape, b16),
            ((rows, width), f32), ((rows, width), b16),
            ((rows, hidden_width), b16), ((rows, hidden_width), b16),
        ],
        conv_scratch(cols, width) + [pltpu.VMEM((2, rows // micros, CHUNK), f32)],
        4 * rows * width * hidden_width,
    )


def point_body(
    cols,
    g_ref, conv_ref, slope_ref, gain_ref, w_in_ref, w_out_ref, scale_ref,
    gs_ref, gh_ref, gc_ref, etop_ref, ebot_ref, wide, halo,
):
    rows, width = g_ref.shape
    hidden_width = w_in_ref.shape[1]
    gs_ref[...] = (scale_ref[...] * g_ref[...].astype(jnp.float32)).astype(jnp.bfloat16)
    grad = gs_ref[...]
    chunks = hidden_width // CHUNK

    def expand(n):
        wide[n % 2] = lax.dot_general(
            grad, w_out_ref[n * CHUNK : (n + 1) * CHUNK, :], NT, preferred_element_type=jnp.float32
        )

    expand(0)
    for n in range(chunks):
        if n + 1 < chunks:
            expand(n + 1)
        lanes = slice(n * CHUNK, (n + 1) * CHUNK)
        for i in range(rows // 32):
            at = slice(i * 32, (i + 1) * 32)
            gh_ref[at, lanes] = (wide[n % 2, at, :] * slope_ref[at, lanes].astype(jnp.float32)).astype(
                jnp.bfloat16
            )
    gc_ref[...] = lax.dot_general(gh_ref[...], w_in_ref[...], NT, preferred_element_type=jnp.float32)

    def norm_back(at):
        conv = conv_ref[at, :]
        centred = conv - jnp.mean(conv, axis=-1, keepdims=True)
        spread = jnp.mean(centred * centred, axis=-1, keepdims=True)
        scale = lax.rsqrt(spread + norm_eps)
        unit = centred * scale
        grad = gc_ref[at, :] * gain_ref[...]
        first = jnp.mean(grad, axis=-1, keepdims=True)
        second = jnp.mean(grad * unit, axis=-1, keepdims=True)
        gc_ref[at, :] = scale * (grad - first - unit * second)

    row_loop(rows, 64, norm_back)
    write_edges(gc_ref, etop_ref, ebot_ref, halo, cols)


def layer_point(g, conv, slope, params, slot, micros, cols):
    taps, gains, w_in, w_out, scales = params
    rows, width = g.shape
    hidden_width = w_in.shape[2]
    f32, b16 = jnp.float32, jnp.bfloat16
    edge = (micros * 3 * cols, width)
    return per_micro(
        functools.partial(point_body, cols),
        micros,
        (g, conv, slope, (gains, slot), (w_in, slot), (w_out, slot), (scales, slot)),
        [((rows, width), b16), ((rows, hidden_width), b16), ((rows, width), f32), (edge, b16), (edge, b16)],
        [
            pltpu.VMEM((2, rows // micros, CHUNK), f32),
            pltpu.VMEM((width // LANES, cols * SUB, LANES), f32),
        ],
        4 * rows * width * hidden_width,
    )


def spread_body(
    cols, g_ref, gc_ref, top_ref, bot_ref, taps_ref, out_ref, halo, shifts, wide_taps
):
    @pl.when(pl.program_id(0) == 0)
    def first_step():
        spread_taps(taps_ref, wide_taps)

    build_shifts(gc_ref, top_ref, bot_ref, cols, halo, shifts)

    def store(at, lanes, value):
        out_ref[at, lanes] = (g_ref[at, lanes].astype(jnp.float32) + value).astype(out_ref.dtype)

    convolve(shifts, wide_taps, True, cols, g_ref.shape[1], store)


def layer_spread(g, gc, top, bot, params, slot, micros, cols, dtype):
    rows, width = g.shape
    return per_micro(
        functools.partial(spread_body, cols),
        micros,
        (g, gc, top, bot, (params[0], slot)),
        [((rows, width), dtype)],
        conv_scratch(cols, width),
        98 * rows * width,
    )[0]


def weight_body(
    micros, cols, slot,
    count_ref, x_ref, top_ref, bot_ref, gc_ref, normed_ref, gh_ref, active_ref, gs_ref,
    first_ref, second_ref, halo, shifts, sums,
):
    hidden_width = gh_ref.shape[1]
    width = x_ref.shape[1]
    applied = slot < count_ref[0]

    @pl.when(jnp.logical_not(applied))
    def passed():
        first_ref[...] = jnp.zeros_like(first_ref)
        second_ref[...] = jnp.zeros_like(second_ref)

    @pl.when(applied)
    def run():
        first_ref[...] = lax.dot_general(
            normed_ref[...], gh_ref[...], TN, preferred_element_type=jnp.float32
        ).astype(jnp.bfloat16)
        second_ref[:hidden_width, :] = lax.dot_general(
            active_ref[...], gs_ref[...], TN, preferred_element_type=jnp.float32
        ).astype(jnp.bfloat16)
        pixels = cols * SUB
        for m in range(micros):
            at_edge = pl.ds(m * 3 * cols, 3 * cols)
            build_shifts(
                x_ref.at[pl.ds(m * pixels, pixels)], top_ref.at[at_edge], bot_ref.at[at_edge],
                cols, halo, shifts,
            )
            for lane in range(width // LANES):
                lanes = slice(lane * LANES, (lane + 1) * LANES)

                def tap_row(a, carry, lanes=lanes, m=m):
                    found = [jnp.zeros((2 * SUB, LANES), jnp.float32) for _ in range(7)]
                    for kb in range(cols // 16):
                        strip = shifts[a, kb * 8 : kb * 8 + 14, :, lanes]
                        at = pl.ds(m * pixels + kb * 128, 128)
                        grad = gc_ref[at, lanes].astype(jnp.bfloat16).reshape(8, 2 * SUB, LANES)
                        for b in range(7):
                            term = strip[b : b + 8] * grad
                            term = (term[0] + term[1]) + (term[2] + term[3]), (term[4] + term[5]) + (term[6] + term[7])
                            found[b] = found[b] + (term[0].astype(jnp.float32) + term[1].astype(jnp.float32))
                    for b in range(7):
                        total = found[b][:SUB] + found[b][SUB:]
                        if m == 0:
                            sums[a * 7 + b, :, lanes] = total
                        else:
                            sums[a * 7 + b, :, lanes] += total
                    return carry

                lax.fori_loop(0, 7, tap_row, 0)
        taps = jnp.sum(sums[...], axis=1)
        fill = jnp.zeros((TAP_ROWS - taps.shape[0], width), jnp.float32)
        second_ref[hidden_width:, :] = jnp.concatenate([taps, fill], axis=0).astype(jnp.bfloat16)


def layer_weights(count, kept, back, slot, micros, cols):
    x, top, bot, _, normed, active, _ = kept
    gs, gh, gc = back
    rows, width = x.shape
    hidden_width = gh.shape[1]
    f32, b16 = jnp.float32, jnp.bfloat16
    arrays = (x, top, bot, gc, normed, gh, active, gs)
    outs = [((width, hidden_width), b16), ((hidden_width + TAP_ROWS, width), b16)]
    size = sum(math.prod(o[0]) * jnp.dtype(o[1]).itemsize for o in outs)
    size += sum(a.size * a.dtype.itemsize for a in arrays)
    return pl.pallas_call(
        functools.partial(weight_body, micros, cols, slot),
        grid=(1,),
        in_specs=[pl.BlockSpec(memory_space=pltpu.SMEM)] + [block_spec(False, a.shape, 1) for a in arrays],
        out_specs=[block_spec(False, o[0], 1) for o in outs],
        out_shape=[jax.ShapeDtypeStruct(*o) for o in outs],
        scratch_shapes=conv_scratch(cols, width)[:2] + [pltpu.VMEM((49, SUB, width), f32)],
        compiler_params=pltpu.CompilerParams(vmem_limit_bytes=VMEM_LIMIT),
        cost_estimate=pl.CostEstimate(
            flops=4 * rows * width * hidden_width, bytes_accessed=size, transcendentals=0
        ),
    )(count, *arrays)


def loss_body(factor, y_ref, head_ref, labels_ref, g_ref):
    logits = jnp.dot(y_ref[...], head_ref[...], preferred_element_type=jnp.float32)
    spots = lax.broadcasted_iota(jnp.int32, logits.shape, 1)
    target = (labels_ref[...] == spots).astype(jnp.float32)
    grad = (factor * (logits - target)).astype(jnp.bfloat16)
    g_ref[...] = lax.dot_general(
        grad, head_ref[...], NT, preferred_element_type=jnp.float32
    ).astype(jnp.bfloat16)


def on_device(features, section_layers, kernels, gains, w_in, w_out, scales, head_weight, labels):
    sections = lax.axis_size("pipe")
    section_index = lax.axis_index("pipe")
    bands = lax.axis_size("rows")
    micros, band_rows, cols, width = features.shape
    hidden_width = w_in.shape[2]
    classes = head_weight.shape[1]
    layer_count = section_layers[0]
    rows = micros * band_rows * cols
    half = cols // 2
    f32, b16 = jnp.float32, jnp.bfloat16
    params = (kernels, gains[:, None, :], w_in, w_out, scales[:, None, :])
    dims = (micros, cols)
    edge_shape = (micros * 3 * cols, width)

    up = [(i, i + 1) for i in range(bands - 1)]
    down = [(i + 1, i) for i in range(bands - 1)]

    def halo(etop, ebot):
        return lax.ppermute(ebot, "rows", up), lax.ppermute(etop, "rows", down)

    def hop(x, etop, ebot):
        def pairs(by):
            return [
                (p * bands + r, (p + 1) * bands + r + by)
                for p in range(sections - 1)
                for r in range(bands)
                if 0 <= r + by < bands
            ]

        axes = ("pipe", "rows")
        return (
            lax.ppermute(x, axes, pairs(0)),
            lax.ppermute(ebot, axes, pairs(1)),
            lax.ppermute(etop, axes, pairs(-1)),
        )

    def edge_rows(part):
        part = part.reshape(micros, 3, 2, half, width).transpose(0, 1, 3, 2, 4)
        return part.reshape(edge_shape)

    first_x = features.reshape(micros, band_rows, 2, half, width).transpose(0, 3, 2, 1, 4)
    first_in = (
        first_x.reshape(rows, width),
        *halo(edge_rows(features[:, :3]), edge_rows(features[:, band_rows - 3 :])),
    )

    def kept_shapes(dtype_x):
        return [
            ((rows, width), dtype_x), (edge_shape, b16), (edge_shape, b16), ((rows, width), f32),
            ((rows, width), b16), ((rows, hidden_width), b16), ((rows, hidden_width), b16),
        ]

    sent_shapes = [((rows, width), b16), (edge_shape, b16), (edge_shape, b16)]
    back_shapes = [((rows, width), b16), ((rows, hidden_width), b16), ((rows, width), f32)]

    def front(x, top, bot, slot):
        y, out, etop, ebot, conv, normed, active, slope = layer_front(x, top, bot, params, slot, *dims)
        return y, (out, etop, ebot), (x, top, bot, conv, normed, active, slope)

    def forward_section(tick, received, kept0, kept1, sent):
        def leave(received, kept0, kept1, sent):
            return kept0, kept1, sent

        def one(received, kept0, kept1, sent):
            _, sent, kept0 = front(*received, 0)
            return kept0, kept1, sent

        def both(received, kept0, kept1, sent):
            y, (_, etop, ebot), kept0 = front(*received, 0)
            _, sent, kept1 = front(y, *halo(etop, ebot), 1)
            return kept0, kept1, sent

        which = jnp.where(tick == section_index, layer_count, 0)
        return lax.switch(which, (leave, one, both), received, kept0, kept1, sent)

    def forward_tick(tick, state):
        received, kept0, kept1, sent = state
        kept0, kept1, sent = forward_section(tick, received, kept0, kept1, sent)
        return hop(*sent), kept0, kept1, sent

    buffers = unwritten(kept_shapes(b16) + kept_shapes(f32) + sent_shapes)
    state = (first_in, tuple(buffers[:7]), tuple(buffers[7:14]), tuple(buffers[14:]))
    state = lax.fori_loop(0, sections - 1, forward_tick, state)
    kept0, kept1, sent = forward_section(sections - 1, *state)

    total = micros * band_rows * bands * cols
    pixel_labels = labels.reshape(micros, band_rows, 2, half).transpose(0, 3, 2, 1).reshape(rows, 1)
    from_loss = pl.pallas_call(
        functools.partial(loss_body, loss_scale * 2.0 / total),
        out_shape=jax.ShapeDtypeStruct((rows, width), b16),
    )(sent[0], head_weight, pixel_labels)

    def back_layer(g, slot, kept, dtype):
        gs, gh, gc, etop, ebot = layer_point(g, kept[3], kept[6], params, slot, *dims)
        g = layer_spread(g, gc, *halo(etop, ebot), params, slot, *dims, dtype)
        return g, (gs, gh, gc)

    back_pairs = [(p + 1, p) for p in range(sections - 1)]

    def backward_section(tick, incoming, back0, back1, cotangent):
        def leave(incoming, back0, back1, cotangent):
            return back0, back1, cotangent

        def one(incoming, back0, back1, cotangent):
            cotangent, back0 = back_layer(incoming, 0, kept0, b16)
            return back0, back1, cotangent

        def both(incoming, back0, back1, cotangent):
            g, back1 = back_layer(incoming, 1, kept1, f32)
            cotangent, back0 = back_layer(g, 0, kept0, b16)
            return back0, back1, cotangent

        which = jnp.where(tick == sections - 1 - section_index, layer_count, 0)
        return lax.switch(which, (leave, one, both), incoming, back0, back1, cotangent)

    def backward_tick(tick, state):
        incoming, back0, back1, cotangent = state
        back0, back1, cotangent = backward_section(tick, incoming, back0, back1, cotangent)
        return lax.ppermute(cotangent, "pipe", back_pairs), back0, back1, cotangent

    buffers = unwritten(back_shapes + back_shapes + sent_shapes[:1])
    state = (from_loss, tuple(buffers[:3]), tuple(buffers[3:6]), buffers[6])
    state = lax.fori_loop(0, sections - 1, backward_tick, state)
    incoming, back0, back1, cotangent = state

    owner = section_index == 0
    g, back1 = lax.cond(
        owner & (layer_count > 1),
        lambda g, back1: back_layer(g, 1, kept1, f32),
        lambda g, back1: (g.astype(f32), back1),
        incoming, back1,
    )
    sum1 = lax.psum(layer_weights(section_layers, kept1, back1, 1, *dims), "rows")

    def last_point(g, back0, sent):
        gs, gh, gc, etop, ebot = layer_point(g, kept0[3], kept0[6], params, 0, *dims)
        return (gs, gh, gc), halo(etop, ebot)

    back0, edges = lax.cond(
        owner, last_point, lambda g, back0, sent: (back0, sent[1:]), g, back0, tuple(sent)
    )
    part0 = layer_weights(section_layers, kept0, back0, 0, *dims)
    part0, sum1 = lax.optimization_barrier((part0, sum1))
    sum0 = lax.psum(part0, "rows")
    cotangent = lax.cond(
        owner,
        lambda g, edges, gc, cotangent: layer_spread(g, gc, *edges, params, 0, *dims, b16),
        lambda g, edges, gc, cotangent: cotangent,
        g, edges, back0[2], cotangent,
    )
    w_in_grad, tall = (jnp.stack(pair) for pair in zip(sum0, sum1))
    w_out_grad = tall[:, :hidden_width]
    kernel_grad = tall[:, hidden_width : hidden_width + kernels.shape[1]].astype(f32)
    boundary = cotangent.reshape(micros, half, 2, band_rows, width).transpose(0, 3, 2, 1, 4)
    boundary = boundary.reshape(micros, band_rows, cols, width)
    return (boundary[None], kernel_grad, w_in_grad, w_out_grad)


def solution(mesh):
    return jax.shard_map(
        on_device,
        mesh=mesh,
        in_specs=(
            P(None, "rows", None, None),
            P("pipe"),
            P("pipe", None, None),
            P("pipe", None),
            P("pipe", None, None),
            P("pipe", None, None),
            P("pipe", None),
            P(),
            P(None, "rows", None),
        ),
        out_specs=(
            P("pipe", None, "rows", None, None),
            P("pipe", None, None),
            P("pipe", None, None),
            P("pipe", None, None),
        ),
        check_vma=False,
    )
```

```python
import functools
import math

import jax
import jax.numpy as jnp
from jax import lax
from jax.experimental import pallas as pl
from jax.experimental.pallas import tpu as pltpu
from jax.sharding import PartitionSpec as P

root_tau = 1.0 / math.sqrt(2.0 * math.pi)
norm_eps = 1e-06
loss_scale = 1024.0
erf_p = 0.3275911
erf_poly = (1.061405429, -1.453152027, 1.421413741, -0.284496736, 0.254829592)
LANES = 128
SUB = 8
NT = (((1,), (1,)), ((), ()))
TN = (((0,), (0,)), ((), ()))
VMEM_LIMIT = 48 * 1024 * 1024
CHUNK = 256
GELU = jnp.bfloat16
TAP_ROWS = 64


def whole_spec(shape):
    return pl.BlockSpec(shape, lambda *_: (0,) * len(shape))


def slot_spec(shape, slot):
    return pl.BlockSpec((None,) + tuple(shape[1:]), lambda *_: (slot,) + (0,) * (len(shape) - 1))


def micro_spec(shape, micros):
    return pl.BlockSpec((shape[0] // micros,) + tuple(shape[1:]), lambda _, at: (at[0], 0))


def one_micro(body, micros, at, operands, parts, stores, outs, scratch, flops):
    arrays, specs = [], []
    for item in operands:
        if isinstance(item, tuple):
            arrays.append(item[0])
            specs.append(slot_spec(item[0].shape, item[1]))
        else:
            arrays.append(item)
            specs.append(whole_spec(item.shape))
    arrays += list(parts)
    specs += [micro_spec(p.shape, micros) for p in parts]
    first = 1 + len(arrays)
    skip = len(stores)
    count = len(arrays)

    def run(at_ref, *refs):
        body(at_ref, *refs[:count], *refs[count + skip :])

    size = sum(math.prod(o[0]) * jnp.dtype(o[1]).itemsize for o in outs)
    size += sum(a.size * a.dtype.itemsize for a in arrays)
    return pl.pallas_call(
        run,
        grid_spec=pltpu.PrefetchScalarGridSpec(
            num_scalar_prefetch=1,
            grid=(1,),
            in_specs=specs + [pl.BlockSpec(memory_space=pl.ANY) for _ in stores],
            out_specs=[micro_spec(t.shape, micros) for t in stores] + [whole_spec(o[0]) for o in outs],
            scratch_shapes=scratch,
        ),
        out_shape=[jax.ShapeDtypeStruct(t.shape, t.dtype) for t in stores]
        + [jax.ShapeDtypeStruct(*o) for o in outs],
        input_output_aliases={first + i: i for i in range(len(stores))},
        compiler_params=pltpu.CompilerParams(vmem_limit_bytes=VMEM_LIMIT),
        cost_estimate=pl.CostEstimate(flops=flops, bytes_accessed=size, transcendentals=0),
    )(at, *arrays, *stores)


def unwritten(shapes):
    return pl.pallas_call(
        lambda *refs: None,
        out_specs=[pl.BlockSpec(memory_space=pl.ANY) for _ in shapes],
        out_shape=[jax.ShapeDtypeStruct(*s) for s in shapes],
    )()


def gelu_pair(h):
    e = jnp.exp(h * h * -0.5)
    t = 1.0 / (1.0 + (erf_p * math.sqrt(0.5)) * jnp.abs(h))
    q = t * (0.5 * erf_poly[0]) + 0.5 * erf_poly[1]
    for coef in erf_poly[2:]:
        q = q * t + 0.5 * coef
    q = q * t * e
    phi = jnp.where(h >= 0.0, 1.0 - q, q)
    return h * phi, phi + h * (e * root_tau)


def spread_taps(taps_ref, wide_taps):
    count, width = taps_ref.shape
    for tap in range(count):
        row = jnp.broadcast_to(taps_ref[tap : tap + 1, :], (2 * SUB, width))
        wide_taps[tap] = row.astype(jnp.bfloat16)


def build_shifts(own_ref, top_ref, bot_ref, cols, halo, shifts):
    planes = halo.shape[0]
    half = cols // 2
    for q in range(3):
        at = pl.ds(q * cols, cols)
        for lane in range(planes):
            lanes = slice(lane * LANES, (lane + 1) * LANES)
            plane = halo.at[lane]
            plane[pl.ds(5 + q, cols, stride=SUB), :] = top_ref[at, lanes].astype(jnp.float32)
            plane[pl.ds(q, cols, stride=SUB), :] = bot_ref[at, lanes].astype(jnp.float32)
    sub = lax.broadcasted_iota(jnp.int32, (SUB, LANES), 0)

    def pair(k, carry):
        for lane in range(planes):
            lanes = slice(lane * LANES, (lane + 1) * LANES)
            at = pl.ds(pl.multiple_of(k * 2 * SUB, 2 * SUB), 2 * SUB)
            own = own_ref[at, lanes].astype(jnp.float32)
            edge = halo[lane, at, :]
            for a in range(7):
                if a == 3:
                    both = own
                else:
                    mask = sub >= 5 + a if a < 3 else sub < a - 3
                    both = jnp.concatenate(
                        [
                            pltpu.roll(
                                jnp.where(mask, edge[h * SUB : (h + 1) * SUB], own[h * SUB : (h + 1) * SUB]),
                                (3 - a) % SUB,
                                0,
                            )
                            for h in range(2)
                        ],
                        axis=0,
                    )
                shifts[a, k + 3, :, lanes] = both.astype(jnp.bfloat16)
        return carry

    lax.fori_loop(0, half, pair, 0, unroll=2)
    blank = jnp.zeros((SUB, planes * LANES), jnp.float32)
    for a in range(7):
        for k in range(3):
            right = shifts[a, k + 3].astype(jnp.float32)[SUB:]
            shifts[a, half + 3 + k] = jnp.concatenate([right, blank], axis=0).astype(jnp.bfloat16)
            left = shifts[a, half + k].astype(jnp.float32)[:SUB]
            shifts[a, k] = jnp.concatenate([blank, left], axis=0).astype(jnp.bfloat16)


def convolve(shifts, wide_taps, flip, cols, width, store):
    for lane in range(width // LANES):
        lanes = slice(lane * LANES, (lane + 1) * LANES)

        def block(kb, carry, lanes=lanes):
            acc = jnp.zeros((8, 2 * SUB, LANES), jnp.float32)
            for a in range(7):
                strip = shifts[a, pl.ds(kb * 8, 14), :, lanes]
                line = None
                for b in range(7):
                    tap = 48 - (a * 7 + b) if flip else a * 7 + b
                    term = strip[b : b + 8] * wide_taps[tap, :, lanes][None]
                    line = term if line is None else line + term
                acc = acc + line.astype(jnp.float32)
            store(pl.ds(pl.multiple_of(kb * 128, 128), 128), lanes, acc.reshape(16 * SUB, LANES))
            return carry

        lax.fori_loop(0, cols // 16, block, 0)


def write_edges(source_ref, etop_ref, ebot_ref, halo, cols):
    for lane in range(halo.shape[0]):
        lanes = slice(lane * LANES, (lane + 1) * LANES)
        plane = halo.at[lane]
        plane[...] = source_ref[:, lanes]
        for q in range(3):
            to = pl.ds(q * cols, cols)
            etop_ref[to, lanes] = plane[pl.ds(q, cols, stride=SUB), :].astype(jnp.bfloat16)
            ebot_ref[to, lanes] = plane[pl.ds(q + 5, cols, stride=SUB), :].astype(jnp.bfloat16)


def row_loop(rows, step, fn):
    def body(i, carry):
        fn(pl.ds(pl.multiple_of(i * step, step), step))
        return carry

    lax.fori_loop(0, rows // step, body, 0)


def conv_scratch(cols, width):
    return [
        pltpu.VMEM((width // LANES, cols * SUB, LANES), jnp.float32),
        pltpu.VMEM((7, cols // 2 + 6, 2 * SUB, width), jnp.bfloat16),
        pltpu.VMEM((49, 2 * SUB, width), jnp.bfloat16),
    ]


def front_body(
    cols, slot,
    at_ref, *refs,
):
    if slot == 0:
        in_x_ref, in_top_ref, in_bot_ref, *refs = refs
    else:
        x_ref, in_top_ref, in_bot_ref, *refs = refs
    taps_ref, gain_ref, w_in_ref, w_out_ref, scale_ref, *refs = refs
    if slot == 0:
        first_x_ref, first_top_ref, first_bot_ref, *refs = refs
    kept_x_ref, top_ref, bot_ref, conv_ref, normed_ref, active_ref, slope_ref, *refs = refs
    y_ref, out_ref, etop_ref, ebot_ref, halo, shifts, wide_taps, hidden = refs
    rows, width = kept_x_ref.shape
    hidden_width = w_in_ref.shape[1]
    if slot == 0:
        x_ref = kept_x_ref

        @pl.when(at_ref[1] == 1)
        def from_features():
            kept_x_ref[...] = first_x_ref[...]
            top_ref[...] = first_top_ref[...]
            bot_ref[...] = first_bot_ref[...]

        @pl.when(at_ref[1] == 0)
        def from_section():
            kept_x_ref[...] = in_x_ref[...]
            top_ref[...] = in_top_ref[...]
            bot_ref[...] = in_bot_ref[...]

    else:
        kept_x_ref[...] = x_ref[...].astype(jnp.bfloat16)
        top_ref[...] = in_top_ref[...]
        bot_ref[...] = in_bot_ref[...]
    spread_taps(taps_ref, wide_taps)
    build_shifts(kept_x_ref, top_ref, bot_ref, cols, halo, shifts)

    def store(at, lanes, value):
        conv_ref[at, lanes] = value

    convolve(shifts, wide_taps, False, cols, width, store)

    def norm(at):
        conv = conv_ref[at, :]
        centred = conv - jnp.mean(conv, axis=-1, keepdims=True)
        spread = jnp.mean(centred * centred, axis=-1, keepdims=True)
        normed_ref[at, :] = (centred * lax.rsqrt(spread + norm_eps) * gain_ref[...]).astype(
            jnp.bfloat16
        )

    row_loop(rows, 64, norm)
    normed = normed_ref[...]
    chunks = hidden_width // CHUNK

    def expand(n):
        hidden[n % 2] = jnp.dot(
            normed, w_in_ref[:, n * CHUNK : (n + 1) * CHUNK], preferred_element_type=jnp.float32
        )

    expand(0)
    for n in range(chunks):
        if n + 1 < chunks:
            expand(n + 1)
        lanes = slice(n * CHUNK, (n + 1) * CHUNK)
        for i in range(rows // 32):
            at = slice(i * 32, (i + 1) * 32)
            value, slope = gelu_pair(hidden[n % 2, at, :].astype(GELU))
            active_ref[at, lanes] = value.astype(jnp.bfloat16)
            slope_ref[at, lanes] = slope.astype(jnp.bfloat16)
    y_ref[...] = x_ref[...].astype(jnp.float32) + scale_ref[...] * jnp.dot(
        active_ref[...], w_out_ref[...], preferred_element_type=jnp.float32
    )
    out_ref[...] = y_ref[...].astype(jnp.bfloat16)
    write_edges(y_ref, etop_ref, ebot_ref, halo, cols)


def layer_front(at, x, top, bot, first_in, kept, params, slot, micros, cols):
    taps, gains, w_in, w_out, scales = params
    rows, width = x.shape
    hidden_width = w_in.shape[2]
    f32, b16 = jnp.float32, jnp.bfloat16
    found = one_micro(
        functools.partial(front_body, cols, slot),
        micros,
        at,
        (x, top, bot, (taps, slot), (gains, slot), (w_in, slot), (w_out, slot), (scales, slot)),
        first_in if slot == 0 else (),
        kept,
        [((rows, width), f32), ((rows, width), b16), (top.shape, b16), (bot.shape, b16)],
        conv_scratch(cols, width) + [pltpu.VMEM((2, rows, CHUNK), f32)],
        4 * rows * width * hidden_width,
    )
    y, out, etop, ebot = found[7:]
    return y, (out, etop, ebot), tuple(found[:7])


def point_body(
    cols,
    at_ref, g_ref, gain_ref, w_in_ref, w_out_ref, scale_ref, conv_ref, slope_ref,
    gs_ref, gh_ref, gc_ref, etop_ref, ebot_ref, wide, halo,
):
    rows, width = g_ref.shape
    hidden_width = w_in_ref.shape[1]
    gs_ref[...] = (scale_ref[...] * g_ref[...].astype(jnp.float32)).astype(jnp.bfloat16)
    grad = gs_ref[...]
    chunks = hidden_width // CHUNK

    def expand(n):
        wide[n % 2] = lax.dot_general(
            grad, w_out_ref[n * CHUNK : (n + 1) * CHUNK, :], NT, preferred_element_type=jnp.float32
        )

    expand(0)
    for n in range(chunks):
        if n + 1 < chunks:
            expand(n + 1)
        lanes = slice(n * CHUNK, (n + 1) * CHUNK)
        for i in range(rows // 32):
            at = slice(i * 32, (i + 1) * 32)
            gh_ref[at, lanes] = (wide[n % 2, at, :] * slope_ref[at, lanes].astype(jnp.float32)).astype(
                jnp.bfloat16
            )
    gc_ref[...] = lax.dot_general(gh_ref[...], w_in_ref[...], NT, preferred_element_type=jnp.float32)

    def norm_back(at):
        conv = conv_ref[at, :]
        centred = conv - jnp.mean(conv, axis=-1, keepdims=True)
        spread = jnp.mean(centred * centred, axis=-1, keepdims=True)
        scale = lax.rsqrt(spread + norm_eps)
        unit = centred * scale
        grad = gc_ref[at, :] * gain_ref[...]
        first = jnp.mean(grad, axis=-1, keepdims=True)
        second = jnp.mean(grad * unit, axis=-1, keepdims=True)
        gc_ref[at, :] = scale * (grad - first - unit * second)

    row_loop(rows, 64, norm_back)
    write_edges(gc_ref, etop_ref, ebot_ref, halo, cols)


def layer_point(at, g, kept, back, params, slot, micros, cols):
    taps, gains, w_in, w_out, scales = params
    rows, width = g.shape
    hidden_width = w_in.shape[2]
    edge = ((3 * cols, width), jnp.bfloat16)
    found = one_micro(
        functools.partial(point_body, cols),
        micros,
        at,
        (g, (gains, slot), (w_in, slot), (w_out, slot), (scales, slot)),
        (kept[3], kept[6]),
        back,
        [edge, edge],
        [
            pltpu.VMEM((2, rows, CHUNK), jnp.float32),
            pltpu.VMEM((width // LANES, cols * SUB, LANES), jnp.float32),
        ],
        4 * rows * width * hidden_width,
    )
    return tuple(found[:3]), found[3:]


def spread_body(cols, at_ref, g_ref, top_ref, bot_ref, taps_ref, gc_ref, *refs):
    *out_refs, halo, shifts, wide_taps = refs
    spread_taps(taps_ref, wide_taps)
    build_shifts(gc_ref, top_ref, bot_ref, cols, halo, shifts)

    def store(at, lanes, value):
        value = g_ref[at, lanes].astype(jnp.float32) + value
        for out_ref in out_refs:
            out_ref[at, lanes] = value.astype(out_ref.dtype)

    convolve(shifts, wide_taps, True, cols, g_ref.shape[1], store)


def layer_spread(at, g, gc, top, bot, stores, params, slot, micros, cols, dtype):
    rows, width = g.shape
    return one_micro(
        functools.partial(spread_body, cols),
        micros,
        at,
        (g, top, bot, (params[0], slot)),
        (gc,),
        stores,
        [((rows, width), dtype)],
        conv_scratch(cols, width),
        98 * rows * width,
    )


def weight_body(
    micros, cols, slot,
    count_ref, x_ref, top_ref, bot_ref, gc_ref, normed_ref, gh_ref, active_ref, gs_ref,
    *refs,
):
    first_ref, second_ref, halo, shifts, sums = refs[-5:]
    hidden_width = gh_ref.shape[1]
    width = x_ref.shape[1]
    applied = slot < count_ref[0]

    @pl.when(jnp.logical_not(applied))
    def passed():
        first_ref[...] = jnp.zeros_like(first_ref)
        second_ref[...] = jnp.zeros_like(second_ref)

    @pl.when(applied)
    def run():
        first_ref[...] = lax.dot_general(
            normed_ref[...], gh_ref[...], TN, preferred_element_type=jnp.float32
        ).astype(jnp.bfloat16)
        second_ref[:hidden_width, :] = lax.dot_general(
            active_ref[...], gs_ref[...], TN, preferred_element_type=jnp.float32
        ).astype(jnp.bfloat16)
        pixels = cols * SUB
        for m in range(micros):
            at_edge = pl.ds(m * 3 * cols, 3 * cols)
            build_shifts(
                x_ref.at[pl.ds(m * pixels, pixels)], top_ref.at[at_edge], bot_ref.at[at_edge],
                cols, halo, shifts,
            )
            for lane in range(width // LANES):
                lanes = slice(lane * LANES, (lane + 1) * LANES)

                def tap_row(a, carry, lanes=lanes, m=m):
                    found = [jnp.zeros((2 * SUB, LANES), jnp.float32) for _ in range(7)]
                    for kb in range(cols // 16):
                        strip = shifts[a, kb * 8 : kb * 8 + 14, :, lanes]
                        at = pl.ds(m * pixels + kb * 128, 128)
                        grad = gc_ref[at, lanes].astype(jnp.bfloat16).reshape(8, 2 * SUB, LANES)
                        for b in range(7):
                            term = strip[b : b + 8] * grad
                            term = (term[0] + term[1]) + (term[2] + term[3]), (term[4] + term[5]) + (term[6] + term[7])
                            found[b] = found[b] + (term[0].astype(jnp.float32) + term[1].astype(jnp.float32))
                    for b in range(7):
                        total = found[b][:SUB] + found[b][SUB:]
                        if m == 0:
                            sums[a * 7 + b, :, lanes] = total
                        else:
                            sums[a * 7 + b, :, lanes] += total
                    return carry

                lax.fori_loop(0, 7, tap_row, 0)
        taps = jnp.sum(sums[...], axis=1)
        fill = jnp.zeros((TAP_ROWS - taps.shape[0], width), jnp.float32)
        second_ref[hidden_width:, :] = jnp.concatenate([taps, fill], axis=0).astype(jnp.bfloat16)


def layer_weights(count, kept, back, stacked, slots, slot, micros, cols):
    x, top, bot, _, normed, active, _ = kept
    gs, gh, gc = back
    rows, width = x.shape
    hidden_width = gh.shape[1]
    f32, b16 = jnp.float32, jnp.bfloat16
    arrays = (x, top, bot, gc, normed, gh, active, gs)
    shapes = [(slots, width, hidden_width), (slots, hidden_width + TAP_ROWS, width)]
    size = sum(math.prod(o[1:]) * 2 for o in shapes) + sum(a.size * a.dtype.itemsize for a in arrays)
    return pl.pallas_call(
        functools.partial(weight_body, micros, cols, slot),
        grid=(1,),
        in_specs=[pl.BlockSpec(memory_space=pltpu.SMEM)]
        + [whole_spec(a.shape) for a in arrays]
        + [pl.BlockSpec(memory_space=pl.ANY) for _ in stacked],
        out_specs=[slot_spec(o, slot) for o in shapes],
        out_shape=[jax.ShapeDtypeStruct(o, b16) for o in shapes],
        input_output_aliases={1 + len(arrays) + i: i for i in range(len(stacked))},
        scratch_shapes=conv_scratch(cols, width)[:2] + [pltpu.VMEM((49, SUB, width), f32)],
        compiler_params=pltpu.CompilerParams(vmem_limit_bytes=VMEM_LIMIT),
        cost_estimate=pl.CostEstimate(
            flops=4 * rows * width * hidden_width, bytes_accessed=size, transcendentals=0
        ),
    )(count, *arrays, *stacked)


def loss_body(factor, y_ref, head_ref, labels_ref, g_ref):
    logits = jnp.dot(y_ref[...], head_ref[...], preferred_element_type=jnp.float32)
    spots = lax.broadcasted_iota(jnp.int32, logits.shape, 1)
    target = (labels_ref[...] == spots).astype(jnp.float32)
    grad = (factor * (logits - target)).astype(jnp.bfloat16)
    g_ref[...] = lax.dot_general(
        grad, head_ref[...], NT, preferred_element_type=jnp.float32
    ).astype(jnp.bfloat16)


def on_device(features, section_layers, kernels, gains, w_in, w_out, scales, head_weight, labels):
    sections = lax.axis_size("pipe")
    section_index = lax.axis_index("pipe")
    bands = lax.axis_size("rows")
    micros, band_rows, cols, width = features.shape
    slots = kernels.shape[0]
    hidden_width = w_in.shape[2]
    layer_count = section_layers[0]
    rows = band_rows * cols
    half = cols // 2
    ticks = sections + micros - 1
    f32, b16 = jnp.float32, jnp.bfloat16
    params = (kernels, gains[:, None, :], w_in, w_out, scales[:, None, :])
    dims = (micros, cols)
    edge_shape = (3 * cols, width)

    up = [(i, i + 1) for i in range(bands - 1)]
    down = [(i + 1, i) for i in range(bands - 1)]

    def halo(etop, ebot):
        return lax.ppermute(ebot, "rows", up), lax.ppermute(etop, "rows", down)

    def hop(x, etop, ebot):
        def pairs(by):
            return [
                (p * bands + r, (p + 1) * bands + r + by)
                for p in range(sections - 1)
                for r in range(bands)
                if 0 <= r + by < bands
            ]

        axes = ("pipe", "rows")
        return (
            lax.ppermute(x, axes, pairs(0)),
            lax.ppermute(ebot, axes, pairs(1)),
            lax.ppermute(etop, axes, pairs(-1)),
        )

    def edge_rows(part):
        part = part.reshape(micros, 3, 2, half, width).transpose(0, 1, 3, 2, 4)
        return part.reshape(micros * 3 * cols, width)

    first_x = features.reshape(micros, band_rows, 2, half, width).transpose(0, 3, 2, 1, 4)
    first_in = (
        first_x.reshape(micros * rows, width),
        *halo(edge_rows(features[:, :3]), edge_rows(features[:, band_rows - 3 :])),
    )

    tall, tall_edge = (micros * rows, width), (micros * 3 * cols, width)
    kept_shapes = [
        (tall, b16), (tall_edge, b16), (tall_edge, b16), (tall, f32), (tall, b16),
        ((micros * rows, hidden_width), b16), ((micros * rows, hidden_width), b16),
    ]
    sent_shapes = [((rows, width), b16), (edge_shape, b16), (edge_shape, b16)]
    back_shapes = [(tall, b16), ((micros * rows, hidden_width), b16), (tall, f32)]

    def turn(steps_before, tick):
        micro_no = tick - steps_before
        busy = (micro_no >= 0) & (micro_no < micros)
        at = jnp.stack([jnp.clip(micro_no, 0, micros - 1), (section_index == 0).astype(jnp.int32)])
        return jnp.where(busy, layer_count, 0), at.astype(jnp.int32)

    def forward_section(tick, received, kept0, kept1, sent):
        which, at = turn(section_index, tick)

        def leave(received, kept0, kept1, sent):
            return kept0, kept1, sent

        def one(received, kept0, kept1, sent):
            _, sent, kept0 = layer_front(at, *received, first_in, kept0, params, 0, *dims)
            return kept0, kept1, sent

        def both(received, kept0, kept1, sent):
            y, edges, kept0 = layer_front(at, *received, first_in, kept0, params, 0, *dims)
            _, sent, kept1 = layer_front(at, y, *halo(*edges[1:]), (), kept1, params, 1, *dims)
            return kept0, kept1, sent

        return lax.switch(which, (leave, one, both), received, kept0, kept1, sent)

    def loss_cotangent(out, micro_no):
        return pl.pallas_call(
            functools.partial(loss_body, loss_scale * 2.0 / (micros * rows * bands)),
            out_shape=jax.ShapeDtypeStruct((rows, width), b16),
        )(out, head_weight, pixel_labels[micro_no])

    def forward_tick(tick, state):
        received, kept0, kept1, sent = state
        kept0, kept1, sent = forward_section(tick, received, kept0, kept1, sent)
        return hop(*sent), kept0, kept1, sent

    pixel_labels = labels.reshape(micros, band_rows, 2, half).transpose(0, 3, 2, 1)
    pixel_labels = pixel_labels.reshape(micros, rows, 1)
    buffers = tuple(unwritten(kept_shapes + kept_shapes + sent_shapes + sent_shapes))
    state = (buffers[17:], buffers[:7], buffers[7:14], buffers[14:17])
    state = lax.fori_loop(0, sections - 1, forward_tick, state)
    from_loss = []
    for micro_no in range(micros):
        received, kept0, kept1, sent = state
        kept0, kept1, sent = forward_section(sections - 1 + micro_no, received, kept0, kept1, sent)
        from_loss.append(loss_cotangent(sent[0], micro_no))
        if micro_no + 1 < micros:
            received = hop(*sent)
        state = (received, kept0, kept1, sent)
    from_loss = jnp.stack(from_loss)

    def back_layer(at, g, slot, kept, back, stores, dtype):
        back, edges = layer_point(at, g, kept, back, params, slot, *dims)
        return layer_spread(at, g, back[2], *halo(*edges), stores, params, slot, *dims, dtype), back

    back_pairs = [(p + 1, p) for p in range(sections - 1)]
    is_last = section_index == sections - 1

    def backward_tick(tick, state):
        received, back0, back1, boundary, sent = state
        which, at = turn(sections - 1 - section_index, tick)

        def leave(received, back0, back1, boundary, sent):
            return back0, back1, boundary, sent

        def begin(received):
            return jnp.where(is_last, from_loss[at[0]], received)

        def one(received, back0, back1, boundary, sent):
            g = begin(received)
            (boundary, sent), back0 = back_layer(at, g, 0, kept0, back0, (boundary,), b16)
            return back0, back1, boundary, sent

        def both(received, back0, back1, boundary, sent):
            g = begin(received)
            (g,), back1 = back_layer(at, g, 1, kept1, back1, (), f32)
            (boundary, sent), back0 = back_layer(at, g, 0, kept0, back0, (boundary,), b16)
            return back0, back1, boundary, sent

        back0, back1, boundary, sent = lax.switch(
            which, (leave, one, both), received, back0, back1, boundary, sent
        )
        return lax.ppermute(sent, "pipe", back_pairs), back0, back1, boundary, sent

    buffers = tuple(unwritten(back_shapes + back_shapes + [(tall, b16)] + sent_shapes[:1] * 2))
    state = (buffers[8], buffers[:3], buffers[3:6], buffers[6], buffers[7])
    state = lax.fori_loop(0, ticks - 1, backward_tick, state)
    received, back0, back1, boundary, _ = state

    _, at = turn(sections - 1 - section_index, ticks - 1)
    owner = section_index == 0

    def last_leave(received, back0, back1, edges):
        return received.astype(f32), back0, back1, edges

    def last_one(received, back0, back1, edges):
        back0, edges = layer_point(at, received, kept0, back0, params, 0, *dims)
        return received.astype(f32), back0, back1, halo(*edges)

    def last_both(received, back0, back1, edges):
        (g,), back1 = back_layer(at, received, 1, kept1, back1, (), f32)
        back0, edges = layer_point(at, g, kept0, back0, params, 0, *dims)
        return g, back0, back1, halo(*edges)

    g, back0, back1, edges = lax.switch(
        jnp.where(owner, layer_count, 0), (last_leave, last_one, last_both),
        received, back0, back1, (sent[1], sent[2]),
    )
    stacked = layer_weights(section_layers, kept1, back1, (), slots, 1, *dims)
    stacked = layer_weights(section_layers, kept0, back0, stacked, slots, 0, *dims)
    w_in_grad, tall_grad = lax.psum(tuple(stacked), "rows")
    boundary = lax.cond(
        owner,
        lambda g, edges, gc, boundary: layer_spread(at, g, gc, *edges, (boundary,), params, 0, *dims, b16)[0],
        lambda g, edges, gc, boundary: boundary,
        g, edges, back0[2], boundary,
    )
    w_out_grad = tall_grad[:, :hidden_width]
    kernel_grad = tall_grad[:, hidden_width : hidden_width + kernels.shape[1]].astype(f32)
    boundary = boundary.reshape(micros, half, 2, band_rows, width).transpose(0, 3, 2, 1, 4)
    boundary = boundary.reshape(micros, band_rows, cols, width)
    return (boundary[None], kernel_grad, w_in_grad, w_out_grad)


def solution(mesh):
    return jax.shard_map(
        on_device,
        mesh=mesh,
        in_specs=(
            P(None, "rows", None, None),
            P("pipe"),
            P("pipe", None, None),
            P("pipe", None),
            P("pipe", None, None),
            P("pipe", None, None),
            P("pipe", None),
            P(),
            P(None, "rows", None),
        ),
        out_specs=(
            P("pipe", None, "rows", None, None),
            P("pipe", None, None),
            P("pipe", None, None),
            P("pipe", None, None),
        ),
        check_vma=False,
    )
```

```python
import functools
import math

import jax
import jax.numpy as jnp
from jax import lax
from jax.experimental import pallas as pl
from jax.experimental.pallas import tpu as pltpu
from jax.sharding import PartitionSpec as P

root_tau = 1.0 / math.sqrt(2.0 * math.pi)
norm_eps = 1e-06
loss_scale = 1024.0
erf_p = 0.3275911
erf_poly = (1.061405429, -1.453152027, 1.421413741, -0.284496736, 0.254829592)
LANES = 128
SUB = 8
NT = (((1,), (1,)), ((), ()))
TN = (((0,), (0,)), ((), ()))
VMEM_LIMIT = 20 * 1024 * 1024
VMEM_WEIGHTS = 32 * 1024 * 1024
CHUNK = 256
GELU = jnp.bfloat16
TAP_ROWS = 64


def whole_spec(shape):
    return pl.BlockSpec(shape, lambda *_: (0,) * len(shape))


def slot_spec(shape, slot):
    return pl.BlockSpec((None,) + tuple(shape[1:]), lambda *_: (slot,) + (0,) * (len(shape) - 1))


def micro_spec(shape, micros):
    return pl.BlockSpec((shape[0] // micros,) + tuple(shape[1:]), lambda _, at: (at[0], 0))


def one_micro(body, micros, at, operands, parts, stores, outs, scratch, flops):
    arrays, specs = [], []
    for item in operands:
        if isinstance(item, tuple):
            arrays.append(item[0])
            specs.append(slot_spec(item[0].shape, item[1]))
        else:
            arrays.append(item)
            specs.append(whole_spec(item.shape))
    arrays += list(parts)
    specs += [micro_spec(p.shape, micros) for p in parts]
    first = 1 + len(arrays)
    skip = len(stores)
    count = len(arrays)

    def run(at_ref, *refs):
        body(at_ref, *refs[:count], *refs[count + skip :])

    size = sum(math.prod(o[0]) * jnp.dtype(o[1]).itemsize for o in outs)
    size += sum(a.size * a.dtype.itemsize for a in arrays)
    return pl.pallas_call(
        run,
        grid_spec=pltpu.PrefetchScalarGridSpec(
            num_scalar_prefetch=1,
            grid=(1,),
            in_specs=specs + [pl.BlockSpec(memory_space=pl.ANY) for _ in stores],
            out_specs=[micro_spec(t.shape, micros) for t in stores] + [whole_spec(o[0]) for o in outs],
            scratch_shapes=scratch,
        ),
        out_shape=[jax.ShapeDtypeStruct(t.shape, t.dtype) for t in stores]
        + [jax.ShapeDtypeStruct(*o) for o in outs],
        input_output_aliases={first + i: i for i in range(len(stores))},
        compiler_params=pltpu.CompilerParams(vmem_limit_bytes=VMEM_LIMIT),
        cost_estimate=pl.CostEstimate(flops=flops, bytes_accessed=size, transcendentals=0),
    )(at, *arrays, *stores)


def unwritten(shapes):
    return pl.pallas_call(
        lambda *refs: None,
        out_specs=[pl.BlockSpec(memory_space=pl.ANY) for _ in shapes],
        out_shape=[jax.ShapeDtypeStruct(*s) for s in shapes],
    )()


def gelu_pair(h):
    e = jnp.exp(h * h * -0.5)
    t = 1.0 / (1.0 + (erf_p * math.sqrt(0.5)) * jnp.abs(h))
    q = t * (0.5 * erf_poly[0]) + 0.5 * erf_poly[1]
    for coef in erf_poly[2:]:
        q = q * t + 0.5 * coef
    q = q * t * e
    phi = jnp.where(h >= 0.0, 1.0 - q, q)
    return h * phi, phi + h * (e * root_tau)


def spread_taps(taps_ref, wide_taps):
    count, width = taps_ref.shape
    for tap in range(count):
        row = jnp.broadcast_to(taps_ref[tap : tap + 1, :], (2 * SUB, width))
        wide_taps[tap] = row.astype(jnp.bfloat16)


def build_shifts(own_ref, top_ref, bot_ref, cols, halo, shifts):
    planes = halo.shape[0]
    half = cols // 2
    for q in range(3):
        at = pl.ds(q * cols, cols)
        for lane in range(planes):
            lanes = slice(lane * LANES, (lane + 1) * LANES)
            plane = halo.at[lane]
            plane[pl.ds(5 + q, cols, stride=SUB), :] = top_ref[at, lanes].astype(jnp.float32)
            plane[pl.ds(q, cols, stride=SUB), :] = bot_ref[at, lanes].astype(jnp.float32)
    sub = lax.broadcasted_iota(jnp.int32, (SUB, LANES), 0)

    def pair(k, carry):
        for lane in range(planes):
            lanes = slice(lane * LANES, (lane + 1) * LANES)
            at = pl.ds(pl.multiple_of(k * 2 * SUB, 2 * SUB), 2 * SUB)
            own = own_ref[at, lanes].astype(jnp.float32)
            edge = halo[lane, at, :]
            for a in range(7):
                if a == 3:
                    both = own
                else:
                    mask = sub >= 5 + a if a < 3 else sub < a - 3
                    both = jnp.concatenate(
                        [
                            pltpu.roll(
                                jnp.where(mask, edge[h * SUB : (h + 1) * SUB], own[h * SUB : (h + 1) * SUB]),
                                (3 - a) % SUB,
                                0,
                            )
                            for h in range(2)
                        ],
                        axis=0,
                    )
                shifts[a, k + 3, :, lanes] = both.astype(jnp.bfloat16)
        return carry

    lax.fori_loop(0, half, pair, 0, unroll=2)
    blank = jnp.zeros((SUB, planes * LANES), jnp.float32)
    for a in range(7):
        for k in range(3):
            right = shifts[a, k + 3].astype(jnp.float32)[SUB:]
            shifts[a, half + 3 + k] = jnp.concatenate([right, blank], axis=0).astype(jnp.bfloat16)
            left = shifts[a, half + k].astype(jnp.float32)[:SUB]
            shifts[a, k] = jnp.concatenate([blank, left], axis=0).astype(jnp.bfloat16)


def convolve(shifts, wide_taps, flip, cols, width, store):
    for lane in range(width // LANES):
        lanes = slice(lane * LANES, (lane + 1) * LANES)

        def block(kb, carry, lanes=lanes):
            acc = jnp.zeros((8, 2 * SUB, LANES), jnp.float32)
            for a in range(7):
                strip = shifts[a, pl.ds(kb * 8, 14), :, lanes]
                line = None
                for b in range(7):
                    tap = 48 - (a * 7 + b) if flip else a * 7 + b
                    term = strip[b : b + 8] * wide_taps[tap, :, lanes][None]
                    line = term if line is None else line + term
                acc = acc + line.astype(jnp.float32)
            store(pl.ds(pl.multiple_of(kb * 128, 128), 128), lanes, acc.reshape(16 * SUB, LANES))
            return carry

        lax.fori_loop(0, cols // 16, block, 0)


def write_edges(source_ref, etop_ref, ebot_ref, halo, cols):
    for lane in range(halo.shape[0]):
        lanes = slice(lane * LANES, (lane + 1) * LANES)
        plane = halo.at[lane]
        plane[...] = source_ref[:, lanes]
        for q in range(3):
            to = pl.ds(q * cols, cols)
            etop_ref[to, lanes] = plane[pl.ds(q, cols, stride=SUB), :].astype(jnp.bfloat16)
            ebot_ref[to, lanes] = plane[pl.ds(q + 5, cols, stride=SUB), :].astype(jnp.bfloat16)


def row_loop(rows, step, fn):
    def body(i, carry):
        fn(pl.ds(pl.multiple_of(i * step, step), step))
        return carry

    lax.fori_loop(0, rows // step, body, 0)


def conv_scratch(cols, width):
    return [
        pltpu.VMEM((width // LANES, cols * SUB, LANES), jnp.float32),
        pltpu.VMEM((7, cols // 2 + 6, 2 * SUB, width), jnp.bfloat16),
        pltpu.VMEM((49, 2 * SUB, width), jnp.bfloat16),
    ]


def front_body(
    cols, slot,
    at_ref, *refs,
):
    if slot == 0:
        in_x_ref, in_top_ref, in_bot_ref, *refs = refs
    else:
        x_ref, in_top_ref, in_bot_ref, *refs = refs
    taps_ref, gain_ref, w_in_ref, w_out_ref, scale_ref, *refs = refs
    if slot == 0:
        first_x_ref, first_top_ref, first_bot_ref, *refs = refs
    kept_x_ref, top_ref, bot_ref, conv_ref, normed_ref, active_ref, slope_ref, *refs = refs
    outs_ref, y_ref, out_ref, etop_ref, ebot_ref, halo, shifts, wide_taps, hidden = refs
    rows, width = kept_x_ref.shape
    hidden_width = w_in_ref.shape[1]
    if slot == 0:
        x_ref = kept_x_ref

        @pl.when(at_ref[1] == 1)
        def from_features():
            kept_x_ref[...] = first_x_ref[...]
            top_ref[...] = first_top_ref[...]
            bot_ref[...] = first_bot_ref[...]

        @pl.when(at_ref[1] == 0)
        def from_section():
            kept_x_ref[...] = in_x_ref[...]
            top_ref[...] = in_top_ref[...]
            bot_ref[...] = in_bot_ref[...]

    else:
        kept_x_ref[...] = x_ref[...].astype(jnp.bfloat16)
        top_ref[...] = in_top_ref[...]
        bot_ref[...] = in_bot_ref[...]
    spread_taps(taps_ref, wide_taps)
    build_shifts(kept_x_ref, top_ref, bot_ref, cols, halo, shifts)

    def store(at, lanes, value):
        conv_ref[at, lanes] = value

    convolve(shifts, wide_taps, False, cols, width, store)

    def norm(at):
        conv = conv_ref[at, :]
        centred = conv - jnp.mean(conv, axis=-1, keepdims=True)
        spread = jnp.mean(centred * centred, axis=-1, keepdims=True)
        normed_ref[at, :] = (centred * lax.rsqrt(spread + norm_eps) * gain_ref[...]).astype(
            jnp.bfloat16
        )

    row_loop(rows, 64, norm)
    normed = normed_ref[...]
    chunks = hidden_width // CHUNK

    def expand(n):
        hidden[n % 2] = jnp.dot(
            normed, w_in_ref[:, n * CHUNK : (n + 1) * CHUNK], preferred_element_type=jnp.float32
        )

    expand(0)
    for n in range(chunks):
        if n + 1 < chunks:
            expand(n + 1)
        lanes = slice(n * CHUNK, (n + 1) * CHUNK)
        for i in range(rows // 32):
            at = slice(i * 32, (i + 1) * 32)
            value, slope = gelu_pair(hidden[n % 2, at, :].astype(GELU))
            active_ref[at, lanes] = value.astype(jnp.bfloat16)
            slope_ref[at, lanes] = slope.astype(jnp.bfloat16)
    y_ref[...] = x_ref[...].astype(jnp.float32) + scale_ref[...] * jnp.dot(
        active_ref[...], w_out_ref[...], preferred_element_type=jnp.float32
    )
    out_ref[...] = y_ref[...].astype(jnp.bfloat16)
    outs_ref[...] = out_ref[...]
    write_edges(y_ref, etop_ref, ebot_ref, halo, cols)


def layer_front(at, x, top, bot, first_in, kept, outs, params, slot, micros, cols):
    taps, gains, w_in, w_out, scales = params
    rows, width = x.shape
    hidden_width = w_in.shape[2]
    f32, b16 = jnp.float32, jnp.bfloat16
    found = one_micro(
        functools.partial(front_body, cols, slot),
        micros,
        at,
        (x, top, bot, (taps, slot), (gains, slot), (w_in, slot), (w_out, slot), (scales, slot)),
        first_in if slot == 0 else (),
        (*kept, outs),
        [((rows, width), f32), ((rows, width), b16), (top.shape, b16), (bot.shape, b16)],
        conv_scratch(cols, width) + [pltpu.VMEM((2, rows, CHUNK), f32)],
        4 * rows * width * hidden_width,
    )
    outs, y, out, etop, ebot = found[7:]
    return y, (out, etop, ebot), tuple(found[:7]), outs


def point_body(
    cols, choose,
    at_ref, g_ref, gain_ref, w_in_ref, w_out_ref, scale_ref, conv_ref, slope_ref, *refs,
):
    if choose:
        loss_ref, *refs = refs
    gs_ref, gh_ref, gc_ref, etop_ref, ebot_ref, wide, halo = refs
    rows, width = g_ref.shape
    hidden_width = w_in_ref.shape[1]

    def scaled(source_ref):
        gs_ref[...] = (scale_ref[...] * source_ref[...].astype(jnp.float32)).astype(jnp.bfloat16)

    if choose:
        pl.when(at_ref[2] == 1)(lambda: scaled(loss_ref))
        pl.when(at_ref[2] == 0)(lambda: scaled(g_ref))
    else:
        scaled(g_ref)
    grad = gs_ref[...]
    chunks = hidden_width // CHUNK

    def expand(n):
        wide[n % 2] = lax.dot_general(
            grad, w_out_ref[n * CHUNK : (n + 1) * CHUNK, :], NT, preferred_element_type=jnp.float32
        )

    expand(0)
    for n in range(chunks):
        if n + 1 < chunks:
            expand(n + 1)
        lanes = slice(n * CHUNK, (n + 1) * CHUNK)
        for i in range(rows // 32):
            at = slice(i * 32, (i + 1) * 32)
            gh_ref[at, lanes] = (wide[n % 2, at, :] * slope_ref[at, lanes].astype(jnp.float32)).astype(
                jnp.bfloat16
            )
    gc_ref[...] = lax.dot_general(gh_ref[...], w_in_ref[...], NT, preferred_element_type=jnp.float32)

    def norm_back(at):
        conv = conv_ref[at, :]
        centred = conv - jnp.mean(conv, axis=-1, keepdims=True)
        spread = jnp.mean(centred * centred, axis=-1, keepdims=True)
        scale = lax.rsqrt(spread + norm_eps)
        unit = centred * scale
        grad = gc_ref[at, :] * gain_ref[...]
        first = jnp.mean(grad, axis=-1, keepdims=True)
        second = jnp.mean(grad * unit, axis=-1, keepdims=True)
        gc_ref[at, :] = scale * (grad - first - unit * second)

    row_loop(rows, 64, norm_back)
    write_edges(gc_ref, etop_ref, ebot_ref, halo, cols)


def layer_point(at, g, loss, kept, back, params, slot, micros, cols):
    taps, gains, w_in, w_out, scales = params
    rows, width = g.shape
    hidden_width = w_in.shape[2]
    edge = ((3 * cols, width), jnp.bfloat16)
    found = one_micro(
        functools.partial(point_body, cols, bool(loss)),
        micros,
        at,
        (g, (gains, slot), (w_in, slot), (w_out, slot), (scales, slot)),
        (kept[3], kept[6], *loss),
        back,
        [edge, edge],
        [
            pltpu.VMEM((2, rows, CHUNK), jnp.float32),
            pltpu.VMEM((width // LANES, cols * SUB, LANES), jnp.float32),
        ],
        4 * rows * width * hidden_width,
    )
    return tuple(found[:3]), found[3:]


def spread_body(cols, choose, at_ref, g_ref, top_ref, bot_ref, taps_ref, gc_ref, *refs):
    *out_refs, halo, shifts, wide_taps = refs
    if choose:
        loss_ref, *out_refs = out_refs
    spread_taps(taps_ref, wide_taps)
    build_shifts(gc_ref, top_ref, bot_ref, cols, halo, shifts)

    def store(at, lanes, value):
        own = g_ref[at, lanes].astype(jnp.float32)
        if choose:
            own = jnp.where(at_ref[2] == 1, loss_ref[at, lanes].astype(jnp.float32), own)
        value = own + value
        for out_ref in out_refs:
            out_ref[at, lanes] = value.astype(out_ref.dtype)

    convolve(shifts, wide_taps, True, cols, g_ref.shape[1], store)


def layer_spread(at, g, loss, gc, top, bot, stores, params, slot, micros, cols, dtype):
    rows, width = g.shape
    return one_micro(
        functools.partial(spread_body, cols, bool(loss)),
        micros,
        at,
        (g, top, bot, (params[0], slot)),
        (gc, *loss),
        stores,
        [((rows, width), dtype)],
        conv_scratch(cols, width),
        98 * rows * width,
    )


def weight_body(
    micros, cols, slot,
    count_ref, x_ref, top_ref, bot_ref, gc_ref, normed_ref, gh_ref, active_ref, gs_ref,
    *refs,
):
    first_ref, second_ref, halo, shifts, sums = refs[-5:]
    hidden_width = gh_ref.shape[1]
    width = x_ref.shape[1]
    applied = slot < count_ref[0]

    @pl.when(jnp.logical_not(applied))
    def passed():
        first_ref[...] = jnp.zeros_like(first_ref)
        second_ref[...] = jnp.zeros_like(second_ref)

    @pl.when(applied)
    def run():
        first_ref[...] = lax.dot_general(
            normed_ref[...], gh_ref[...], TN, preferred_element_type=jnp.float32
        ).astype(jnp.bfloat16)
        second_ref[:hidden_width, :] = lax.dot_general(
            active_ref[...], gs_ref[...], TN, preferred_element_type=jnp.float32
        ).astype(jnp.bfloat16)
        pixels = cols * SUB
        for m in range(micros):
            at_edge = pl.ds(m * 3 * cols, 3 * cols)
            build_shifts(
                x_ref.at[pl.ds(m * pixels, pixels)], top_ref.at[at_edge], bot_ref.at[at_edge],
                cols, halo, shifts,
            )
            for lane in range(width // LANES):
                lanes = slice(lane * LANES, (lane + 1) * LANES)

                def tap_row(a, carry, lanes=lanes, m=m):
                    found = [jnp.zeros((2 * SUB, LANES), jnp.float32) for _ in range(7)]
                    for kb in range(cols // 16):
                        strip = shifts[a, kb * 8 : kb * 8 + 14, :, lanes]
                        at = pl.ds(m * pixels + kb * 128, 128)
                        grad = gc_ref[at, lanes].astype(jnp.bfloat16).reshape(8, 2 * SUB, LANES)
                        for b in range(7):
                            term = strip[b : b + 8] * grad
                            term = (term[0] + term[1]) + (term[2] + term[3]), (term[4] + term[5]) + (term[6] + term[7])
                            found[b] = found[b] + (term[0].astype(jnp.float32) + term[1].astype(jnp.float32))
                    for b in range(7):
                        total = found[b][:SUB] + found[b][SUB:]
                        if m == 0:
                            sums[a * 7 + b, :, lanes] = total
                        else:
                            sums[a * 7 + b, :, lanes] += total
                    return carry

                lax.fori_loop(0, 7, tap_row, 0)
        taps = jnp.sum(sums[...], axis=1)
        fill = jnp.zeros((TAP_ROWS - taps.shape[0], width), jnp.float32)
        second_ref[hidden_width:, :] = jnp.concatenate([taps, fill], axis=0).astype(jnp.bfloat16)


def layer_weights(count, kept, back, stacked, slots, slot, micros, cols):
    x, top, bot, _, normed, active, _ = kept
    gs, gh, gc = back
    rows, width = x.shape
    hidden_width = gh.shape[1]
    f32, b16 = jnp.float32, jnp.bfloat16
    arrays = (x, top, bot, gc, normed, gh, active, gs)
    shapes = [(slots, width, hidden_width), (slots, hidden_width + TAP_ROWS, width)]
    size = sum(math.prod(o[1:]) * 2 for o in shapes) + sum(a.size * a.dtype.itemsize for a in arrays)
    return pl.pallas_call(
        functools.partial(weight_body, micros, cols, slot),
        grid=(1,),
        in_specs=[pl.BlockSpec(memory_space=pltpu.SMEM)]
        + [whole_spec(a.shape) for a in arrays]
        + [pl.BlockSpec(memory_space=pl.ANY) for _ in stacked],
        out_specs=[slot_spec(o, slot) for o in shapes],
        out_shape=[jax.ShapeDtypeStruct(o, b16) for o in shapes],
        input_output_aliases={1 + len(arrays) + i: i for i in range(len(stacked))},
        scratch_shapes=conv_scratch(cols, width)[:2] + [pltpu.VMEM((49, SUB, width), f32)],
        compiler_params=pltpu.CompilerParams(vmem_limit_bytes=VMEM_WEIGHTS),
        cost_estimate=pl.CostEstimate(
            flops=4 * rows * width * hidden_width, bytes_accessed=size, transcendentals=0
        ),
    )(count, *arrays, *stacked)


def loss_body(factor, y_ref, head_ref, labels_ref, g_ref):
    logits = jnp.dot(y_ref[...], head_ref[...], preferred_element_type=jnp.float32)
    spots = lax.broadcasted_iota(jnp.int32, logits.shape, 1)
    target = (labels_ref[...] == spots).astype(jnp.float32)
    grad = (factor * (logits - target)).astype(jnp.bfloat16)
    g_ref[...] = lax.dot_general(
        grad, head_ref[...], NT, preferred_element_type=jnp.float32
    ).astype(jnp.bfloat16)


def on_device(features, section_layers, kernels, gains, w_in, w_out, scales, head_weight, labels):
    sections = lax.axis_size("pipe")
    section_index = lax.axis_index("pipe")
    bands = lax.axis_size("rows")
    micros, band_rows, cols, width = features.shape
    slots = kernels.shape[0]
    hidden_width = w_in.shape[2]
    layer_count = section_layers[0]
    rows = band_rows * cols
    half = cols // 2
    ticks = sections + micros - 1
    f32, b16 = jnp.float32, jnp.bfloat16
    params = (kernels, gains[:, None, :], w_in, w_out, scales[:, None, :])
    dims = (micros, cols)
    edge_shape = (3 * cols, width)

    up = [(i, i + 1) for i in range(bands - 1)]
    down = [(i + 1, i) for i in range(bands - 1)]

    def halo(etop, ebot):
        return lax.ppermute(ebot, "rows", up), lax.ppermute(etop, "rows", down)

    def hop(x, etop, ebot):
        def pairs(by):
            return [
                (p * bands + r, (p + 1) * bands + r + by)
                for p in range(sections - 1)
                for r in range(bands)
                if 0 <= r + by < bands
            ]

        axes = ("pipe", "rows")
        return (
            lax.ppermute(x, axes, pairs(0)),
            lax.ppermute(ebot, axes, pairs(1)),
            lax.ppermute(etop, axes, pairs(-1)),
        )

    def edge_rows(part):
        part = part.reshape(micros, 3, 2, half, width).transpose(0, 1, 3, 2, 4)
        return part.reshape(micros * 3 * cols, width)

    first_x = features.reshape(micros, band_rows, 2, half, width).transpose(0, 3, 2, 1, 4)
    first_in = (
        first_x.reshape(micros * rows, width),
        *halo(edge_rows(features[:, :3]), edge_rows(features[:, band_rows - 3 :])),
    )

    tall, tall_edge = (micros * rows, width), (micros * 3 * cols, width)
    kept_shapes = [
        (tall, b16), (tall_edge, b16), (tall_edge, b16), (tall, f32), (tall, b16),
        ((micros * rows, hidden_width), b16), ((micros * rows, hidden_width), b16),
    ]
    sent_shapes = [((rows, width), b16), (edge_shape, b16), (edge_shape, b16)]
    back_shapes = [(tall, b16), ((micros * rows, hidden_width), b16), (tall, f32)]

    def turn(steps_before, tick):
        micro_no = tick - steps_before
        busy = (micro_no >= 0) & (micro_no < micros)
        ends = [section_index == 0, section_index == sections - 1]
        at = jnp.stack([jnp.clip(micro_no, 0, micros - 1)] + [e.astype(jnp.int32) for e in ends])
        return jnp.where(busy, layer_count, 0), at.astype(jnp.int32)

    def forward_tick(tick, state):
        received, kept0, kept1, outs, sent = state
        which, at = turn(section_index, tick)

        def leave(received, kept0, kept1, outs, sent):
            return kept0, kept1, outs, sent

        def one(received, kept0, kept1, outs, sent):
            _, sent, kept0, outs = layer_front(at, *received, first_in, kept0, outs, params, 0, *dims)
            return kept0, kept1, outs, sent

        def both(received, kept0, kept1, outs, sent):
            y, edges, kept0, outs = layer_front(at, *received, first_in, kept0, outs, params, 0, *dims)
            received = (y, *halo(*edges[1:]))
            _, sent, kept1, outs = layer_front(at, *received, (), kept1, outs, params, 1, *dims)
            return kept0, kept1, outs, sent

        kept0, kept1, outs, sent = lax.switch(
            which, (leave, one, both), received, kept0, kept1, outs, sent
        )
        received = lax.cond(tick < ticks - 1, lambda s: hop(*s), lambda s: tuple(s), sent)
        return received, kept0, kept1, outs, sent

    buffers = tuple(unwritten(kept_shapes + kept_shapes + sent_shapes + sent_shapes + kept_shapes[:1]))
    state = (buffers[17:20], buffers[:7], buffers[7:14], buffers[20], buffers[14:17])
    _, kept0, kept1, outs, sent = lax.fori_loop(0, ticks, forward_tick, state)

    pixel_labels = labels.reshape(micros, band_rows, 2, half).transpose(0, 3, 2, 1)
    from_loss = pl.pallas_call(
        functools.partial(loss_body, loss_scale * 2.0 / (micros * rows * bands)),
        out_shape=jax.ShapeDtypeStruct(tall, b16),
    )(outs, head_weight, pixel_labels.reshape(micros * rows, 1))

    def back_layer(at, g, loss, slot, kept, back, stores, dtype):
        back, edges = layer_point(at, g, loss, kept, back, params, slot, *dims)
        found = layer_spread(at, g, loss, back[2], *halo(*edges), stores, params, slot, *dims, dtype)
        return found, back

    back_pairs = [(p + 1, p) for p in range(sections - 1)]

    def backward_tick(tick, state):
        received, back0, back1, boundary, sent = state
        which, at = turn(sections - 1 - section_index, tick)

        def leave(received, back0, back1, boundary, sent):
            return back0, back1, boundary, sent

        def one(received, back0, back1, boundary, sent):
            (boundary, sent), back0 = back_layer(
                at, received, (from_loss,), 0, kept0, back0, (boundary,), b16
            )
            return back0, back1, boundary, sent

        def both(received, back0, back1, boundary, sent):
            (g,), back1 = back_layer(at, received, (from_loss,), 1, kept1, back1, (), f32)
            (boundary, sent), back0 = back_layer(at, g, (), 0, kept0, back0, (boundary,), b16)
            return back0, back1, boundary, sent

        back0, back1, boundary, sent = lax.switch(
            which, (leave, one, both), received, back0, back1, boundary, sent
        )
        return lax.ppermute(sent, "pipe", back_pairs), back0, back1, boundary, sent

    buffers = tuple(unwritten(back_shapes + back_shapes + [(tall, b16)] + sent_shapes[:1] * 2))
    state = (buffers[8], buffers[:3], buffers[3:6], buffers[6], buffers[7])
    state = lax.fori_loop(0, ticks - 1, backward_tick, state)
    received, back0, back1, boundary, _ = state

    _, at = turn(sections - 1 - section_index, ticks - 1)
    owner = section_index == 0

    def last_leave(received, back0, back1, edges):
        return received.astype(f32), back0, back1, edges

    def last_one(received, back0, back1, edges):
        back0, edges = layer_point(at, received, (), kept0, back0, params, 0, *dims)
        return received.astype(f32), back0, back1, halo(*edges)

    def last_both(received, back0, back1, edges):
        (g,), back1 = back_layer(at, received, (), 1, kept1, back1, (), f32)
        back0, edges = layer_point(at, g, (), kept0, back0, params, 0, *dims)
        return g, back0, back1, halo(*edges)

    g, back0, back1, edges = lax.switch(
        jnp.where(owner, layer_count, 0), (last_leave, last_one, last_both),
        received, back0, back1, (sent[1], sent[2]),
    )
    stacked = layer_weights(section_layers, kept1, back1, (), slots, 1, *dims)
    stacked = layer_weights(section_layers, kept0, back0, stacked, slots, 0, *dims)
    w_in_grad, tall_grad = lax.psum(tuple(stacked), "rows")
    boundary = lax.cond(
        owner,
        lambda g, edges, gc, boundary: layer_spread(at, g, (), gc, *edges, (boundary,), params, 0, *dims, b16)[0],
        lambda g, edges, gc, boundary: boundary,
        g, edges, back0[2], boundary,
    )
    w_out_grad = tall_grad[:, :hidden_width]
    kernel_grad = tall_grad[:, hidden_width : hidden_width + kernels.shape[1]].astype(f32)
    boundary = boundary.reshape(micros, half, 2, band_rows, width).transpose(0, 3, 2, 1, 4)
    boundary = boundary.reshape(micros, band_rows, cols, width)
    return (boundary[None], kernel_grad, w_in_grad, w_out_grad)


def solution(mesh):
    return jax.shard_map(
        on_device,
        mesh=mesh,
        in_specs=(
            P(None, "rows", None, None),
            P("pipe"),
            P("pipe", None, None),
            P("pipe", None),
            P("pipe", None, None),
            P("pipe", None, None),
            P("pipe", None),
            P(),
            P(None, "rows", None),
        ),
        out_specs=(
            P("pipe", None, "rows", None, None),
            P("pipe", None, None),
            P("pipe", None, None),
            P("pipe", None, None),
        ),
        check_vma=False,
    )
```

```python
import functools
import math

import jax
import jax.numpy as jnp
from jax import lax
from jax.experimental import pallas as pl
from jax.experimental.pallas import tpu as pltpu
from jax.sharding import PartitionSpec as P

root_tau = 1.0 / math.sqrt(2.0 * math.pi)
norm_eps = 1e-06
loss_scale = 1024.0
erf_p = 0.3275911
erf_poly = (1.061405429, -1.453152027, 1.421413741, -0.284496736, 0.254829592)
LANES = 128
SUB = 8
NT = (((1,), (1,)), ((), ()))
TN = (((0,), (0,)), ((), ()))
VMEM_LIMIT = 20 * 1024 * 1024
VMEM_WEIGHTS = 32 * 1024 * 1024
CHUNK = 256
GELU = jnp.bfloat16
TAP_ROWS = 64


VMEM = pl.BlockSpec(memory_space=pltpu.VMEM)
SMEM = pl.BlockSpec(memory_space=pltpu.SMEM)
HBM = pl.BlockSpec(memory_space=pltpu.HBM)
ANY = pl.BlockSpec(memory_space=pl.ANY)


class Copies:
    def __init__(self, sems):
        self.sems, self.used, self.open = sems, 0, []

    def make(self, source, target):
        copy = pltpu.make_async_copy(source, target, self.sems.at[self.used])
        self.used += 1
        return copy

    def fetch(self, source, target):
        copy = self.make(source, target)
        copy.start()
        return copy

    def keep(self, source, target):
        self.open.append(self.fetch(source, target))

    def either(self, flag, source, other, target):
        copy, second = self.make(source, target), None
        second = pltpu.make_async_copy(other, target, self.sems.at[self.used - 1])
        pl.when(flag == 1)(copy.start)
        pl.when(flag == 0)(second.start)
        return copy

    def finish(self):
        for copy in self.open:
            copy.wait()


def own_rows(ref, at_ref, micros):
    size = ref.shape[0] // micros
    return ref.at[pl.ds(pl.multiple_of(at_ref[0] * size, 16), size)]


def kernel_call(body, at, inputs, stores, outs, scratch, flops, limit=None):
    arrays = [i[0] for i in inputs]
    count, skip = 1 + len(arrays), len(stores)

    def run(*refs):
        body(*refs[:count], *refs[count + skip :])

    size = sum(math.prod(o[0]) * jnp.dtype(o[1]).itemsize for o in outs)
    size += sum(a.size * a.dtype.itemsize for a in arrays)
    return pl.pallas_call(
        run,
        in_specs=[SMEM] + [i[1] for i in inputs] + [HBM] * skip,
        out_specs=[HBM] * skip + [o[2] if len(o) > 2 else VMEM for o in outs],
        out_shape=[jax.ShapeDtypeStruct(t.shape, t.dtype) for t in stores]
        + [jax.ShapeDtypeStruct(*o[:2]) for o in outs],
        scratch_shapes=scratch + [pltpu.SemaphoreType.DMA((24,))],
        input_output_aliases={count + i: i for i in range(skip)},
        compiler_params=pltpu.CompilerParams(vmem_limit_bytes=limit or VMEM_LIMIT),
        cost_estimate=pl.CostEstimate(flops=flops, bytes_accessed=size, transcendentals=0),
    )(at, *arrays, *stores)


def unwritten(shapes):
    return pl.pallas_call(
        lambda *refs: None,
        out_specs=[ANY] * len(shapes),
        out_shape=[jax.ShapeDtypeStruct(*s) for s in shapes],
    )()


def gelu_pair(h):
    e = jnp.exp(h * h * -0.5)
    t = 1.0 / (1.0 + (erf_p * math.sqrt(0.5)) * jnp.abs(h))
    q = t * (0.5 * erf_poly[0]) + 0.5 * erf_poly[1]
    for coef in erf_poly[2:]:
        q = q * t + 0.5 * coef
    q = q * t * e
    phi = jnp.where(h >= 0.0, 1.0 - q, q)
    return h * phi, phi + h * (e * root_tau)


def spread_taps(taps_ref, wide_taps):
    count, width = taps_ref.shape
    for tap in range(count):
        row = jnp.broadcast_to(taps_ref[tap : tap + 1, :], (2 * SUB, width))
        wide_taps[tap] = row.astype(jnp.bfloat16)


def build_shifts(own_ref, top_ref, bot_ref, cols, halo, shifts):
    planes = halo.shape[0]
    half = cols // 2
    for q in range(3):
        at = pl.ds(q * cols, cols)
        for lane in range(planes):
            lanes = slice(lane * LANES, (lane + 1) * LANES)
            plane = halo.at[lane]
            plane[pl.ds(5 + q, cols, stride=SUB), :] = top_ref[at, lanes].astype(jnp.float32)
            plane[pl.ds(q, cols, stride=SUB), :] = bot_ref[at, lanes].astype(jnp.float32)
    sub = lax.broadcasted_iota(jnp.int32, (SUB, LANES), 0)

    def pair(k, carry):
        for lane in range(planes):
            lanes = slice(lane * LANES, (lane + 1) * LANES)
            at = pl.ds(pl.multiple_of(k * 2 * SUB, 2 * SUB), 2 * SUB)
            own = own_ref[at, lanes].astype(jnp.float32)
            edge = halo[lane, at, :]
            for a in range(7):
                if a == 3:
                    both = own
                else:
                    mask = sub >= 5 + a if a < 3 else sub < a - 3
                    both = jnp.concatenate(
                        [
                            pltpu.roll(
                                jnp.where(mask, edge[h * SUB : (h + 1) * SUB], own[h * SUB : (h + 1) * SUB]),
                                (3 - a) % SUB,
                                0,
                            )
                            for h in range(2)
                        ],
                        axis=0,
                    )
                shifts[a, k + 3, :, lanes] = both.astype(jnp.bfloat16)
        return carry

    lax.fori_loop(0, half, pair, 0, unroll=2)
    blank = jnp.zeros((SUB, planes * LANES), jnp.float32)
    for a in range(7):
        for k in range(3):
            right = shifts[a, k + 3].astype(jnp.float32)[SUB:]
            shifts[a, half + 3 + k] = jnp.concatenate([right, blank], axis=0).astype(jnp.bfloat16)
            left = shifts[a, half + k].astype(jnp.float32)[:SUB]
            shifts[a, k] = jnp.concatenate([blank, left], axis=0).astype(jnp.bfloat16)


def convolve(shifts, wide_taps, flip, cols, width, store):
    for lane in range(width // LANES):
        lanes = slice(lane * LANES, (lane + 1) * LANES)

        def block(kb, carry, lanes=lanes):
            acc = jnp.zeros((8, 2 * SUB, LANES), jnp.float32)
            for a in range(7):
                strip = shifts[a, pl.ds(kb * 8, 14), :, lanes]
                line = None
                for b in range(7):
                    tap = 48 - (a * 7 + b) if flip else a * 7 + b
                    term = strip[b : b + 8] * wide_taps[tap, :, lanes][None]
                    line = term if line is None else line + term
                acc = acc + line.astype(jnp.float32)
            store(pl.ds(pl.multiple_of(kb * 128, 128), 128), lanes, acc.reshape(16 * SUB, LANES))
            return carry

        lax.fori_loop(0, cols // 16, block, 0)


def write_edges(source_ref, etop_ref, ebot_ref, halo, cols):
    for lane in range(halo.shape[0]):
        lanes = slice(lane * LANES, (lane + 1) * LANES)
        plane = halo.at[lane]
        plane[...] = source_ref[:, lanes]
        for q in range(3):
            to = pl.ds(q * cols, cols)
            etop_ref[to, lanes] = plane[pl.ds(q, cols, stride=SUB), :].astype(jnp.bfloat16)
            ebot_ref[to, lanes] = plane[pl.ds(q + 5, cols, stride=SUB), :].astype(jnp.bfloat16)


def row_loop(rows, step, fn):
    def body(i, carry):
        fn(pl.ds(pl.multiple_of(i * step, step), step))
        return carry

    lax.fori_loop(0, rows // step, body, 0)


def conv_scratch(cols, width):
    return [
        pltpu.VMEM((width // LANES, cols * SUB, LANES), jnp.float32),
        pltpu.VMEM((7, cols // 2 + 6, 2 * SUB, width), jnp.bfloat16),
        pltpu.VMEM((49, 2 * SUB, width), jnp.bfloat16),
    ]


def front_body(
    micros, cols, slot,
    at_ref, x_ref, top_in, bot_in, taps_ref, gain_ref, scale_ref, w_in_hbm, w_out_hbm, *refs,
):
    copies = Copies(refs[-1])
    refs = refs[:-1]
    if slot == 0:
        first, refs = [own_rows(r, at_ref, micros) for r in refs[:3]], refs[3:]
    kept, refs = [own_rows(r, at_ref, micros) for r in refs[:8]], refs[8:]
    y_ref, out_ref, etop_ref, ebot_ref, *refs = refs
    kept_x_ref, top_ref, bot_ref, conv_ref, normed_ref, active_ref, slope_ref, *refs = refs
    w_in_ref, w_out_ref, halo, shifts, wide_taps, hidden = refs
    taps_ref, gain_ref, scale_ref = taps_ref.at[slot], gain_ref.at[slot], scale_ref.at[slot]
    rows, width = kept_x_ref.shape
    hidden_width = w_in_ref.shape[1]
    if slot == 0:
        arrive = [
            copies.either(at_ref[1], *three)
            for three in zip(first, (x_ref, top_in, bot_in), (kept_x_ref, top_ref, bot_ref))
        ]
    else:
        arrive = [copies.fetch(top_in, top_ref), copies.fetch(bot_in, bot_ref)]
    expansion = copies.fetch(w_in_hbm.at[slot], w_in_ref)
    projection = copies.fetch(w_out_hbm.at[slot], w_out_ref)
    spread_taps(taps_ref, wide_taps)
    if slot == 0:
        x_ref = kept_x_ref
    else:
        kept_x_ref[...] = x_ref[...].astype(jnp.bfloat16)
    for copy in arrive:
        copy.wait()
    for source, target in zip((kept_x_ref, top_ref, bot_ref), kept[:3]):
        copies.keep(source, target)
    build_shifts(kept_x_ref, top_ref, bot_ref, cols, halo, shifts)

    def store(at, lanes, value):
        conv_ref[at, lanes] = value

    convolve(shifts, wide_taps, False, cols, width, store)
    copies.keep(conv_ref, kept[3])

    def norm(at):
        conv = conv_ref[at, :]
        centred = conv - jnp.mean(conv, axis=-1, keepdims=True)
        spread = jnp.mean(centred * centred, axis=-1, keepdims=True)
        normed_ref[at, :] = (centred * lax.rsqrt(spread + norm_eps) * gain_ref[...]).astype(
            jnp.bfloat16
        )

    row_loop(rows, 64, norm)
    copies.keep(normed_ref, kept[4])
    normed = normed_ref[...]
    expansion.wait()
    chunks = hidden_width // CHUNK

    def expand(n):
        hidden[n % 2] = jnp.dot(
            normed, w_in_ref[:, n * CHUNK : (n + 1) * CHUNK], preferred_element_type=jnp.float32
        )

    expand(0)
    for n in range(chunks):
        if n + 1 < chunks:
            expand(n + 1)
        lanes = slice(n * CHUNK, (n + 1) * CHUNK)
        for i in range(rows // 32):
            at = slice(i * 32, (i + 1) * 32)
            value, slope = gelu_pair(hidden[n % 2, at, :].astype(GELU))
            active_ref[at, lanes] = value.astype(jnp.bfloat16)
            slope_ref[at, lanes] = slope.astype(jnp.bfloat16)
        if n % 2:
            two = slice((n - 1) * CHUNK, (n + 1) * CHUNK)
            copies.keep(active_ref.at[:, two], kept[5].at[:, two])
            copies.keep(slope_ref.at[:, two], kept[6].at[:, two])
    projection.wait()
    y_ref[...] = x_ref[...].astype(jnp.float32) + scale_ref[...] * jnp.dot(
        active_ref[...], w_out_ref[...], preferred_element_type=jnp.float32
    )
    out_ref[...] = y_ref[...].astype(jnp.bfloat16)
    copies.keep(out_ref, kept[7])
    write_edges(y_ref, etop_ref, ebot_ref, halo, cols)
    copies.finish()


def layer_front(at, x, top, bot, first_in, kept, outs, params, slot, micros, cols):
    taps, gains, w_in, w_out, scales = params
    rows, width = x.shape
    hidden_width = w_in.shape[2]
    f32, b16 = jnp.float32, jnp.bfloat16
    inputs = [(x, ANY if slot == 0 else VMEM), (top, ANY), (bot, ANY), (taps, VMEM), (gains, VMEM), (scales, VMEM)]
    inputs += [(w_in, HBM), (w_out, HBM)]
    if slot == 0:
        inputs += [(part, ANY) for part in first_in]
    wide = pltpu.VMEM((rows, hidden_width), b16)
    found = kernel_call(
        functools.partial(front_body, micros, cols, slot),
        at,
        inputs,
        (*kept, outs),
        [((rows, width), f32), ((rows, width), b16), (top.shape, b16), (bot.shape, b16)],
        [
            pltpu.VMEM((rows, width), b16), pltpu.VMEM(top.shape, b16), pltpu.VMEM(bot.shape, b16),
            pltpu.VMEM((rows, width), f32), pltpu.VMEM((rows, width), b16), wide, wide,
            pltpu.VMEM(w_in.shape[1:], b16), pltpu.VMEM(w_out.shape[1:], b16),
        ]
        + conv_scratch(cols, width)
        + [pltpu.VMEM((2, rows, CHUNK), f32)],
        4 * rows * width * hidden_width,
    )
    outs, y, out, etop, ebot = found[7:]
    return y, (out, etop, ebot), tuple(found[:7]), outs


def point_body(
    micros, choose, slot,
    at_ref, g_ref, gain_ref, scale_ref, w_in_hbm, w_out_hbm, conv_hbm, slope_hbm, *refs,
):
    copies = Copies(refs[-1])
    refs = refs[:-1]
    if choose:
        loss, refs = own_rows(refs[0], at_ref, micros), refs[1:]
    kept, refs = [own_rows(r, at_ref, micros) for r in refs[:3]], refs[3:]
    gc_ref, etop_ref, ebot_ref, g_own, gs_ref, gh_ref, conv_ref, slope_ref, *refs = refs
    w_in_ref, w_out_ref, wide, halo = refs
    gain_ref, scale_ref = gain_ref.at[slot], scale_ref.at[slot]
    rows, width = gs_ref.shape
    hidden_width = w_in_ref.shape[1]
    cols = rows // SUB
    if choose:
        arrive = copies.either(at_ref[2], loss, g_ref, g_own)
    parts = 3
    third = hidden_width // parts
    weights, slopes = [], []
    for i in range(parts):
        at = pl.ds(i * third, third)
        weights.append(copies.fetch(w_out_hbm.at[slot, at], w_out_ref.at[at]))
        slopes.append(copies.fetch(own_rows(slope_hbm, at_ref, micros).at[:, at], slope_ref.at[:, at]))
    back = copies.fetch(w_in_hbm.at[slot], w_in_ref)
    front = copies.fetch(own_rows(conv_hbm, at_ref, micros), conv_ref)
    if choose:
        arrive.wait()
        g_ref = g_own
    gs_ref[...] = (scale_ref[...] * g_ref[...].astype(jnp.float32)).astype(jnp.bfloat16)
    copies.keep(gs_ref, kept[0])
    grad = gs_ref[...]
    chunks = hidden_width // CHUNK

    def expand(n):
        if n * CHUNK % third == 0:
            weights[n * CHUNK // third].wait()
            slopes[n * CHUNK // third].wait()
        wide[n % 2] = lax.dot_general(
            grad, w_out_ref[n * CHUNK : (n + 1) * CHUNK, :], NT, preferred_element_type=jnp.float32
        )

    expand(0)
    for n in range(chunks):
        if n + 1 < chunks:
            expand(n + 1)
        lanes = slice(n * CHUNK, (n + 1) * CHUNK)
        for i in range(rows // 32):
            at = slice(i * 32, (i + 1) * 32)
            gh_ref[at, lanes] = (wide[n % 2, at, :] * slope_ref[at, lanes].astype(jnp.float32)).astype(
                jnp.bfloat16
            )
        if n % 2:
            two = slice((n - 1) * CHUNK, (n + 1) * CHUNK)
            copies.keep(gh_ref.at[:, two], kept[1].at[:, two])
    back.wait()
    gc_ref[...] = lax.dot_general(gh_ref[...], w_in_ref[...], NT, preferred_element_type=jnp.float32)

    def norm_back(at):
        conv = conv_ref[at, :]
        centred = conv - jnp.mean(conv, axis=-1, keepdims=True)
        spread = jnp.mean(centred * centred, axis=-1, keepdims=True)
        scale = lax.rsqrt(spread + norm_eps)
        unit = centred * scale
        grad = gc_ref[at, :] * gain_ref[...]
        first = jnp.mean(grad, axis=-1, keepdims=True)
        second = jnp.mean(grad * unit, axis=-1, keepdims=True)
        gc_ref[at, :] = scale * (grad - first - unit * second)

    front.wait()
    row_loop(rows, 64, norm_back)
    copies.keep(gc_ref, kept[2])
    write_edges(gc_ref, etop_ref, ebot_ref, halo, cols)
    copies.finish()


def layer_point(at, g, loss, kept, back, params, slot, micros, cols):
    taps, gains, w_in, w_out, scales = params
    rows, width = g.shape
    hidden_width = w_in.shape[2]
    f32, b16 = jnp.float32, jnp.bfloat16
    edge = ((3 * cols, width), b16)
    inputs = [(g, ANY if loss else VMEM), (gains, VMEM), (scales, VMEM), (w_in, HBM), (w_out, HBM)]
    inputs += [(kept[3], HBM), (kept[6], HBM)] + [(part, ANY) for part in loss]
    wide = pltpu.VMEM((rows, hidden_width), b16)
    found = kernel_call(
        functools.partial(point_body, micros, bool(loss), slot),
        at,
        inputs,
        back,
        [((rows, width), f32), edge, edge],
        [
            pltpu.VMEM((rows, width), b16), pltpu.VMEM((rows, width), b16), wide,
            pltpu.VMEM((rows, width), f32), wide,
            pltpu.VMEM(w_in.shape[1:], b16), pltpu.VMEM(w_out.shape[1:], b16),
            pltpu.VMEM((2, rows, CHUNK), f32),
            pltpu.VMEM((width // LANES, cols * SUB, LANES), f32),
        ],
        4 * rows * width * hidden_width,
    )
    return tuple(found[:3]), found[3], found[4:]


def spread_body(micros, choose, slot, at_ref, g_ref, top_ref, bot_ref, taps_ref, gc_ref, *refs):
    copies = Copies(refs[-1])
    *refs, g_own, halo, shifts, wide_taps = refs[:-1]
    if choose:
        arrive = copies.either(at_ref[2], own_rows(refs[0], at_ref, micros), g_ref, g_own)
        refs = refs[1:]
        g_ref = g_own
    *kept, out_ref = refs
    spread_taps(taps_ref.at[slot], wide_taps)
    cols, width = gc_ref.shape[0] // SUB, gc_ref.shape[1]
    build_shifts(gc_ref, top_ref, bot_ref, cols, halo, shifts)
    if choose:
        arrive.wait()

    def store(at, lanes, value):
        out_ref[at, lanes] = (g_ref[at, lanes].astype(jnp.float32) + value).astype(out_ref.dtype)

    convolve(shifts, wide_taps, True, cols, width, store)
    for target in kept:
        copies.keep(out_ref, own_rows(target, at_ref, micros))
    copies.finish()


def layer_spread(at, g, loss, gc, top, bot, stores, params, slot, micros, cols, dtype):
    rows, width = g.shape
    inputs = [(g, ANY if loss else VMEM), (top, VMEM), (bot, VMEM), (params[0], VMEM), (gc, VMEM)]
    return kernel_call(
        functools.partial(spread_body, micros, bool(loss), slot),
        at,
        inputs + [(part, ANY) for part in loss],
        stores,
        [((rows, width), dtype)],
        [pltpu.VMEM((rows, width), jnp.bfloat16)] + conv_scratch(cols, width),
        98 * rows * width,
    )


def weight_body(
    micros, cols, slot,
    count_ref, x_hbm, top_hbm, bot_hbm, gc_hbm, normed_hbm, gh_hbm, active_hbm, gs_hbm, *refs,
):
    copies = Copies(refs[-1])
    first_hbm, second_hbm, *refs = refs[:-1]
    first_ref, second_ref, halo, shifts, sums, *held = refs
    sources = (x_hbm, top_hbm, bot_hbm, gc_hbm, normed_hbm, gh_hbm, active_hbm, gs_hbm)
    x_ref, top_ref, bot_ref, gc_ref, normed_ref, gh_ref, active_ref, gs_ref = held
    hidden_width = gh_ref.shape[1]
    width = x_ref.shape[1]
    applied = slot < count_ref[0]

    @pl.when(jnp.logical_not(applied))
    def passed():
        first_ref[...] = jnp.zeros_like(first_ref)
        second_ref[...] = jnp.zeros_like(second_ref)

    @pl.when(applied)
    def run():
        arrive = [copies.fetch(source, target) for source, target in zip(sources, held)]
        for copy in arrive[:4]:
            copy.wait()
        pixels = cols * SUB
        for m in range(micros):
            at_edge = pl.ds(m * 3 * cols, 3 * cols)
            build_shifts(
                x_ref.at[pl.ds(m * pixels, pixels)], top_ref.at[at_edge], bot_ref.at[at_edge],
                cols, halo, shifts,
            )
            for lane in range(width // LANES):
                lanes = slice(lane * LANES, (lane + 1) * LANES)

                def tap_row(a, carry, lanes=lanes, m=m):
                    found = [jnp.zeros((2 * SUB, LANES), jnp.float32) for _ in range(7)]
                    for kb in range(cols // 16):
                        strip = shifts[a, kb * 8 : kb * 8 + 14, :, lanes]
                        at = pl.ds(m * pixels + kb * 128, 128)
                        grad = gc_ref[at, lanes].astype(jnp.bfloat16).reshape(8, 2 * SUB, LANES)
                        for b in range(7):
                            term = strip[b : b + 8] * grad
                            low = (term[0] + term[1]) + (term[2] + term[3])
                            high = (term[4] + term[5]) + (term[6] + term[7])
                            found[b] = found[b] + (low.astype(jnp.float32) + high.astype(jnp.float32))
                    for b in range(7):
                        total = found[b][:SUB] + found[b][SUB:]
                        if m == 0:
                            sums[a * 7 + b, :, lanes] = total
                        else:
                            sums[a * 7 + b, :, lanes] += total
                    return carry

                lax.fori_loop(0, 7, tap_row, 0)
        taps = jnp.sum(sums[...], axis=1)
        fill = jnp.zeros((TAP_ROWS - taps.shape[0], width), jnp.float32)
        second_ref[hidden_width:, :] = jnp.concatenate([taps, fill], axis=0).astype(jnp.bfloat16)
        for copy in arrive[4:]:
            copy.wait()
        first_ref[...] = lax.dot_general(
            normed_ref[...], gh_ref[...], TN, preferred_element_type=jnp.float32
        ).astype(jnp.bfloat16)

    copies.used = 8
    copies.keep(first_ref, first_hbm.at[slot])

    @pl.when(applied)
    def rest():
        second_ref[:hidden_width, :] = lax.dot_general(
            active_ref[...], gs_ref[...], TN, preferred_element_type=jnp.float32
        ).astype(jnp.bfloat16)

    copies.keep(second_ref, second_hbm.at[slot])
    copies.finish()


def layer_weights(count, kept, back, stacked, slot, micros, cols):
    x, top, bot, _, normed, active, _ = kept
    gs, gh, gc = back
    rows, width = x.shape
    hidden_width = gh.shape[1]
    arrays = (x, top, bot, gc, normed, gh, active, gs)
    return kernel_call(
        functools.partial(weight_body, micros, cols, slot),
        count,
        [(a, HBM) for a in arrays],
        stacked,
        [],
        [pltpu.VMEM((width, hidden_width), jnp.bfloat16), pltpu.VMEM((hidden_width + TAP_ROWS, width), jnp.bfloat16)]
        + conv_scratch(cols, width)[:2]
        + [pltpu.VMEM((49, SUB, width), jnp.float32)]
        + [pltpu.VMEM(a.shape, a.dtype) for a in arrays],
        4 * rows * width * hidden_width,
        VMEM_WEIGHTS,
    )


def loss_body(factor, y_ref, head_ref, labels_ref, g_ref):
    logits = jnp.dot(y_ref[...], head_ref[...], preferred_element_type=jnp.float32)
    spots = lax.broadcasted_iota(jnp.int32, logits.shape, 1)
    target = (labels_ref[...] == spots).astype(jnp.float32)
    grad = (factor * (logits - target)).astype(jnp.bfloat16)
    g_ref[...] = lax.dot_general(
        grad, head_ref[...], NT, preferred_element_type=jnp.float32
    ).astype(jnp.bfloat16)


def on_device(features, section_layers, kernels, gains, w_in, w_out, scales, head_weight, labels):
    sections = lax.axis_size("pipe")
    section_index = lax.axis_index("pipe")
    bands = lax.axis_size("rows")
    micros, band_rows, cols, width = features.shape
    slots = kernels.shape[0]
    hidden_width = w_in.shape[2]
    layer_count = section_layers[0]
    rows = band_rows * cols
    half = cols // 2
    ticks = sections + micros - 1
    f32, b16 = jnp.float32, jnp.bfloat16
    params = (kernels, gains[:, None, :], w_in, w_out, scales[:, None, :])
    dims = (micros, cols)
    edge_shape = (3 * cols, width)

    up = [(i, i + 1) for i in range(bands - 1)]
    down = [(i + 1, i) for i in range(bands - 1)]

    def halo(etop, ebot):
        return lax.ppermute(ebot, "rows", up), lax.ppermute(etop, "rows", down)

    def hop(x, etop, ebot):
        def pairs(by):
            return [
                (p * bands + r, (p + 1) * bands + r + by)
                for p in range(sections - 1)
                for r in range(bands)
                if 0 <= r + by < bands
            ]

        axes = ("pipe", "rows")
        return (
            lax.ppermute(x, axes, pairs(0)),
            lax.ppermute(ebot, axes, pairs(1)),
            lax.ppermute(etop, axes, pairs(-1)),
        )

    def edge_rows(part):
        part = part.reshape(micros, 3, 2, half, width).transpose(0, 1, 3, 2, 4)
        return part.reshape(micros * 3 * cols, width)

    first_x = features.reshape(micros, band_rows, 2, half, width).transpose(0, 3, 2, 1, 4)
    first_in = (
        first_x.reshape(micros * rows, width),
        *halo(edge_rows(features[:, :3]), edge_rows(features[:, band_rows - 3 :])),
    )

    tall, tall_edge = (micros * rows, width), (micros * 3 * cols, width)
    kept_shapes = [
        (tall, b16), (tall_edge, b16), (tall_edge, b16), (tall, f32), (tall, b16),
        ((micros * rows, hidden_width), b16), ((micros * rows, hidden_width), b16),
    ]
    sent_shapes = [((rows, width), b16), (edge_shape, b16), (edge_shape, b16)]
    back_shapes = [(tall, b16), ((micros * rows, hidden_width), b16), (tall, f32)]

    def turn(steps_before, tick):
        micro_no = tick - steps_before
        busy = (micro_no >= 0) & (micro_no < micros)
        ends = [section_index == 0, section_index == sections - 1]
        at = jnp.stack([jnp.clip(micro_no, 0, micros - 1)] + [e.astype(jnp.int32) for e in ends])
        return jnp.where(busy, layer_count, 0), at.astype(jnp.int32)

    def forward_tick(tick, state):
        received, kept0, kept1, outs, sent = state
        which, at = turn(section_index, tick)

        def leave(received, kept0, kept1, outs, sent):
            return kept0, kept1, outs, sent

        def one(received, kept0, kept1, outs, sent):
            _, sent, kept0, outs = layer_front(at, *received, first_in, kept0, outs, params, 0, *dims)
            return kept0, kept1, outs, sent

        def both(received, kept0, kept1, outs, sent):
            y, edges, kept0, outs = layer_front(at, *received, first_in, kept0, outs, params, 0, *dims)
            received = (y, *halo(*edges[1:]))
            _, sent, kept1, outs = layer_front(at, *received, (), kept1, outs, params, 1, *dims)
            return kept0, kept1, outs, sent

        kept0, kept1, outs, sent = lax.switch(
            which, (leave, one, both), received, kept0, kept1, outs, sent
        )
        received = lax.cond(tick < ticks - 1, lambda s: hop(*s), lambda s: tuple(s), sent)
        return received, kept0, kept1, outs, sent

    buffers = tuple(unwritten(kept_shapes + kept_shapes + sent_shapes + sent_shapes + kept_shapes[:1]))
    state = (buffers[17:20], buffers[:7], buffers[7:14], buffers[20], buffers[14:17])
    _, kept0, kept1, outs, sent = lax.fori_loop(0, ticks, forward_tick, state)

    pixel_labels = labels.reshape(micros, band_rows, 2, half).transpose(0, 3, 2, 1)
    from_loss = pl.pallas_call(
        functools.partial(loss_body, loss_scale * 2.0 / (micros * rows * bands)),
        out_shape=jax.ShapeDtypeStruct(tall, b16),
    )(outs, head_weight, pixel_labels.reshape(micros * rows, 1))

    def back_layer(at, g, loss, slot, kept, back, stores, dtype):
        back, gc, edges = layer_point(at, g, loss, kept, back, params, slot, *dims)
        found = layer_spread(at, g, loss, gc, *halo(*edges), stores, params, slot, *dims, dtype)
        return found, back

    back_pairs = [(p + 1, p) for p in range(sections - 1)]

    def backward_tick(tick, state):
        received, back0, back1, boundary, sent = state
        which, at = turn(sections - 1 - section_index, tick)

        def leave(received, back0, back1, boundary, sent):
            return back0, back1, boundary, sent

        def one(received, back0, back1, boundary, sent):
            (boundary, sent), back0 = back_layer(
                at, received, (from_loss,), 0, kept0, back0, (boundary,), b16
            )
            return back0, back1, boundary, sent

        def both(received, back0, back1, boundary, sent):
            (g,), back1 = back_layer(at, received, (from_loss,), 1, kept1, back1, (), f32)
            (boundary, sent), back0 = back_layer(at, g, (), 0, kept0, back0, (boundary,), b16)
            return back0, back1, boundary, sent

        back0, back1, boundary, sent = lax.switch(
            which, (leave, one, both), received, back0, back1, boundary, sent
        )
        return lax.ppermute(sent, "pipe", back_pairs), back0, back1, boundary, sent

    buffers = tuple(unwritten(back_shapes + back_shapes + [(tall, b16)] + sent_shapes[:1] * 2))
    state = (buffers[8], buffers[:3], buffers[3:6], buffers[6], buffers[7])
    state = lax.fori_loop(0, ticks - 1, backward_tick, state)
    received, back0, back1, boundary, _ = state

    _, at = turn(sections - 1 - section_index, ticks - 1)
    owner = section_index == 0

    def last_leave(received, back0, back1, gc, edges):
        return received.astype(f32), back0, back1, gc, edges

    def last_one(received, back0, back1, gc, edges):
        back0, gc, edges = layer_point(at, received, (), kept0, back0, params, 0, *dims)
        return received.astype(f32), back0, back1, gc, halo(*edges)

    def last_both(received, back0, back1, gc, edges):
        (g,), back1 = back_layer(at, received, (), 1, kept1, back1, (), f32)
        back0, gc, edges = layer_point(at, g, (), kept0, back0, params, 0, *dims)
        return g, back0, back1, gc, halo(*edges)

    stacked_shapes = [(slots, width, hidden_width), (slots, hidden_width + TAP_ROWS, width)]
    blank_gc, *stacked = unwritten([((rows, width), f32)] + [(shape, b16) for shape in stacked_shapes])
    g, back0, back1, gc, edges = lax.switch(
        jnp.where(owner, layer_count, 0), (last_leave, last_one, last_both),
        received, back0, back1, blank_gc, (sent[1], sent[2]),
    )
    stacked = layer_weights(section_layers, kept1, back1, stacked, 1, *dims)
    stacked = layer_weights(section_layers, kept0, back0, stacked, 0, *dims)
    w_in_grad, tall_grad = lax.psum(tuple(stacked), "rows")
    boundary = lax.cond(
        owner,
        lambda g, edges, gc, boundary: layer_spread(at, g, (), gc, *edges, (boundary,), params, 0, *dims, b16)[0],
        lambda g, edges, gc, boundary: boundary,
        g, edges, gc, boundary,
    )
    w_out_grad = tall_grad[:, :hidden_width]
    kernel_grad = tall_grad[:, hidden_width : hidden_width + kernels.shape[1]].astype(f32)
    boundary = boundary.reshape(micros, half, 2, band_rows, width).transpose(0, 3, 2, 1, 4)
    boundary = boundary.reshape(micros, band_rows, cols, width)
    return (boundary[None], kernel_grad, w_in_grad, w_out_grad)


def solution(mesh):
    return jax.shard_map(
        on_device,
        mesh=mesh,
        in_specs=(
            P(None, "rows", None, None),
            P("pipe"),
            P("pipe", None, None),
            P("pipe", None),
            P("pipe", None, None),
            P("pipe", None, None),
            P("pipe", None),
            P(),
            P(None, "rows", None),
        ),
        out_specs=(
            P("pipe", None, "rows", None, None),
            P("pipe", None, None),
            P("pipe", None, None),
            P("pipe", None, None),
        ),
        check_vma=False,
    )
```

```python
import functools
import math

import jax
import jax.numpy as jnp
from jax import lax
from jax.experimental import pallas as pl
from jax.experimental.pallas import tpu as pltpu
from jax.sharding import PartitionSpec as P

root_tau = 1.0 / math.sqrt(2.0 * math.pi)
norm_eps = 1e-06
loss_scale = 1024.0
erf_p = 0.3275911
erf_poly = (1.061405429, -1.453152027, 1.421413741, -0.284496736, 0.254829592)
LANES = 128
SUB = 8
NT = (((1,), (1,)), ((), ()))
TN = (((0,), (0,)), ((), ()))
VMEM_LIMIT = 48 * 1024 * 1024
CHUNK = 256
GELU = jnp.bfloat16
TAP_ROWS = 64


def block_spec(array_rows, shape, micros):
    if array_rows:
        return pl.BlockSpec((shape[0] // micros,) + tuple(shape[1:]), lambda m: (m,) + (0,) * (len(shape) - 1))
    return pl.BlockSpec(shape, lambda m: (0,) * len(shape))


def slot_spec(shape, slot):
    return pl.BlockSpec((None,) + tuple(shape[1:]), lambda m: (slot,) + (0,) * (len(shape) - 1))


def per_micro(body, micros, operands, outs, scratch, flops):
    arrays, specs = [], []
    for item in operands:
        if isinstance(item, tuple):
            arrays.append(item[0])
            specs.append(slot_spec(item[0].shape, item[1]))
        else:
            arrays.append(item)
            specs.append(block_spec(True, item.shape, micros))
    size = sum(math.prod(o[0]) * jnp.dtype(o[1]).itemsize for o in outs)
    size += sum(a.size * a.dtype.itemsize for a in arrays)
    return pl.pallas_call(
        body,
        grid=(micros,),
        in_specs=specs,
        out_specs=[block_spec(True, o[0], micros) for o in outs],
        out_shape=[jax.ShapeDtypeStruct(*o) for o in outs],
        scratch_shapes=scratch,
        compiler_params=pltpu.CompilerParams(vmem_limit_bytes=VMEM_LIMIT),
        cost_estimate=pl.CostEstimate(flops=flops, bytes_accessed=size, transcendentals=0),
    )(*arrays)


def unwritten(shapes):
    return pl.pallas_call(
        lambda *refs: None,
        out_specs=[pl.BlockSpec(memory_space=pl.ANY) for _ in shapes],
        out_shape=[jax.ShapeDtypeStruct(*s) for s in shapes],
    )()


def gelu_pair(h):
    e = jnp.exp(h * h * -0.5)
    t = 1.0 / (1.0 + (erf_p * math.sqrt(0.5)) * jnp.abs(h))
    q = t * (0.5 * erf_poly[0]) + 0.5 * erf_poly[1]
    for coef in erf_poly[2:]:
        q = q * t + 0.5 * coef
    q = q * t * e
    phi = jnp.where(h >= 0.0, 1.0 - q, q)
    return h * phi, phi + h * (e * root_tau)


def spread_taps(taps_ref, wide_taps):
    count, width = taps_ref.shape
    for tap in range(count):
        row = jnp.broadcast_to(taps_ref[tap : tap + 1, :], (2 * SUB, width))
        wide_taps[tap] = row.astype(jnp.bfloat16)


def build_shifts(own_ref, top_ref, bot_ref, cols, halo, shifts):
    planes = halo.shape[0]
    half = cols // 2
    for q in range(3):
        at = pl.ds(q * cols, cols)
        for lane in range(planes):
            lanes = slice(lane * LANES, (lane + 1) * LANES)
            plane = halo.at[lane]
            plane[pl.ds(5 + q, cols, stride=SUB), :] = top_ref[at, lanes].astype(jnp.float32)
            plane[pl.ds(q, cols, stride=SUB), :] = bot_ref[at, lanes].astype(jnp.float32)
    sub = lax.broadcasted_iota(jnp.int32, (SUB, LANES), 0)

    def pair(k, carry):
        for lane in range(planes):
            lanes = slice(lane * LANES, (lane + 1) * LANES)
            at = pl.ds(pl.multiple_of(k * 2 * SUB, 2 * SUB), 2 * SUB)
            own = own_ref[at, lanes].astype(jnp.float32)
            edge = halo[lane, at, :]
            for a in range(7):
                if a == 3:
                    both = own
                else:
                    mask = sub >= 5 + a if a < 3 else sub < a - 3
                    both = jnp.concatenate(
                        [
                            pltpu.roll(
                                jnp.where(mask, edge[h * SUB : (h + 1) * SUB], own[h * SUB : (h + 1) * SUB]),
                                (3 - a) % SUB,
                                0,
                            )
                            for h in range(2)
                        ],
                        axis=0,
                    )
                shifts[a, k + 3, :, lanes] = both.astype(jnp.bfloat16)
        return carry

    lax.fori_loop(0, half, pair, 0, unroll=2)
    blank = jnp.zeros((SUB, planes * LANES), jnp.float32)
    for a in range(7):
        for k in range(3):
            right = shifts[a, k + 3].astype(jnp.float32)[SUB:]
            shifts[a, half + 3 + k] = jnp.concatenate([right, blank], axis=0).astype(jnp.bfloat16)
            left = shifts[a, half + k].astype(jnp.float32)[:SUB]
            shifts[a, k] = jnp.concatenate([blank, left], axis=0).astype(jnp.bfloat16)


def convolve(shifts, wide_taps, flip, cols, width, store):
    for lane in range(width // LANES):
        lanes = slice(lane * LANES, (lane + 1) * LANES)

        def block(kb, carry, lanes=lanes):
            acc = jnp.zeros((8, 2 * SUB, LANES), jnp.float32)
            for a in range(7):
                strip = shifts[a, pl.ds(kb * 8, 14), :, lanes]
                line = None
                for b in range(7):
                    tap = 48 - (a * 7 + b) if flip else a * 7 + b
                    term = strip[b : b + 8] * wide_taps[tap, :, lanes][None]
                    line = term if line is None else line + term
                acc = acc + line.astype(jnp.float32)
            store(pl.ds(pl.multiple_of(kb * 128, 128), 128), lanes, acc.reshape(16 * SUB, LANES))
            return carry

        lax.fori_loop(0, cols // 16, block, 0)


def write_edges(source_ref, etop_ref, ebot_ref, halo, cols):
    for lane in range(halo.shape[0]):
        lanes = slice(lane * LANES, (lane + 1) * LANES)
        plane = halo.at[lane]
        plane[...] = source_ref[:, lanes]
        for q in range(3):
            to = pl.ds(q * cols, cols)
            etop_ref[to, lanes] = plane[pl.ds(q, cols, stride=SUB), :].astype(jnp.bfloat16)
            ebot_ref[to, lanes] = plane[pl.ds(q + 5, cols, stride=SUB), :].astype(jnp.bfloat16)


def row_loop(rows, step, fn):
    def body(i, carry):
        fn(pl.ds(pl.multiple_of(i * step, step), step))
        return carry

    lax.fori_loop(0, rows // step, body, 0)


def conv_scratch(cols, width):
    return [
        pltpu.VMEM((width // LANES, cols * SUB, LANES), jnp.float32),
        pltpu.VMEM((7, cols // 2 + 6, 2 * SUB, width), jnp.bfloat16),
        pltpu.VMEM((49, 2 * SUB, width), jnp.bfloat16),
    ]


def front_body(
    cols,
    x_ref, top_ref, bot_ref, taps_ref, gain_ref, w_in_ref, w_out_ref, scale_ref,
    y_ref, out_ref, etop_ref, ebot_ref, conv_ref, normed_ref, active_ref, slope_ref,
    halo, shifts, wide_taps, hidden,
):
    rows, width = x_ref.shape
    hidden_width = w_in_ref.shape[1]

    @pl.when(pl.program_id(0) == 0)
    def first_step():
        spread_taps(taps_ref, wide_taps)

    build_shifts(x_ref, top_ref, bot_ref, cols, halo, shifts)

    def store(at, lanes, value):
        conv_ref[at, lanes] = value

    convolve(shifts, wide_taps, False, cols, width, store)

    def norm(at):
        conv = conv_ref[at, :]
        centred = conv - jnp.mean(conv, axis=-1, keepdims=True)
        spread = jnp.mean(centred * centred, axis=-1, keepdims=True)
        normed_ref[at, :] = (centred * lax.rsqrt(spread + norm_eps) * gain_ref[...]).astype(
            jnp.bfloat16
        )

    row_loop(rows, 64, norm)
    normed = normed_ref[...]
    chunks = hidden_width // CHUNK

    def expand(n):
        hidden[n % 2] = jnp.dot(
            normed, w_in_ref[:, n * CHUNK : (n + 1) * CHUNK], preferred_element_type=jnp.float32
        )

    expand(0)
    for n in range(chunks):
        if n + 1 < chunks:
            expand(n + 1)
        lanes = slice(n * CHUNK, (n + 1) * CHUNK)
        for i in range(rows // 32):
            at = slice(i * 32, (i + 1) * 32)
            value, slope = gelu_pair(hidden[n % 2, at, :].astype(GELU))
            active_ref[at, lanes] = value.astype(jnp.bfloat16)
            slope_ref[at, lanes] = slope.astype(jnp.bfloat16)
    y_ref[...] = x_ref[...].astype(jnp.float32) + scale_ref[...] * jnp.dot(
        active_ref[...], w_out_ref[...], preferred_element_type=jnp.float32
    )
    out_ref[...] = y_ref[...].astype(jnp.bfloat16)
    write_edges(y_ref, etop_ref, ebot_ref, halo, cols)


def layer_front(x, top, bot, params, slot, micros, cols):
    taps, gains, w_in, w_out, scales = params
    rows, width = x.shape
    hidden_width = w_in.shape[2]
    f32, b16 = jnp.float32, jnp.bfloat16
    return per_micro(
        functools.partial(front_body, cols),
        micros,
        (x, top, bot, (taps, slot), (gains, slot), (w_in, slot), (w_out, slot), (scales, slot)),
        [
            ((rows, width), f32), ((rows, width), b16), (top.shape, b16), (bot.shape, b16),
            ((rows, width), f32), ((rows, width), b16),
            ((rows, hidden_width), b16), ((rows, hidden_width), b16),
        ],
        conv_scratch(cols, width) + [pltpu.VMEM((2, rows // micros, CHUNK), f32)],
        4 * rows * width * hidden_width,
    )


def point_body(
    cols,
    g_ref, conv_ref, slope_ref, gain_ref, w_in_ref, w_out_ref, scale_ref,
    gs_ref, gh_ref, gc_ref, etop_ref, ebot_ref, wide, halo,
):
    rows, width = g_ref.shape
    hidden_width = w_in_ref.shape[1]
    gs_ref[...] = (scale_ref[...] * g_ref[...].astype(jnp.float32)).astype(jnp.bfloat16)
    grad = gs_ref[...]
    chunks = hidden_width // CHUNK

    def expand(n):
        wide[n % 2] = lax.dot_general(
            grad, w_out_ref[n * CHUNK : (n + 1) * CHUNK, :], NT, preferred_element_type=jnp.float32
        )

    expand(0)
    for n in range(chunks):
        if n + 1 < chunks:
            expand(n + 1)
        lanes = slice(n * CHUNK, (n + 1) * CHUNK)
        for i in range(rows // 32):
            at = slice(i * 32, (i + 1) * 32)
            gh_ref[at, lanes] = (wide[n % 2, at, :] * slope_ref[at, lanes].astype(jnp.float32)).astype(
                jnp.bfloat16
            )
    gc_ref[...] = lax.dot_general(gh_ref[...], w_in_ref[...], NT, preferred_element_type=jnp.float32)

    def norm_back(at):
        conv = conv_ref[at, :]
        centred = conv - jnp.mean(conv, axis=-1, keepdims=True)
        spread = jnp.mean(centred * centred, axis=-1, keepdims=True)
        scale = lax.rsqrt(spread + norm_eps)
        unit = centred * scale
        grad = gc_ref[at, :] * gain_ref[...]
        first = jnp.mean(grad, axis=-1, keepdims=True)
        second = jnp.mean(grad * unit, axis=-1, keepdims=True)
        gc_ref[at, :] = scale * (grad - first - unit * second)

    row_loop(rows, 64, norm_back)
    write_edges(gc_ref, etop_ref, ebot_ref, halo, cols)


def layer_point(g, conv, slope, params, slot, micros, cols):
    taps, gains, w_in, w_out, scales = params
    rows, width = g.shape
    hidden_width = w_in.shape[2]
    f32, b16 = jnp.float32, jnp.bfloat16
    edge = (micros * 3 * cols, width)
    return per_micro(
        functools.partial(point_body, cols),
        micros,
        (g, conv, slope, (gains, slot), (w_in, slot), (w_out, slot), (scales, slot)),
        [((rows, width), b16), ((rows, hidden_width), b16), ((rows, width), f32), (edge, b16), (edge, b16)],
        [
            pltpu.VMEM((2, rows // micros, CHUNK), f32),
            pltpu.VMEM((width // LANES, cols * SUB, LANES), f32),
        ],
        4 * rows * width * hidden_width,
    )


def spread_body(
    cols, g_ref, gc_ref, top_ref, bot_ref, taps_ref, out_ref, halo, shifts, wide_taps
):
    @pl.when(pl.program_id(0) == 0)
    def first_step():
        spread_taps(taps_ref, wide_taps)

    build_shifts(gc_ref, top_ref, bot_ref, cols, halo, shifts)

    def store(at, lanes, value):
        out_ref[at, lanes] = (g_ref[at, lanes].astype(jnp.float32) + value).astype(out_ref.dtype)

    convolve(shifts, wide_taps, True, cols, g_ref.shape[1], store)


def layer_spread(g, gc, top, bot, params, slot, micros, cols, dtype):
    rows, width = g.shape
    return per_micro(
        functools.partial(spread_body, cols),
        micros,
        (g, gc, top, bot, (params[0], slot)),
        [((rows, width), dtype)],
        conv_scratch(cols, width),
        98 * rows * width,
    )[0]


def weight_body(
    micros, cols, slot,
    count_ref, x_ref, top_ref, bot_ref, gc_ref, normed_ref, gh_ref, active_ref, gs_ref,
    *refs,
):
    first_ref, second_ref, halo, shifts, sums = refs[-5:]
    hidden_width = gh_ref.shape[1]
    width = x_ref.shape[1]
    applied = slot < count_ref[0]

    @pl.when(jnp.logical_not(applied))
    def passed():
        first_ref[...] = jnp.zeros_like(first_ref)
        second_ref[...] = jnp.zeros_like(second_ref)

    @pl.when(applied)
    def run():
        first_ref[...] = lax.dot_general(
            normed_ref[...], gh_ref[...], TN, preferred_element_type=jnp.float32
        ).astype(jnp.bfloat16)
        second_ref[:hidden_width, :] = lax.dot_general(
            active_ref[...], gs_ref[...], TN, preferred_element_type=jnp.float32
        ).astype(jnp.bfloat16)
        pixels = cols * SUB
        for m in range(micros):
            at_edge = pl.ds(m * 3 * cols, 3 * cols)
            build_shifts(
                x_ref.at[pl.ds(m * pixels, pixels)], top_ref.at[at_edge], bot_ref.at[at_edge],
                cols, halo, shifts,
            )
            for lane in range(width // LANES):
                lanes = slice(lane * LANES, (lane + 1) * LANES)

                def tap_row(a, carry, lanes=lanes, m=m):
                    found = [jnp.zeros((2 * SUB, LANES), jnp.float32) for _ in range(7)]
                    for kb in range(cols // 16):
                        strip = shifts[a, kb * 8 : kb * 8 + 14, :, lanes]
                        at = pl.ds(m * pixels + kb * 128, 128)
                        grad = gc_ref[at, lanes].astype(jnp.bfloat16).reshape(8, 2 * SUB, LANES)
                        for b in range(7):
                            term = strip[b : b + 8] * grad
                            term = (term[0] + term[1]) + (term[2] + term[3]), (term[4] + term[5]) + (term[6] + term[7])
                            found[b] = found[b] + (term[0].astype(jnp.float32) + term[1].astype(jnp.float32))
                    for b in range(7):
                        total = found[b][:SUB] + found[b][SUB:]
                        if m == 0:
                            sums[a * 7 + b, :, lanes] = total
                        else:
                            sums[a * 7 + b, :, lanes] += total
                    return carry

                lax.fori_loop(0, 7, tap_row, 0)
        taps = jnp.sum(sums[...], axis=1)
        fill = jnp.zeros((TAP_ROWS - taps.shape[0], width), jnp.float32)
        second_ref[hidden_width:, :] = jnp.concatenate([taps, fill], axis=0).astype(jnp.bfloat16)


def layer_weights(count, kept, back, stacked, slots, slot, micros, cols):
    x, top, bot, _, normed, active, _ = kept
    gs, gh, gc = back
    rows, width = x.shape
    hidden_width = gh.shape[1]
    f32, b16 = jnp.float32, jnp.bfloat16
    arrays = (x, top, bot, gc, normed, gh, active, gs)
    outs = [((slots, width, hidden_width), b16), ((slots, hidden_width + TAP_ROWS, width), b16)]
    size = sum(math.prod(o[0]) * jnp.dtype(o[1]).itemsize for o in outs)
    size += sum(a.size * a.dtype.itemsize for a in arrays)
    return pl.pallas_call(
        functools.partial(weight_body, micros, cols, slot),
        grid=(1,),
        in_specs=[pl.BlockSpec(memory_space=pltpu.SMEM)] + [block_spec(False, a.shape, 1) for a in arrays]
        + [pl.BlockSpec(memory_space=pl.ANY) for _ in stacked],
        out_specs=[slot_spec(o[0], slot) for o in outs],
        input_output_aliases={1 + len(arrays) + i: i for i in range(len(stacked))},
        out_shape=[jax.ShapeDtypeStruct(*o) for o in outs],
        scratch_shapes=conv_scratch(cols, width)[:2] + [pltpu.VMEM((49, SUB, width), f32)],
        compiler_params=pltpu.CompilerParams(vmem_limit_bytes=VMEM_LIMIT),
        cost_estimate=pl.CostEstimate(
            flops=4 * rows * width * hidden_width, bytes_accessed=size, transcendentals=0
        ),
    )(count, *arrays, *stacked)


def loss_body(factor, y_ref, head_ref, labels_ref, g_ref):
    logits = jnp.dot(y_ref[...], head_ref[...], preferred_element_type=jnp.float32)
    spots = lax.broadcasted_iota(jnp.int32, logits.shape, 1)
    target = (labels_ref[...] == spots).astype(jnp.float32)
    grad = (factor * (logits - target)).astype(jnp.bfloat16)
    g_ref[...] = lax.dot_general(
        grad, head_ref[...], NT, preferred_element_type=jnp.float32
    ).astype(jnp.bfloat16)


def on_device(features, section_layers, kernels, gains, w_in, w_out, scales, head_weight, labels):
    sections = lax.axis_size("pipe")
    section_index = lax.axis_index("pipe")
    bands = lax.axis_size("rows")
    micros, band_rows, cols, width = features.shape
    hidden_width = w_in.shape[2]
    classes = head_weight.shape[1]
    layer_count = section_layers[0]
    rows = micros * band_rows * cols
    half = cols // 2
    f32, b16 = jnp.float32, jnp.bfloat16
    params = (kernels, gains[:, None, :], w_in, w_out, scales[:, None, :])
    dims = (micros, cols)
    edge_shape = (micros * 3 * cols, width)

    up = [(i, i + 1) for i in range(bands - 1)]
    down = [(i + 1, i) for i in range(bands - 1)]

    def halo(etop, ebot):
        return lax.ppermute(ebot, "rows", up), lax.ppermute(etop, "rows", down)

    def hop(x, etop, ebot):
        def pairs(by):
            return [
                (p * bands + r, (p + 1) * bands + r + by)
                for p in range(sections - 1)
                for r in range(bands)
                if 0 <= r + by < bands
            ]

        axes = ("pipe", "rows")
        return (
            lax.ppermute(x, axes, pairs(0)),
            lax.ppermute(ebot, axes, pairs(1)),
            lax.ppermute(etop, axes, pairs(-1)),
        )

    def edge_rows(part):
        part = part.reshape(micros, 3, 2, half, width).transpose(0, 1, 3, 2, 4)
        return part.reshape(edge_shape)

    first_x = features.reshape(micros, band_rows, 2, half, width).transpose(0, 3, 2, 1, 4)
    first_in = (
        first_x.reshape(rows, width),
        *halo(edge_rows(features[:, :3]), edge_rows(features[:, band_rows - 3 :])),
    )

    def kept_shapes(dtype_x):
        return [
            ((rows, width), dtype_x), (edge_shape, b16), (edge_shape, b16), ((rows, width), f32),
            ((rows, width), b16), ((rows, hidden_width), b16), ((rows, hidden_width), b16),
        ]

    sent_shapes = [((rows, width), b16), (edge_shape, b16), (edge_shape, b16)]
    back_shapes = [((rows, width), b16), ((rows, hidden_width), b16), ((rows, width), f32)]

    def front(x, top, bot, slot):
        y, out, etop, ebot, conv, normed, active, slope = layer_front(x, top, bot, params, slot, *dims)
        return y, (out, etop, ebot), (x, top, bot, conv, normed, active, slope)

    def forward_section(tick, received, kept0, kept1, sent):
        def leave(received, kept0, kept1, sent):
            return kept0, kept1, sent

        def one(received, kept0, kept1, sent):
            _, sent, kept0 = front(*received, 0)
            return kept0, kept1, sent

        def both(received, kept0, kept1, sent):
            y, (_, etop, ebot), kept0 = front(*received, 0)
            _, sent, kept1 = front(y, *halo(etop, ebot), 1)
            return kept0, kept1, sent

        which = jnp.where(tick == section_index, layer_count, 0)
        return lax.switch(which, (leave, one, both), received, kept0, kept1, sent)

    def forward_tick(tick, state):
        received, kept0, kept1, sent = state
        kept0, kept1, sent = forward_section(tick, received, kept0, kept1, sent)
        return hop(*sent), kept0, kept1, sent

    buffers = unwritten(kept_shapes(b16) + kept_shapes(f32) + sent_shapes)
    state = (first_in, tuple(buffers[:7]), tuple(buffers[7:14]), tuple(buffers[14:]))
    state = lax.fori_loop(0, sections - 1, forward_tick, state)
    kept0, kept1, sent = forward_section(sections - 1, *state)

    total = micros * band_rows * bands * cols
    pixel_labels = labels.reshape(micros, band_rows, 2, half).transpose(0, 3, 2, 1).reshape(rows, 1)
    from_loss = pl.pallas_call(
        functools.partial(loss_body, loss_scale * 2.0 / total),
        out_shape=jax.ShapeDtypeStruct((rows, width), b16),
    )(sent[0], head_weight, pixel_labels)

    def back_layer(g, slot, kept, dtype):
        gs, gh, gc, etop, ebot = layer_point(g, kept[3], kept[6], params, slot, *dims)
        g = layer_spread(g, gc, *halo(etop, ebot), params, slot, *dims, dtype)
        return g, (gs, gh, gc)

    back_pairs = [(p + 1, p) for p in range(sections - 1)]

    def backward_section(tick, incoming, back0, back1, cotangent):
        def leave(incoming, back0, back1, cotangent):
            return back0, back1, cotangent

        def one(incoming, back0, back1, cotangent):
            cotangent, back0 = back_layer(incoming, 0, kept0, b16)
            return back0, back1, cotangent

        def both(incoming, back0, back1, cotangent):
            g, back1 = back_layer(incoming, 1, kept1, f32)
            cotangent, back0 = back_layer(g, 0, kept0, b16)
            return back0, back1, cotangent

        which = jnp.where(tick == sections - 1 - section_index, layer_count, 0)
        return lax.switch(which, (leave, one, both), incoming, back0, back1, cotangent)

    def backward_tick(tick, state):
        incoming, back0, back1, cotangent = state
        back0, back1, cotangent = backward_section(tick, incoming, back0, back1, cotangent)
        return lax.ppermute(cotangent, "pipe", back_pairs), back0, back1, cotangent

    buffers = unwritten(back_shapes + back_shapes + sent_shapes[:1])
    state = (from_loss, tuple(buffers[:3]), tuple(buffers[3:6]), buffers[6])
    state = lax.fori_loop(0, sections - 1, backward_tick, state)
    incoming, back0, back1, cotangent = state

    owner = section_index == 0
    g, back1 = lax.cond(
        owner & (layer_count > 1),
        lambda g, back1: back_layer(g, 1, kept1, f32),
        lambda g, back1: (g.astype(f32), back1),
        incoming, back1,
    )

    def last_point(g, back0, sent):
        gs, gh, gc, etop, ebot = layer_point(g, kept0[3], kept0[6], params, 0, *dims)
        return (gs, gh, gc), halo(etop, ebot)

    back0, edges = lax.cond(
        owner, last_point, lambda g, back0, sent: (back0, sent[1:]), g, back0, tuple(sent)
    )
    slots = kernels.shape[0]
    stacked = layer_weights(section_layers, kept1, back1, (), slots, 1, *dims)
    stacked = layer_weights(section_layers, kept0, back0, stacked, slots, 0, *dims)
    w_in_grad, tall = lax.psum(tuple(stacked), "rows")
    cotangent = lax.cond(
        owner,
        lambda g, edges, gc, cotangent: layer_spread(g, gc, *edges, params, 0, *dims, b16),
        lambda g, edges, gc, cotangent: cotangent,
        g, edges, back0[2], cotangent,
    )
    w_out_grad = tall[:, :hidden_width]
    kernel_grad = tall[:, hidden_width : hidden_width + kernels.shape[1]].astype(f32)
    boundary = cotangent.reshape(micros, half, 2, band_rows, width).transpose(0, 3, 2, 1, 4)
    boundary = boundary.reshape(micros, band_rows, cols, width)
    return (boundary[None], kernel_grad, w_in_grad, w_out_grad)


def solution(mesh):
    return jax.shard_map(
        on_device,
        mesh=mesh,
        in_specs=(
            P(None, "rows", None, None),
            P("pipe"),
            P("pipe", None, None),
            P("pipe", None),
            P("pipe", None, None),
            P("pipe", None, None),
            P("pipe", None),
            P(),
            P(None, "rows", None),
        ),
        out_specs=(
            P("pipe", None, "rows", None, None),
            P("pipe", None, None),
            P("pipe", None, None),
            P("pipe", None, None),
        ),
        check_vma=False,
    )
```

```python
import functools
import math

import jax
import jax.numpy as jnp
from jax import lax
from jax.experimental import pallas as pl
from jax.experimental.pallas import tpu as pltpu
from jax.sharding import PartitionSpec as P

root_tau = 1.0 / math.sqrt(2.0 * math.pi)
norm_eps = 1e-06
loss_scale = 1024.0
erf_p = 0.3275911
erf_poly = (1.061405429, -1.453152027, 1.421413741, -0.284496736, 0.254829592)
LANES = 128
SUB = 8
NT = (((1,), (1,)), ((), ()))
TN = (((0,), (0,)), ((), ()))
VMEM_LIMIT = 48 * 1024 * 1024
CHUNK = 256
GELU = jnp.bfloat16
TAP_ROWS = 64


def block_spec(array_rows, shape, micros):
    if array_rows:
        return pl.BlockSpec((shape[0] // micros,) + tuple(shape[1:]), lambda m: (m,) + (0,) * (len(shape) - 1))
    return pl.BlockSpec(shape, lambda m: (0,) * len(shape))


def slot_spec(shape, slot):
    return pl.BlockSpec((None,) + tuple(shape[1:]), lambda m: (slot,) + (0,) * (len(shape) - 1))


def per_micro(body, micros, operands, outs, scratch, flops):
    arrays, specs = [], []
    for item in operands:
        if isinstance(item, tuple):
            arrays.append(item[0])
            specs.append(slot_spec(item[0].shape, item[1]))
        else:
            arrays.append(item)
            specs.append(block_spec(True, item.shape, micros))
    size = sum(math.prod(o[0]) * jnp.dtype(o[1]).itemsize for o in outs)
    size += sum(a.size * a.dtype.itemsize for a in arrays)
    return pl.pallas_call(
        body,
        grid=(micros,),
        in_specs=specs,
        out_specs=[block_spec(True, o[0], micros) for o in outs],
        out_shape=[jax.ShapeDtypeStruct(*o) for o in outs],
        scratch_shapes=scratch,
        compiler_params=pltpu.CompilerParams(vmem_limit_bytes=VMEM_LIMIT),
        cost_estimate=pl.CostEstimate(flops=flops, bytes_accessed=size, transcendentals=0),
    )(*arrays)


def unwritten(shapes):
    return pl.pallas_call(
        lambda *refs: None,
        out_specs=[pl.BlockSpec(memory_space=pl.ANY) for _ in shapes],
        out_shape=[jax.ShapeDtypeStruct(*s) for s in shapes],
    )()


def gelu_pair(h):
    e = jnp.exp(h * h * -0.5)
    t = pl.reciprocal(1.0 + (erf_p * math.sqrt(0.5)) * jnp.abs(h), approx=True)
    q = t * (0.5 * erf_poly[0]) + 0.5 * erf_poly[1]
    for coef in erf_poly[2:]:
        q = q * t + 0.5 * coef
    q = q * t * e
    phi = jnp.where(h >= 0.0, 1.0 - q, q)
    return h * phi, phi + h * (e * root_tau)


def spread_taps(taps_ref, wide_taps):
    count, width = taps_ref.shape
    for tap in range(count):
        row = jnp.broadcast_to(taps_ref[tap : tap + 1, :], (2 * SUB, width))
        wide_taps[tap] = row.astype(jnp.bfloat16)


def build_shifts(own_ref, top_ref, bot_ref, cols, halo, shifts):
    planes = halo.shape[0]
    half = cols // 2
    for q in range(3):
        at = pl.ds(q * cols, cols)
        for lane in range(planes):
            lanes = slice(lane * LANES, (lane + 1) * LANES)
            plane = halo.at[lane]
            plane[pl.ds(5 + q, cols, stride=SUB), :] = top_ref[at, lanes].astype(jnp.float32)
            plane[pl.ds(q, cols, stride=SUB), :] = bot_ref[at, lanes].astype(jnp.float32)
    sub = lax.broadcasted_iota(jnp.int32, (SUB, LANES), 0)

    def pair(k, carry):
        for lane in range(planes):
            lanes = slice(lane * LANES, (lane + 1) * LANES)
            at = pl.ds(pl.multiple_of(k * 2 * SUB, 2 * SUB), 2 * SUB)
            own = own_ref[at, lanes].astype(jnp.float32)
            edge = halo[lane, at, :]
            for a in range(7):
                if a == 3:
                    both = own
                else:
                    mask = sub >= 5 + a if a < 3 else sub < a - 3
                    both = jnp.concatenate(
                        [
                            pltpu.roll(
                                jnp.where(mask, edge[h * SUB : (h + 1) * SUB], own[h * SUB : (h + 1) * SUB]),
                                (3 - a) % SUB,
                                0,
                            )
                            for h in range(2)
                        ],
                        axis=0,
                    )
                shifts[a, k + 3, :, lanes] = both.astype(jnp.bfloat16)
        return carry

    lax.fori_loop(0, half, pair, 0, unroll=2)
    blank = jnp.zeros((SUB, planes * LANES), jnp.float32)
    for a in range(7):
        for k in range(3):
            right = shifts[a, k + 3].astype(jnp.float32)[SUB:]
            shifts[a, half + 3 + k] = jnp.concatenate([right, blank], axis=0).astype(jnp.bfloat16)
            left = shifts[a, half + k].astype(jnp.float32)[:SUB]
            shifts[a, k] = jnp.concatenate([blank, left], axis=0).astype(jnp.bfloat16)


def convolve(shifts, wide_taps, flip, cols, width, store):
    for lane in range(width // LANES):
        lanes = slice(lane * LANES, (lane + 1) * LANES)

        def block(kb, carry, lanes=lanes):
            acc = jnp.zeros((8, 2 * SUB, LANES), jnp.float32)
            for a in range(7):
                strip = shifts[a, pl.ds(kb * 8, 14), :, lanes]
                line = None
                for b in range(7):
                    tap = 48 - (a * 7 + b) if flip else a * 7 + b
                    term = strip[b : b + 8] * wide_taps[tap, :, lanes][None]
                    line = term if line is None else line + term
                acc = acc + line.astype(jnp.float32)
            store(pl.ds(pl.multiple_of(kb * 128, 128), 128), lanes, acc.reshape(16 * SUB, LANES))
            return carry

        lax.fori_loop(0, cols // 16, block, 0)


def write_edges(source_ref, etop_ref, ebot_ref, halo, cols):
    for lane in range(halo.shape[0]):
        lanes = slice(lane * LANES, (lane + 1) * LANES)
        plane = halo.at[lane]
        plane[...] = source_ref[:, lanes]
        for q in range(3):
            to = pl.ds(q * cols, cols)
            etop_ref[to, lanes] = plane[pl.ds(q, cols, stride=SUB), :].astype(jnp.bfloat16)
            ebot_ref[to, lanes] = plane[pl.ds(q + 5, cols, stride=SUB), :].astype(jnp.bfloat16)


def row_loop(rows, step, fn):
    def body(i, carry):
        fn(pl.ds(pl.multiple_of(i * step, step), step))
        return carry

    lax.fori_loop(0, rows // step, body, 0)


def conv_scratch(cols, width):
    return [
        pltpu.VMEM((width // LANES, cols * SUB, LANES), jnp.float32),
        pltpu.VMEM((7, cols // 2 + 6, 2 * SUB, width), jnp.bfloat16),
        pltpu.VMEM((49, 2 * SUB, width), jnp.bfloat16),
    ]


def front_body(
    cols,
    x_ref, top_ref, bot_ref, taps_ref, gain_ref, w_in_ref, w_out_ref, scale_ref,
    out_ref, etop_ref, ebot_ref, centred_ref, normed_ref, active_ref, slope_ref,
    halo, shifts, wide_taps, hidden, conv_ref,
):
    rows, width = x_ref.shape
    hidden_width = w_in_ref.shape[1]

    @pl.when(pl.program_id(0) == 0)
    def first_step():
        spread_taps(taps_ref, wide_taps)

    build_shifts(x_ref, top_ref, bot_ref, cols, halo, shifts)

    def store(at, lanes, value):
        conv_ref[at, lanes] = value

    convolve(shifts, wide_taps, False, cols, width, store)

    def norm(at):
        conv = conv_ref[at, :]
        centred = conv - jnp.mean(conv, axis=-1, keepdims=True)
        spread = jnp.mean(centred * centred, axis=-1, keepdims=True)
        centred_ref[at, :] = centred.astype(jnp.bfloat16)
        normed_ref[at, :] = (centred * lax.rsqrt(spread + norm_eps) * gain_ref[...]).astype(
            jnp.bfloat16
        )

    row_loop(rows, 64, norm)
    normed = normed_ref[...]
    chunks = hidden_width // CHUNK

    def expand(n):
        hidden[n % 2] = jnp.dot(
            normed, w_in_ref[:, n * CHUNK : (n + 1) * CHUNK], preferred_element_type=jnp.float32
        )

    expand(0)
    for n in range(chunks):
        if n + 1 < chunks:
            expand(n + 1)
        lanes = slice(n * CHUNK, (n + 1) * CHUNK)
        for i in range(rows // 32):
            at = slice(i * 32, (i + 1) * 32)
            value, slope = gelu_pair(hidden[n % 2, at, :].astype(GELU))
            active_ref[at, lanes] = value.astype(jnp.bfloat16)
            slope_ref[at, lanes] = slope.astype(jnp.bfloat16)
    y_ref = conv_ref
    y_ref[...] = x_ref[...].astype(jnp.float32) + scale_ref[...] * jnp.dot(
        active_ref[...], w_out_ref[...], preferred_element_type=jnp.float32
    )
    out_ref[...] = y_ref[...].astype(out_ref.dtype)
    write_edges(y_ref, etop_ref, ebot_ref, halo, cols)


def layer_front(x, top, bot, params, slot, micros, cols, dtype):
    taps, gains, w_in, w_out, scales = params
    rows, width = x.shape
    hidden_width = w_in.shape[2]
    f32, b16 = jnp.float32, jnp.bfloat16
    return per_micro(
        functools.partial(front_body, cols),
        micros,
        (x, top, bot, (taps, slot), (gains, slot), (w_in, slot), (w_out, slot), (scales, slot)),
        [
            ((rows, width), dtype), (top.shape, b16), (bot.shape, b16),
            ((rows, width), b16), ((rows, width), b16),
            ((rows, hidden_width), b16), ((rows, hidden_width), b16),
        ],
        conv_scratch(cols, width)
        + [pltpu.VMEM((2, rows // micros, CHUNK), f32), pltpu.VMEM((rows // micros, width), f32)],
        4 * rows * width * hidden_width,
    )


def point_body(
    cols,
    g_ref, centred_ref, slope_ref, gain_ref, w_in_ref, w_out_ref, scale_ref,
    gs_ref, gh_ref, gc_ref, etop_ref, ebot_ref, wide, halo,
):
    rows, width = g_ref.shape
    hidden_width = w_in_ref.shape[1]
    gs_ref[...] = (scale_ref[...] * g_ref[...].astype(jnp.float32)).astype(jnp.bfloat16)
    grad = gs_ref[...]
    chunks = hidden_width // CHUNK

    def expand(n):
        wide[n % 2] = lax.dot_general(
            grad, w_out_ref[n * CHUNK : (n + 1) * CHUNK, :], NT, preferred_element_type=jnp.float32
        )

    expand(0)
    for n in range(chunks):
        if n + 1 < chunks:
            expand(n + 1)
        lanes = slice(n * CHUNK, (n + 1) * CHUNK)
        for i in range(rows // 32):
            at = slice(i * 32, (i + 1) * 32)
            gh_ref[at, lanes] = (wide[n % 2, at, :] * slope_ref[at, lanes].astype(jnp.float32)).astype(
                jnp.bfloat16
            )
    gc_ref[...] = lax.dot_general(gh_ref[...], w_in_ref[...], NT, preferred_element_type=jnp.float32)

    def norm_back(at):
        centred = centred_ref[at, :].astype(jnp.float32)
        spread = jnp.mean(centred * centred, axis=-1, keepdims=True)
        scale = lax.rsqrt(spread + norm_eps)
        unit = centred * scale
        grad = gc_ref[at, :] * gain_ref[...]
        first = jnp.mean(grad, axis=-1, keepdims=True)
        second = jnp.mean(grad * unit, axis=-1, keepdims=True)
        gc_ref[at, :] = scale * (grad - first - unit * second)

    row_loop(rows, 64, norm_back)
    write_edges(gc_ref, etop_ref, ebot_ref, halo, cols)


def layer_point(g, conv, slope, params, slot, micros, cols):
    taps, gains, w_in, w_out, scales = params
    rows, width = g.shape
    hidden_width = w_in.shape[2]
    f32, b16 = jnp.float32, jnp.bfloat16
    edge = (micros * 3 * cols, width)
    return per_micro(
        functools.partial(point_body, cols),
        micros,
        (g, conv, slope, (gains, slot), (w_in, slot), (w_out, slot), (scales, slot)),
        [((rows, width), b16), ((rows, hidden_width), b16), ((rows, width), f32), (edge, b16), (edge, b16)],
        [
            pltpu.VMEM((2, rows // micros, CHUNK), f32),
            pltpu.VMEM((width // LANES, cols * SUB, LANES), f32),
        ],
        4 * rows * width * hidden_width,
    )


def spread_body(
    cols, g_ref, gc_ref, top_ref, bot_ref, taps_ref, out_ref, halo, shifts, wide_taps
):
    @pl.when(pl.program_id(0) == 0)
    def first_step():
        spread_taps(taps_ref, wide_taps)

    build_shifts(gc_ref, top_ref, bot_ref, cols, halo, shifts)

    def store(at, lanes, value):
        out_ref[at, lanes] = (g_ref[at, lanes].astype(jnp.float32) + value).astype(out_ref.dtype)

    convolve(shifts, wide_taps, True, cols, g_ref.shape[1], store)


def layer_spread(g, gc, top, bot, params, slot, micros, cols, dtype):
    rows, width = g.shape
    return per_micro(
        functools.partial(spread_body, cols),
        micros,
        (g, gc, top, bot, (params[0], slot)),
        [((rows, width), dtype)],
        conv_scratch(cols, width),
        98 * rows * width,
    )[0]


def weight_body(
    micros, cols, slot,
    count_ref, x_ref, top_ref, bot_ref, gc_ref, normed_ref, gh_ref, active_ref, gs_ref,
    *refs,
):
    first_ref, second_ref, halo, shifts, sums = refs[-5:]
    hidden_width = gh_ref.shape[1]
    width = x_ref.shape[1]
    applied = slot < count_ref[0]

    @pl.when(jnp.logical_not(applied))
    def passed():
        first_ref[...] = jnp.zeros_like(first_ref)
        second_ref[...] = jnp.zeros_like(second_ref)

    @pl.when(applied)
    def run():
        first_ref[...] = lax.dot_general(
            normed_ref[...], gh_ref[...], TN, preferred_element_type=jnp.float32
        ).astype(jnp.bfloat16)
        second_ref[:hidden_width, :] = lax.dot_general(
            active_ref[...], gs_ref[...], TN, preferred_element_type=jnp.float32
        ).astype(jnp.bfloat16)
        pixels = cols * SUB
        for m in range(micros):
            at_edge = pl.ds(m * 3 * cols, 3 * cols)
            build_shifts(
                x_ref.at[pl.ds(m * pixels, pixels)], top_ref.at[at_edge], bot_ref.at[at_edge],
                cols, halo, shifts,
            )
            for lane in range(width // LANES):
                lanes = slice(lane * LANES, (lane + 1) * LANES)

                def tap_row(a, carry, lanes=lanes, m=m):
                    found = [jnp.zeros((2 * SUB, LANES), jnp.float32) for _ in range(7)]
                    for kb in range(cols // 16):
                        strip = shifts[a, kb * 8 : kb * 8 + 14, :, lanes]
                        at = pl.ds(m * pixels + kb * 128, 128)
                        grad = gc_ref[at, lanes].astype(jnp.bfloat16).reshape(8, 2 * SUB, LANES)
                        for b in range(7):
                            term = strip[b : b + 8] * grad
                            term = (term[0] + term[1]) + (term[2] + term[3]), (term[4] + term[5]) + (term[6] + term[7])
                            found[b] = found[b] + (term[0].astype(jnp.float32) + term[1].astype(jnp.float32))
                    for b in range(7):
                        total = found[b][:SUB] + found[b][SUB:]
                        if m == 0:
                            sums[a * 7 + b, :, lanes] = total
                        else:
                            sums[a * 7 + b, :, lanes] += total
                    return carry

                lax.fori_loop(0, 7, tap_row, 0)
        taps = jnp.sum(sums[...], axis=1)
        fill = jnp.zeros((TAP_ROWS - taps.shape[0], width), jnp.float32)
        second_ref[hidden_width:, :] = jnp.concatenate([taps, fill], axis=0).astype(jnp.bfloat16)


def layer_weights(count, kept, back, stacked, slots, slot, micros, cols):
    x, top, bot, _, normed, active, _ = kept
    gs, gh, gc = back
    rows, width = x.shape
    hidden_width = gh.shape[1]
    f32, b16 = jnp.float32, jnp.bfloat16
    arrays = (x, top, bot, gc, normed, gh, active, gs)
    outs = [((slots, width, hidden_width), b16), ((slots, hidden_width + TAP_ROWS, width), b16)]
    size = sum(math.prod(o[0]) * jnp.dtype(o[1]).itemsize for o in outs)
    size += sum(a.size * a.dtype.itemsize for a in arrays)
    return pl.pallas_call(
        functools.partial(weight_body, micros, cols, slot),
        grid=(1,),
        in_specs=[pl.BlockSpec(memory_space=pltpu.SMEM)] + [block_spec(False, a.shape, 1) for a in arrays]
        + [pl.BlockSpec(memory_space=pl.ANY) for _ in stacked],
        out_specs=[slot_spec(o[0], slot) for o in outs],
        input_output_aliases={1 + len(arrays) + i: i for i in range(len(stacked))},
        out_shape=[jax.ShapeDtypeStruct(*o) for o in outs],
        scratch_shapes=conv_scratch(cols, width)[:2] + [pltpu.VMEM((49, SUB, width), f32)],
        compiler_params=pltpu.CompilerParams(vmem_limit_bytes=VMEM_LIMIT),
        cost_estimate=pl.CostEstimate(
            flops=4 * rows * width * hidden_width, bytes_accessed=size, transcendentals=0
        ),
    )(count, *arrays, *stacked)


def loss_body(factor, y_ref, head_ref, labels_ref, g_ref):
    logits = jnp.dot(y_ref[...], head_ref[...], preferred_element_type=jnp.float32)
    spots = lax.broadcasted_iota(jnp.int32, logits.shape, 1)
    target = (labels_ref[...] == spots).astype(jnp.float32)
    grad = (factor * (logits - target)).astype(jnp.bfloat16)
    g_ref[...] = lax.dot_general(
        grad, head_ref[...], NT, preferred_element_type=jnp.float32
    ).astype(jnp.bfloat16)


def on_device(features, section_layers, kernels, gains, w_in, w_out, scales, head_weight, labels):
    sections = lax.axis_size("pipe")
    section_index = lax.axis_index("pipe")
    bands = lax.axis_size("rows")
    micros, band_rows, cols, width = features.shape
    hidden_width = w_in.shape[2]
    classes = head_weight.shape[1]
    layer_count = section_layers[0]
    rows = micros * band_rows * cols
    half = cols // 2
    f32, b16 = jnp.float32, jnp.bfloat16
    params = (kernels, gains[:, None, :], w_in, w_out, scales[:, None, :])
    dims = (micros, cols)
    edge_shape = (micros * 3 * cols, width)

    up = [(i, i + 1) for i in range(bands - 1)]
    down = [(i + 1, i) for i in range(bands - 1)]

    def halo(etop, ebot):
        return lax.ppermute(ebot, "rows", up), lax.ppermute(etop, "rows", down)

    def hop(x, etop, ebot):
        def pairs(by):
            return [
                (p * bands + r, (p + 1) * bands + r + by)
                for p in range(sections - 1)
                for r in range(bands)
                if 0 <= r + by < bands
            ]

        axes = ("pipe", "rows")
        return (
            lax.ppermute(x, axes, pairs(0)),
            lax.ppermute(ebot, axes, pairs(1)),
            lax.ppermute(etop, axes, pairs(-1)),
        )

    def edge_rows(part):
        part = part.reshape(micros, 3, 2, half, width).transpose(0, 1, 3, 2, 4)
        return part.reshape(edge_shape)

    first_x = features.reshape(micros, band_rows, 2, half, width).transpose(0, 3, 2, 1, 4)
    first_in = (
        first_x.reshape(rows, width),
        *halo(edge_rows(features[:, :3]), edge_rows(features[:, band_rows - 3 :])),
    )

    def kept_shapes(dtype_x):
        return [
            ((rows, width), dtype_x), (edge_shape, b16), (edge_shape, b16), ((rows, width), b16),
            ((rows, width), b16), ((rows, hidden_width), b16), ((rows, hidden_width), b16),
        ]

    sent_shapes = [((rows, width), b16), (edge_shape, b16), (edge_shape, b16)]
    back_shapes = [((rows, width), b16), ((rows, hidden_width), b16), ((rows, width), f32)]

    def front(x, top, bot, slot, dtype):
        out, etop, ebot, *values = layer_front(x, top, bot, params, slot, *dims, dtype)
        return (out, etop, ebot), (x, top, bot, *values)

    def forward_section(tick, received, kept0, kept1, sent):
        def leave(received, kept0, kept1, sent):
            return kept0, kept1, sent

        def one(received, kept0, kept1, sent):
            sent, kept0 = front(*received, 0, b16)
            return kept0, kept1, sent

        def both(received, kept0, kept1, sent):
            (y, etop, ebot), kept0 = front(*received, 0, f32)
            sent, kept1 = front(y, *halo(etop, ebot), 1, b16)
            return kept0, kept1, sent

        which = jnp.where(tick == section_index, layer_count, 0)
        return lax.switch(which, (leave, one, both), received, kept0, kept1, sent)

    def forward_tick(tick, state):
        received, kept0, kept1, sent = state
        kept0, kept1, sent = forward_section(tick, received, kept0, kept1, sent)
        return hop(*sent), kept0, kept1, sent

    buffers = unwritten(kept_shapes(b16) + kept_shapes(f32) + sent_shapes)
    state = (first_in, tuple(buffers[:7]), tuple(buffers[7:14]), tuple(buffers[14:]))
    state = lax.fori_loop(0, sections - 1, forward_tick, state)
    kept0, kept1, sent = forward_section(sections - 1, *state)

    total = micros * band_rows * bands * cols
    pixel_labels = labels.reshape(micros, band_rows, 2, half).transpose(0, 3, 2, 1).reshape(rows, 1)
    from_loss = pl.pallas_call(
        functools.partial(loss_body, loss_scale * 2.0 / total),
        out_shape=jax.ShapeDtypeStruct((rows, width), b16),
    )(sent[0], head_weight, pixel_labels)

    def back_layer(g, slot, kept, dtype):
        gs, gh, gc, etop, ebot = layer_point(g, kept[3], kept[6], params, slot, *dims)
        g = layer_spread(g, gc, *halo(etop, ebot), params, slot, *dims, dtype)
        return g, (gs, gh, gc)

    back_pairs = [(p + 1, p) for p in range(sections - 1)]

    def backward_section(tick, incoming, back0, back1, cotangent):
        def leave(incoming, back0, back1, cotangent):
            return back0, back1, cotangent

        def one(incoming, back0, back1, cotangent):
            cotangent, back0 = back_layer(incoming, 0, kept0, b16)
            return back0, back1, cotangent

        def both(incoming, back0, back1, cotangent):
            g, back1 = back_layer(incoming, 1, kept1, f32)
            cotangent, back0 = back_layer(g, 0, kept0, b16)
            return back0, back1, cotangent

        which = jnp.where(tick == sections - 1 - section_index, layer_count, 0)
        return lax.switch(which, (leave, one, both), incoming, back0, back1, cotangent)

    def backward_tick(tick, state):
        incoming, back0, back1, cotangent = state
        back0, back1, cotangent = backward_section(tick, incoming, back0, back1, cotangent)
        return lax.ppermute(cotangent, "pipe", back_pairs), back0, back1, cotangent

    buffers = unwritten(back_shapes + back_shapes + sent_shapes[:1])
    state = (from_loss, tuple(buffers[:3]), tuple(buffers[3:6]), buffers[6])
    state = lax.fori_loop(0, sections - 1, backward_tick, state)
    incoming, back0, back1, cotangent = state

    owner = section_index == 0
    g, back1 = lax.cond(
        owner & (layer_count > 1),
        lambda g, back1: back_layer(g, 1, kept1, f32),
        lambda g, back1: (g.astype(f32), back1),
        incoming, back1,
    )

    def last_point(g, back0, sent):
        gs, gh, gc, etop, ebot = layer_point(g, kept0[3], kept0[6], params, 0, *dims)
        return (gs, gh, gc), halo(etop, ebot)

    back0, edges = lax.cond(
        owner, last_point, lambda g, back0, sent: (back0, sent[1:]), g, back0, tuple(sent)
    )
    slots = kernels.shape[0]
    stacked = layer_weights(section_layers, kept1, back1, (), slots, 1, *dims)
    stacked = layer_weights(section_layers, kept0, back0, stacked, slots, 0, *dims)
    w_in_grad, tall = lax.psum(tuple(stacked), "rows")
    cotangent = lax.cond(
        owner,
        lambda g, edges, gc, cotangent: layer_spread(g, gc, *edges, params, 0, *dims, b16),
        lambda g, edges, gc, cotangent: cotangent,
        g, edges, back0[2], cotangent,
    )
    w_out_grad = tall[:, :hidden_width]
    kernel_grad = tall[:, hidden_width : hidden_width + kernels.shape[1]].astype(f32)
    boundary = cotangent.reshape(micros, half, 2, band_rows, width).transpose(0, 3, 2, 1, 4)
    boundary = boundary.reshape(micros, band_rows, cols, width)
    return (boundary[None], kernel_grad, w_in_grad, w_out_grad)


def solution(mesh):
    return jax.shard_map(
        on_device,
        mesh=mesh,
        in_specs=(
            P(None, "rows", None, None),
            P("pipe"),
            P("pipe", None, None),
            P("pipe", None),
            P("pipe", None, None),
            P("pipe", None, None),
            P("pipe", None),
            P(),
            P(None, "rows", None),
        ),
        out_specs=(
            P("pipe", None, "rows", None, None),
            P("pipe", None, None),
            P("pipe", None, None),
            P("pipe", None, None),
        ),
        check_vma=False,
    )
```

```python
import functools
import math

import jax
import jax.numpy as jnp
from jax import lax
from jax.experimental import pallas as pl
from jax.experimental.pallas import tpu as pltpu
from jax.sharding import PartitionSpec as P

root_tau = 1.0 / math.sqrt(2.0 * math.pi)
norm_eps = 1e-06
loss_scale = 1024.0
erf_p = 0.3275911
erf_poly = (1.061405429, -1.453152027, 1.421413741, -0.284496736, 0.254829592)
LANES = 128
SUB = 8
NT = (((1,), (1,)), ((), ()))
TN = (((0,), (0,)), ((), ()))
VMEM_LIMIT = 48 * 1024 * 1024
CHUNK = 256
GELU = jnp.bfloat16
TAP_ROWS = 64


def block_spec(array_rows, shape, micros):
    if array_rows:
        return pl.BlockSpec((shape[0] // micros,) + tuple(shape[1:]), lambda m: (m,) + (0,) * (len(shape) - 1))
    return pl.BlockSpec(shape, lambda m: (0,) * len(shape))


def slot_spec(shape, slot):
    return pl.BlockSpec((None,) + tuple(shape[1:]), lambda m: (slot,) + (0,) * (len(shape) - 1))


def per_micro(body, micros, operands, outs, scratch, flops):
    arrays, specs = [], []
    for item in operands:
        if isinstance(item, tuple):
            arrays.append(item[0])
            specs.append(slot_spec(item[0].shape, item[1]))
        else:
            arrays.append(item)
            specs.append(block_spec(True, item.shape, micros))
    size = sum(math.prod(o[0]) * jnp.dtype(o[1]).itemsize for o in outs)
    size += sum(a.size * a.dtype.itemsize for a in arrays)
    return pl.pallas_call(
        body,
        grid=(micros,),
        in_specs=specs,
        out_specs=[block_spec(True, o[0], micros) for o in outs],
        out_shape=[jax.ShapeDtypeStruct(*o) for o in outs],
        scratch_shapes=scratch,
        compiler_params=pltpu.CompilerParams(vmem_limit_bytes=VMEM_LIMIT),
        cost_estimate=pl.CostEstimate(flops=flops, bytes_accessed=size, transcendentals=0),
    )(*arrays)


def unwritten(shapes):
    return pl.pallas_call(
        lambda *refs: None,
        out_specs=[pl.BlockSpec(memory_space=pl.ANY) for _ in shapes],
        out_shape=[jax.ShapeDtypeStruct(*s) for s in shapes],
    )()


def gelu_pair(h):
    e = jnp.exp(h * h * -0.5)
    t = pl.reciprocal(1.0 + (erf_p * math.sqrt(0.5)) * jnp.abs(h), approx=True)
    q = t * (0.5 * erf_poly[0]) + 0.5 * erf_poly[1]
    for coef in erf_poly[2:]:
        q = q * t + 0.5 * coef
    q = q * t * e
    phi = jnp.where(h >= 0.0, 1.0 - q, q)
    return h * phi, phi + h * (e * root_tau)


def spread_taps(taps_ref, wide_taps):
    count, width = taps_ref.shape
    for tap in range(count):
        row = jnp.broadcast_to(taps_ref[tap : tap + 1, :], (2 * SUB, width))
        wide_taps[tap] = row.astype(jnp.bfloat16)


def build_shifts(own_ref, top_ref, bot_ref, cols, halo, shifts):
    planes = halo.shape[0]
    half = cols // 2
    for q in range(3):
        at = pl.ds(q * cols, cols)
        for lane in range(planes):
            lanes = slice(lane * LANES, (lane + 1) * LANES)
            plane = halo.at[lane]
            plane[pl.ds(5 + q, cols, stride=SUB), :] = top_ref[at, lanes].astype(jnp.float32)
            plane[pl.ds(q, cols, stride=SUB), :] = bot_ref[at, lanes].astype(jnp.float32)
    sub = lax.broadcasted_iota(jnp.int32, (SUB, LANES), 0)

    def pair(k, carry):
        for lane in range(planes):
            lanes = slice(lane * LANES, (lane + 1) * LANES)
            at = pl.ds(pl.multiple_of(k * 2 * SUB, 2 * SUB), 2 * SUB)
            own = own_ref[at, lanes].astype(jnp.float32)
            edge = halo[lane, at, :]
            for a in range(7):
                if a == 3:
                    both = own
                else:
                    mask = sub >= 5 + a if a < 3 else sub < a - 3
                    both = jnp.concatenate(
                        [
                            pltpu.roll(
                                jnp.where(mask, edge[h * SUB : (h + 1) * SUB], own[h * SUB : (h + 1) * SUB]),
                                (3 - a) % SUB,
                                0,
                            )
                            for h in range(2)
                        ],
                        axis=0,
                    )
                shifts[a, k + 3, :, lanes] = both.astype(jnp.bfloat16)
        return carry

    lax.fori_loop(0, half, pair, 0, unroll=2)
    blank = jnp.zeros((SUB, planes * LANES), jnp.float32)
    for a in range(7):
        for k in range(3):
            right = shifts[a, k + 3].astype(jnp.float32)[SUB:]
            shifts[a, half + 3 + k] = jnp.concatenate([right, blank], axis=0).astype(jnp.bfloat16)
            left = shifts[a, half + k].astype(jnp.float32)[:SUB]
            shifts[a, k] = jnp.concatenate([blank, left], axis=0).astype(jnp.bfloat16)


def convolve(shifts, wide_taps, flip, cols, width, store):
    for lane in range(width // LANES):
        lanes = slice(lane * LANES, (lane + 1) * LANES)

        def block(kb, carry, lanes=lanes):
            acc = jnp.zeros((8, 2 * SUB, LANES), jnp.float32)
            for a in range(7):
                strip = shifts[a, pl.ds(kb * 8, 14), :, lanes]
                if a % 2 == 0:
                    line = None
                for b in range(7):
                    tap = 48 - (a * 7 + b) if flip else a * 7 + b
                    term = strip[b : b + 8] * wide_taps[tap, :, lanes][None]
                    line = term if line is None else line + term
                if a % 2 or a == 6:
                    acc = acc + line.astype(jnp.float32)
            store(pl.ds(pl.multiple_of(kb * 128, 128), 128), lanes, acc.reshape(16 * SUB, LANES))
            return carry

        lax.fori_loop(0, cols // 16, block, 0)


def write_edges(source_ref, etop_ref, ebot_ref, halo, cols):
    for lane in range(halo.shape[0]):
        lanes = slice(lane * LANES, (lane + 1) * LANES)
        plane = halo.at[lane]
        plane[...] = source_ref[:, lanes]
        for q in range(3):
            to = pl.ds(q * cols, cols)
            etop_ref[to, lanes] = plane[pl.ds(q, cols, stride=SUB), :].astype(jnp.bfloat16)
            ebot_ref[to, lanes] = plane[pl.ds(q + 5, cols, stride=SUB), :].astype(jnp.bfloat16)


def row_loop(rows, step, fn):
    def body(i, carry):
        fn(pl.ds(pl.multiple_of(i * step, step), step))
        return carry

    lax.fori_loop(0, rows // step, body, 0)


def conv_scratch(cols, width):
    return [
        pltpu.VMEM((width // LANES, cols * SUB, LANES), jnp.float32),
        pltpu.VMEM((7, cols // 2 + 6, 2 * SUB, width), jnp.bfloat16),
        pltpu.VMEM((49, 2 * SUB, width), jnp.bfloat16),
    ]


def front_body(
    cols,
    x_ref, top_ref, bot_ref, taps_ref, gain_ref, w_in_ref, w_out_ref, scale_ref,
    out_ref, etop_ref, ebot_ref, centred_ref, normed_ref, active_ref, slope_ref,
    halo, shifts, wide_taps, hidden, conv_ref,
):
    rows, width = x_ref.shape
    hidden_width = w_in_ref.shape[1]

    @pl.when(pl.program_id(0) == 0)
    def first_step():
        spread_taps(taps_ref, wide_taps)

    build_shifts(x_ref, top_ref, bot_ref, cols, halo, shifts)

    def store(at, lanes, value):
        conv_ref[at, lanes] = value

    convolve(shifts, wide_taps, False, cols, width, store)

    def norm(at):
        conv = conv_ref[at, :]
        centred = conv - jnp.mean(conv, axis=-1, keepdims=True)
        spread = jnp.mean(centred * centred, axis=-1, keepdims=True)
        centred_ref[at, :] = centred.astype(jnp.bfloat16)
        normed_ref[at, :] = (centred * lax.rsqrt(spread + norm_eps) * gain_ref[...]).astype(
            jnp.bfloat16
        )

    row_loop(rows, 64, norm)
    normed = normed_ref[...]
    chunks = hidden_width // CHUNK

    def expand(n):
        hidden[n % 2] = jnp.dot(
            normed, w_in_ref[:, n * CHUNK : (n + 1) * CHUNK], preferred_element_type=jnp.float32
        )

    expand(0)
    for n in range(chunks):
        if n + 1 < chunks:
            expand(n + 1)
        lanes = slice(n * CHUNK, (n + 1) * CHUNK)
        for i in range(rows // 32):
            at = slice(i * 32, (i + 1) * 32)
            value, slope = gelu_pair(hidden[n % 2, at, :].astype(GELU))
            active_ref[at, lanes] = value.astype(jnp.bfloat16)
            slope_ref[at, lanes] = slope.astype(jnp.bfloat16)
    y_ref = conv_ref
    y_ref[...] = x_ref[...].astype(jnp.float32) + scale_ref[...] * jnp.dot(
        active_ref[...], w_out_ref[...], preferred_element_type=jnp.float32
    )
    out_ref[...] = y_ref[...].astype(out_ref.dtype)
    write_edges(y_ref, etop_ref, ebot_ref, halo, cols)


def layer_front(x, top, bot, params, slot, micros, cols, dtype):
    taps, gains, w_in, w_out, scales = params
    rows, width = x.shape
    hidden_width = w_in.shape[2]
    f32, b16 = jnp.float32, jnp.bfloat16
    return per_micro(
        functools.partial(front_body, cols),
        micros,
        (x, top, bot, (taps, slot), (gains, slot), (w_in, slot), (w_out, slot), (scales, slot)),
        [
            ((rows, width), dtype), (top.shape, b16), (bot.shape, b16),
            ((rows, width), b16), ((rows, width), b16),
            ((rows, hidden_width), b16), ((rows, hidden_width), b16),
        ],
        conv_scratch(cols, width)
        + [pltpu.VMEM((2, rows // micros, CHUNK), f32), pltpu.VMEM((rows // micros, width), f32)],
        4 * rows * width * hidden_width,
    )


def point_body(
    cols,
    g_ref, centred_ref, slope_ref, gain_ref, w_in_ref, w_out_ref, scale_ref,
    gs_ref, gh_ref, gc_ref, etop_ref, ebot_ref, wide, halo,
):
    rows, width = g_ref.shape
    hidden_width = w_in_ref.shape[1]
    gs_ref[...] = (scale_ref[...] * g_ref[...].astype(jnp.float32)).astype(jnp.bfloat16)
    grad = gs_ref[...]
    chunks = hidden_width // CHUNK

    def expand(n):
        wide[n % 2] = lax.dot_general(
            grad, w_out_ref[n * CHUNK : (n + 1) * CHUNK, :], NT, preferred_element_type=jnp.float32
        )

    expand(0)
    for n in range(chunks):
        if n + 1 < chunks:
            expand(n + 1)
        lanes = slice(n * CHUNK, (n + 1) * CHUNK)
        for i in range(rows // 32):
            at = slice(i * 32, (i + 1) * 32)
            gh_ref[at, lanes] = (wide[n % 2, at, :] * slope_ref[at, lanes].astype(jnp.float32)).astype(
                jnp.bfloat16
            )
    gc_ref[...] = lax.dot_general(gh_ref[...], w_in_ref[...], NT, preferred_element_type=jnp.float32)

    def norm_back(at):
        centred = centred_ref[at, :].astype(jnp.float32)
        spread = jnp.mean(centred * centred, axis=-1, keepdims=True)
        scale = lax.rsqrt(spread + norm_eps)
        unit = centred * scale
        grad = gc_ref[at, :] * gain_ref[...]
        first = jnp.mean(grad, axis=-1, keepdims=True)
        second = jnp.mean(grad * unit, axis=-1, keepdims=True)
        gc_ref[at, :] = scale * (grad - first - unit * second)

    row_loop(rows, 64, norm_back)
    write_edges(gc_ref, etop_ref, ebot_ref, halo, cols)


def layer_point(g, conv, slope, params, slot, micros, cols):
    taps, gains, w_in, w_out, scales = params
    rows, width = g.shape
    hidden_width = w_in.shape[2]
    f32, b16 = jnp.float32, jnp.bfloat16
    edge = (micros * 3 * cols, width)
    return per_micro(
        functools.partial(point_body, cols),
        micros,
        (g, conv, slope, (gains, slot), (w_in, slot), (w_out, slot), (scales, slot)),
        [((rows, width), b16), ((rows, hidden_width), b16), ((rows, width), f32), (edge, b16), (edge, b16)],
        [
            pltpu.VMEM((2, rows // micros, CHUNK), f32),
            pltpu.VMEM((width // LANES, cols * SUB, LANES), f32),
        ],
        4 * rows * width * hidden_width,
    )


def spread_body(
    cols, g_ref, gc_ref, top_ref, bot_ref, taps_ref, out_ref, halo, shifts, wide_taps
):
    @pl.when(pl.program_id(0) == 0)
    def first_step():
        spread_taps(taps_ref, wide_taps)

    build_shifts(gc_ref, top_ref, bot_ref, cols, halo, shifts)

    def store(at, lanes, value):
        out_ref[at, lanes] = (g_ref[at, lanes].astype(jnp.float32) + value).astype(out_ref.dtype)

    convolve(shifts, wide_taps, True, cols, g_ref.shape[1], store)


def layer_spread(g, gc, top, bot, params, slot, micros, cols, dtype):
    rows, width = g.shape
    return per_micro(
        functools.partial(spread_body, cols),
        micros,
        (g, gc, top, bot, (params[0], slot)),
        [((rows, width), dtype)],
        conv_scratch(cols, width),
        98 * rows * width,
    )[0]


def weight_body(
    micros, cols, slot,
    count_ref, x_ref, top_ref, bot_ref, gc_ref, normed_ref, gh_ref, active_ref, gs_ref,
    *refs,
):
    first_ref, second_ref, halo, shifts, sums = refs[-5:]
    hidden_width = gh_ref.shape[1]
    width = x_ref.shape[1]
    applied = slot < count_ref[0]

    @pl.when(jnp.logical_not(applied))
    def passed():
        first_ref[...] = jnp.zeros_like(first_ref)
        second_ref[...] = jnp.zeros_like(second_ref)

    @pl.when(applied)
    def run():
        first_ref[...] = lax.dot_general(
            normed_ref[...], gh_ref[...], TN, preferred_element_type=jnp.float32
        ).astype(jnp.bfloat16)
        second_ref[:hidden_width, :] = lax.dot_general(
            active_ref[...], gs_ref[...], TN, preferred_element_type=jnp.float32
        ).astype(jnp.bfloat16)
        pixels = cols * SUB
        for m in range(micros):
            at_edge = pl.ds(m * 3 * cols, 3 * cols)
            build_shifts(
                x_ref.at[pl.ds(m * pixels, pixels)], top_ref.at[at_edge], bot_ref.at[at_edge],
                cols, halo, shifts,
            )
            for lane in range(width // LANES):
                lanes = slice(lane * LANES, (lane + 1) * LANES)

                def tap_row(a, carry, lanes=lanes, m=m):
                    found = [jnp.zeros((2 * SUB, LANES), jnp.float32) for _ in range(7)]
                    for kb in range(cols // 16):
                        strip = shifts[a, kb * 8 : kb * 8 + 14, :, lanes]
                        at = pl.ds(m * pixels + kb * 128, 128)
                        grad = gc_ref[at, lanes].astype(jnp.bfloat16).reshape(8, 2 * SUB, LANES)
                        for b in range(7):
                            term = strip[b : b + 8] * grad
                            term = (term[0] + term[1]) + (term[2] + term[3]), (term[4] + term[5]) + (term[6] + term[7])
                            found[b] = found[b] + (term[0].astype(jnp.float32) + term[1].astype(jnp.float32))
                    for b in range(7):
                        total = found[b][:SUB] + found[b][SUB:]
                        if m == 0:
                            sums[a * 7 + b, :, lanes] = total
                        else:
                            sums[a * 7 + b, :, lanes] += total
                    return carry

                lax.fori_loop(0, 7, tap_row, 0)
        taps = jnp.sum(sums[...], axis=1)
        fill = jnp.zeros((TAP_ROWS - taps.shape[0], width), jnp.float32)
        second_ref[hidden_width:, :] = jnp.concatenate([taps, fill], axis=0).astype(jnp.bfloat16)


def layer_weights(count, kept, back, stacked, slots, slot, micros, cols):
    x, top, bot, _, normed, active, _ = kept
    gs, gh, gc = back
    rows, width = x.shape
    hidden_width = gh.shape[1]
    f32, b16 = jnp.float32, jnp.bfloat16
    arrays = (x, top, bot, gc, normed, gh, active, gs)
    outs = [((slots, width, hidden_width), b16), ((slots, hidden_width + TAP_ROWS, width), b16)]
    size = sum(math.prod(o[0]) * jnp.dtype(o[1]).itemsize for o in outs)
    size += sum(a.size * a.dtype.itemsize for a in arrays)
    return pl.pallas_call(
        functools.partial(weight_body, micros, cols, slot),
        grid=(1,),
        in_specs=[pl.BlockSpec(memory_space=pltpu.SMEM)] + [block_spec(False, a.shape, 1) for a in arrays]
        + [pl.BlockSpec(memory_space=pl.ANY) for _ in stacked],
        out_specs=[slot_spec(o[0], slot) for o in outs],
        input_output_aliases={1 + len(arrays) + i: i for i in range(len(stacked))},
        out_shape=[jax.ShapeDtypeStruct(*o) for o in outs],
        scratch_shapes=conv_scratch(cols, width)[:2] + [pltpu.VMEM((49, SUB, width), f32)],
        compiler_params=pltpu.CompilerParams(vmem_limit_bytes=VMEM_LIMIT),
        cost_estimate=pl.CostEstimate(
            flops=4 * rows * width * hidden_width, bytes_accessed=size, transcendentals=0
        ),
    )(count, *arrays, *stacked)


def loss_body(factor, y_ref, head_ref, labels_ref, g_ref):
    logits = jnp.dot(y_ref[...], head_ref[...], preferred_element_type=jnp.float32)
    spots = lax.broadcasted_iota(jnp.int32, logits.shape, 1)
    target = (labels_ref[...] == spots).astype(jnp.float32)
    grad = (factor * (logits - target)).astype(jnp.bfloat16)
    g_ref[...] = lax.dot_general(
        grad, head_ref[...], NT, preferred_element_type=jnp.float32
    ).astype(jnp.bfloat16)


def on_device(features, section_layers, kernels, gains, w_in, w_out, scales, head_weight, labels):
    sections = lax.axis_size("pipe")
    section_index = lax.axis_index("pipe")
    bands = lax.axis_size("rows")
    micros, band_rows, cols, width = features.shape
    hidden_width = w_in.shape[2]
    classes = head_weight.shape[1]
    layer_count = section_layers[0]
    rows = micros * band_rows * cols
    half = cols // 2
    f32, b16 = jnp.float32, jnp.bfloat16
    params = (kernels, gains[:, None, :], w_in, w_out, scales[:, None, :])
    dims = (micros, cols)
    edge_shape = (micros * 3 * cols, width)

    up = [(i, i + 1) for i in range(bands - 1)]
    down = [(i + 1, i) for i in range(bands - 1)]

    def halo(etop, ebot):
        return lax.ppermute(ebot, "rows", up), lax.ppermute(etop, "rows", down)

    def hop(x, etop, ebot):
        def pairs(by):
            return [
                (p * bands + r, (p + 1) * bands + r + by)
                for p in range(sections - 1)
                for r in range(bands)
                if 0 <= r + by < bands
            ]

        axes = ("pipe", "rows")
        return (
            lax.ppermute(x, axes, pairs(0)),
            lax.ppermute(ebot, axes, pairs(1)),
            lax.ppermute(etop, axes, pairs(-1)),
        )

    def edge_rows(part):
        part = part.reshape(micros, 3, 2, half, width).transpose(0, 1, 3, 2, 4)
        return part.reshape(edge_shape)

    first_x = features.reshape(micros, band_rows, 2, half, width).transpose(0, 3, 2, 1, 4)
    first_in = (
        first_x.reshape(rows, width),
        *halo(edge_rows(features[:, :3]), edge_rows(features[:, band_rows - 3 :])),
    )

    def kept_shapes(dtype_x):
        return [
            ((rows, width), dtype_x), (edge_shape, b16), (edge_shape, b16), ((rows, width), b16),
            ((rows, width), b16), ((rows, hidden_width), b16), ((rows, hidden_width), b16),
        ]

    sent_shapes = [((rows, width), b16), (edge_shape, b16), (edge_shape, b16)]
    back_shapes = [((rows, width), b16), ((rows, hidden_width), b16), ((rows, width), f32)]

    def front(x, top, bot, slot, dtype):
        out, etop, ebot, *values = layer_front(x, top, bot, params, slot, *dims, dtype)
        return (out, etop, ebot), (x, top, bot, *values)

    def forward_section(tick, received, kept0, kept1, sent):
        def leave(received, kept0, kept1, sent):
            return kept0, kept1, sent

        def one(received, kept0, kept1, sent):
            sent, kept0 = front(*received, 0, b16)
            return kept0, kept1, sent

        def both(received, kept0, kept1, sent):
            (y, etop, ebot), kept0 = front(*received, 0, f32)
            sent, kept1 = front(y, *halo(etop, ebot), 1, b16)
            return kept0, kept1, sent

        which = jnp.where(tick == section_index, layer_count, 0)
        return lax.switch(which, (leave, one, both), received, kept0, kept1, sent)

    def forward_tick(tick, state):
        received, kept0, kept1, sent = state
        kept0, kept1, sent = forward_section(tick, received, kept0, kept1, sent)
        return hop(*sent), kept0, kept1, sent

    buffers = unwritten(kept_shapes(b16) + kept_shapes(f32) + sent_shapes)
    state = (first_in, tuple(buffers[:7]), tuple(buffers[7:14]), tuple(buffers[14:]))
    state = lax.fori_loop(0, sections - 1, forward_tick, state)
    kept0, kept1, sent = forward_section(sections - 1, *state)

    total = micros * band_rows * bands * cols
    pixel_labels = labels.reshape(micros, band_rows, 2, half).transpose(0, 3, 2, 1).reshape(rows, 1)
    from_loss = pl.pallas_call(
        functools.partial(loss_body, loss_scale * 2.0 / total),
        out_shape=jax.ShapeDtypeStruct((rows, width), b16),
    )(sent[0], head_weight, pixel_labels)

    def back_layer(g, slot, kept, dtype):
        gs, gh, gc, etop, ebot = layer_point(g, kept[3], kept[6], params, slot, *dims)
        g = layer_spread(g, gc, *halo(etop, ebot), params, slot, *dims, dtype)
        return g, (gs, gh, gc)

    back_pairs = [(p + 1, p) for p in range(sections - 1)]

    def backward_section(tick, incoming, back0, back1, cotangent):
        def leave(incoming, back0, back1, cotangent):
            return back0, back1, cotangent

        def one(incoming, back0, back1, cotangent):
            cotangent, back0 = back_layer(incoming, 0, kept0, b16)
            return back0, back1, cotangent

        def both(incoming, back0, back1, cotangent):
            g, back1 = back_layer(incoming, 1, kept1, f32)
            cotangent, back0 = back_layer(g, 0, kept0, b16)
            return back0, back1, cotangent

        which = jnp.where(tick == sections - 1 - section_index, layer_count, 0)
        return lax.switch(which, (leave, one, both), incoming, back0, back1, cotangent)

    def backward_tick(tick, state):
        incoming, back0, back1, cotangent = state
        back0, back1, cotangent = backward_section(tick, incoming, back0, back1, cotangent)
        return lax.ppermute(cotangent, "pipe", back_pairs), back0, back1, cotangent

    buffers = unwritten(back_shapes + back_shapes + sent_shapes[:1])
    state = (from_loss, tuple(buffers[:3]), tuple(buffers[3:6]), buffers[6])
    state = lax.fori_loop(0, sections - 1, backward_tick, state)
    incoming, back0, back1, cotangent = state

    owner = section_index == 0
    g, back1 = lax.cond(
        owner & (layer_count > 1),
        lambda g, back1: back_layer(g, 1, kept1, f32),
        lambda g, back1: (g.astype(f32), back1),
        incoming, back1,
    )

    def last_point(g, back0, sent):
        gs, gh, gc, etop, ebot = layer_point(g, kept0[3], kept0[6], params, 0, *dims)
        return (gs, gh, gc), halo(etop, ebot)

    back0, edges = lax.cond(
        owner, last_point, lambda g, back0, sent: (back0, sent[1:]), g, back0, tuple(sent)
    )
    slots = kernels.shape[0]
    stacked = layer_weights(section_layers, kept1, back1, (), slots, 1, *dims)
    stacked = layer_weights(section_layers, kept0, back0, stacked, slots, 0, *dims)
    w_in_grad, tall = lax.psum(tuple(stacked), "rows")
    cotangent = lax.cond(
        owner,
        lambda g, edges, gc, cotangent: layer_spread(g, gc, *edges, params, 0, *dims, b16),
        lambda g, edges, gc, cotangent: cotangent,
        g, edges, back0[2], cotangent,
    )
    w_out_grad = tall[:, :hidden_width]
    kernel_grad = tall[:, hidden_width : hidden_width + kernels.shape[1]].astype(f32)
    boundary = cotangent.reshape(micros, half, 2, band_rows, width).transpose(0, 3, 2, 1, 4)
    boundary = boundary.reshape(micros, band_rows, cols, width)
    return (boundary[None], kernel_grad, w_in_grad, w_out_grad)


def solution(mesh):
    return jax.shard_map(
        on_device,
        mesh=mesh,
        in_specs=(
            P(None, "rows", None, None),
            P("pipe"),
            P("pipe", None, None),
            P("pipe", None),
            P("pipe", None, None),
            P("pipe", None, None),
            P("pipe", None),
            P(),
            P(None, "rows", None),
        ),
        out_specs=(
            P("pipe", None, "rows", None, None),
            P("pipe", None, None),
            P("pipe", None, None),
            P("pipe", None, None),
        ),
        check_vma=False,
    )
```
